128 devices in a mesh: row: 8 (over x, core), col: 16 (over z, y).
Axes of the slice: x: 4, y: 4, z: 4, core: 2. Of those that a mesh axis runs over, the one named last changes fastest.
Arguments:
- kohn_blocks: bfloat16 [512, 16, 4, 4096], P('row', 'col'), may hold values from -0.1875 to 0.1875
- kohn_columns: int32 [512, 16, 4], P('row', 'col'), may hold values from 0 to 63
- density_blocks: bfloat16 [16, 64, 8, 4096], P('col', 'row'), may hold values from -6 to 6
- density_columns: int32 [16, 64, 8], P('col', 'row'), may hold values from 0 to 31, as said below
- owner_map: int32 [16384, 1], P(('row', 'col')), may hold values from 0 to 127; in each aligned block of 128 rows (0 to 127, 128 to 255, ...) at most 2 rows name the same one
Outputs:
- owned_blocks: float32 [32768, 4096], P(('row', 'col'))
The draws below stay inside these ranges and needn't reach their ends.
Inputs may be any that keep to these rules, and one draw needn't show every extreme that they name: `density_columns`: the 8 window columns of one density block row are distinct. `owner_map`: the gradient blocks of one device's 4 rows name any one owner at most 2 times.
All inputs are finite; a program needn't handle non-finite values.
Results may differ from the reference program's by a relative error of at most 0.0003.
Values may be sent and summed in bfloat16 or wider, within the bound.
No kernel may reach another device: no remote copies, remote signals or barrier semaphores. Data moves between devices by JAX's collectives and lax.ppermute only.
A program may use at most 320 MiB of HBM per device.

```python
import math
import jax
import jax.numpy as jnp
import numpy as np
from jax import lax

B = 64
NCW = 32
SK = 4
SP = 8
NBP = 64
KR = 512
RPD = 4
CAP = 2
N_COL = 16
DEVICES = 128


def draw_density_columns(key, part):
    key = jax.random.fold_in(key, 7)
    scores = jax.random.randint(key, (N_COL, NBP, NCW), 0, 2 ** 20) * NCW
    scores = scores + jnp.arange(NCW, dtype=jnp.int32)
    order = jnp.argsort(scores, axis=-1)
    return order[..., :SP].astype(jnp.int32)


def plant(drawn, stream_key, smallest, largest):
    dims = drawn.shape
    spot = [jax.random.randint(jax.random.fold_in(stream_key, axis), (), 0, dims[axis]) for axis in range(len(dims))]
    drawn = drawn.at[tuple(spot)].set(smallest)
    longest = dims.index(max(dims))
    spot[longest] = (spot[longest] + 1) % dims[longest]
    return drawn.at[tuple(spot)].set(largest)


def block_levels(rng, shape, split, least, high):
    level, own = 1.0, jax.random.fold_in(rng, 6)
    for position, shards_of in split:
        heights = jnp.exp(jax.random.uniform(jax.random.fold_in(own, position), (shards_of,), jnp.float32, least / len(split), high / len(split)))
        level = level * jnp.repeat(heights, shape[position] // shards_of).reshape([-1 if axis == position else 1 for axis in range(len(shape))])
    return level


def routed_block(own_key, own, number, rows, count, top, limit, slope):
    ranking = jax.random.permutation(own_key, count)
    packed, ordinary = portions_of(count, rows * top, limit, slope, True), portions_of(count, rows * top, limit, slope, False)
    places = jnp.arange(count)

    def named(lengths, offset_by):
        used = int((lengths > 0).sum())
        fixed = max(1, used // 4)
        passed = fixed + (places - fixed + offset_by * (used - fixed)) % max(1, count - fixed)
        return jnp.zeros((count,), jnp.int32).at[ranking[jnp.where(places < fixed, places, passed)]].set(jnp.asarray(lengths, jnp.int32))

    lengths = jnp.where(number % 4 == 0, named(packed, number // 4), named(ordinary, number - number // 4 - 1))
    mixed = jax.random.permutation(jax.random.fold_in(own, 3), count)
    giver, receiver = mixed[0:count // 2 * 2:2], mixed[1:count // 2 * 2:2]
    room = jnp.minimum(lengths[giver] - 1, limit - lengths[receiver]) // 2
    room = jnp.where((giver == ranking[0]) | (receiver == ranking[0]) | (lengths[receiver] == 0), 0, jnp.maximum(room, 0))
    passed = jax.random.randint(jax.random.fold_in(own, 4), (count // 2,), 0, 1 << 20) % (room + 1)
    lengths = lengths.at[giver].add(-passed).at[receiver].add(passed)
    labels = jnp.searchsorted(jnp.cumsum(lengths), jnp.arange(rows * top), side="right").astype(jnp.int32)
    grid = labels.reshape(top, rows).T
    grid = grid[jax.random.permutation(jax.random.fold_in(own, 1), rows)]
    offset_by = jax.random.randint(jax.random.fold_in(own, 2), (rows, 1), 0, top)
    return jnp.take_along_axis(grid, (jnp.arange(top)[None, :] + offset_by) % top, axis=1)


def portions_of(amount, total, limit, skew, full):
    weights = [(1 << 20) // math.isqrt(rank ** skew) + 1 for rank in range(1, amount + 1)]
    largest = limit if full else min(limit, max(-(-total // amount), total * weights[0] // sum(weights)))
    least = 1 if total - largest >= amount - 1 else 0
    holding, surplus = [largest] + [least] * (amount - 1), total - largest - least * (amount - 1)
    while surplus > 0:
        free = [i for i in range(1, amount) if holding[i] < largest] or [i for i in range(1, amount) if holding[i] < limit]
        mass, budget = sum([weights[i] for i in free]), surplus
        for i in free:
            extra = min(limit - holding[i], max(1, budget * weights[i] // mass), surplus)
            holding[i] = holding[i] + extra
            surplus = surplus - extra
    return np.array(holding)


def scatter_about(stream_key, dims, spread, bound, shards=(), kind=jnp.bfloat16):
    loudness = block_levels(stream_key, dims, shards, -0.22, 0.18) if shards else 1.0
    drawn = jax.random.normal(stream_key, dims, jnp.float32) * spread * loudness
    return jnp.minimum(jnp.maximum(drawn, -bound), bound).astype(kind)


def setup_inputs(seed: int = 0) -> dict:
    seeds = jax.random.split(jax.random.key(seed), 6)
    kohn_blocks = scatter_about(seeds[0], (KR, N_COL, SK, B * B), (B * SK * N_COL * SP // NCW) ** -0.5, 0.1875, ((0, 8), (1, 16)))
    kohn_columns = plant(jax.random.randint(seeds[1], (KR, N_COL, SK), 0, NBP), jax.random.fold_in(seeds[1], 1), 0, NBP - 1).astype(jnp.int32)
    density_blocks = scatter_about(seeds[2], (N_COL, NBP, SP, B * B), 1.0, 6.0, ((0, 16), (1, 8)))
    density_columns = draw_density_columns(jax.random.fold_in(seeds[5], 71), 0)
    owner_map_keys = jax.random.split(jax.random.fold_in(seeds[4], 1), (KR * NCW) // (RPD * NCW))
    owner_map_turns = jax.random.permutation(jax.random.fold_in(seeds[4], 3), (KR * NCW) // (RPD * NCW))
    owner_map = jax.vmap(lambda own, number: routed_block(jax.random.fold_in(seeds[4], 2), own, number, RPD * NCW, DEVICES, 1, CAP, 2))(owner_map_keys, owner_map_turns).reshape((KR * NCW, 1))
    return dict(kohn_blocks=kohn_blocks, kohn_columns=kohn_columns, density_blocks=density_blocks, density_columns=density_columns, owner_map=owner_map)


def one_row(pieces, density_blocks, density_columns):
    row_blocks, row_columns = pieces
    panels = jnp.arange(N_COL, dtype=jnp.int32)[:, None]
    picked = density_blocks[panels, row_columns]
    picked_columns = density_columns[panels, row_columns]
    left = row_blocks.reshape(N_COL, SK, B, B).astype(jnp.float32)
    right = picked.reshape(N_COL, SK, SP, B, B).astype(jnp.float32)
    products = jnp.einsum("qaxy,qabyz->qabxz", left, right)
    onehot = (picked_columns[..., None] == jnp.arange(NCW, dtype=jnp.int32)).astype(jnp.float32)
    per_panel = jnp.einsum("qabj,qabxz->qjxz", onehot, products, precision=lax.Precision.HIGHEST)
    summed = jnp.sum(per_panel, axis=0)
    return summed.reshape(NCW, B * B)


def route(pieces):
    blocks, targets = pieces
    onehot = (targets[:, None] == jnp.arange(DEVICES, dtype=jnp.int32)).astype(jnp.int32)
    ranks = jnp.sum(jnp.cumsum(onehot, axis=0) * onehot, axis=1) - 1
    slots = targets * CAP + ranks
    return jnp.zeros((DEVICES * CAP, B * B), jnp.float32).at[slots].set(blocks)


def reference(kohn_blocks, kohn_columns, density_blocks, density_columns, owner_map):
    gradient = lax.map(lambda pieces: one_row(pieces, density_blocks, density_columns), (kohn_blocks, kohn_columns))
    blocks = gradient.reshape(DEVICES, RPD * NCW, B * B)
    targets = owner_map.reshape(DEVICES, RPD * NCW)
    sent = lax.map(route, (blocks, targets))
    owned = sent.reshape(DEVICES, DEVICES, CAP, B * B).transpose(1, 0, 2, 3)
    return owned.reshape(DEVICES * DEVICES * CAP, B * B)
```

```python
import functools

import jax
import jax.numpy as jnp
from jax import lax
from jax.experimental import pallas as pl
from jax.experimental.pallas import tpu as pltpu
from jax.sharding import Mesh, PartitionSpec as P

B = 64
HALF = 32
NCW = 32
SK = 4
SP = 8
X, C, Z, Y = 4, 2, 4, 4
ALL = ("x", "core", "z", "y")


def chunk_masks(shape):
    lane = lax.broadcasted_iota(jnp.int32, shape, len(shape) - 1)
    return (lane & 64) == 0, (lane & 32) == 0


def panel_kernel(kcol, jcol, k_ref, d_ref, o_ref):
    step = pl.program_id(0) * pl.num_programs(1) + pl.program_id(1)
    low64, low32 = chunk_masks((16, 128))
    o_ref[...] = jnp.zeros_like(o_ref)
    for p in range(Z * SK):
        z, a = p // SK, p % SK
        k = kcol[step * (Z * SK) + p]
        blk = k_ref[0, z, 0, 0, a * 32:(a + 1) * 32, :]
        left = jnp.concatenate([blk[:, :B], blk[:, B:]], axis=0)
        r = jnp.dot(left, d_ref[k], preferred_element_type=jnp.float32)
        for t in range(2):
            v = [r[ch * 16:(ch + 1) * 16, t * 128:(t + 1) * 128] for ch in range(4)]
            w = [None] * 4
            for c0 in range(2):
                lo, hi = v[c0], v[2 + c0]
                w[c0] = jnp.where(low64, lo, pltpu.roll(hi, 64, 1))
                w[2 + c0] = jnp.where(low64, pltpu.roll(lo, 64, 1), hi)
            u = [None] * 4
            for b1 in range(2):
                lo, hi = w[2 * b1], w[2 * b1 + 1]
                u[2 * b1] = jnp.where(low32, lo, pltpu.roll(hi, 32, 1))
                u[2 * b1 + 1] = jnp.where(low32, pltpu.roll(lo, 96, 1), hi)
            js = [jcol[k * SP + t * 4 + b] for b in range(4)]
            old = [o_ref[0, 0, js[b]] for b in range(4)]
            for b in range(4):
                o_ref[0, 0, js[b]] = old[b] + u[b]


def panel_sums(kcol, jcol, kohn, dens):
    grid_spec = pltpu.PrefetchScalarGridSpec(
        num_scalar_prefetch=2,
        grid=(Y, 8),
        in_specs=[
            pl.BlockSpec((1, Z, 1, 1, 128, 128), lambda y, r, *_: (r // 4, 0, y, r % 4, 0, 0)),
            pl.BlockSpec((Z * 64, 64, 256), lambda y, r, *_: (0, 0, 0), pipeline_mode=pl.Buffered(1)),
        ],
        out_specs=pl.BlockSpec((1, 1, NCW, 16, 128), lambda y, r, *_: (y, r, 0, 0, 0)),
    )
    return pl.pallas_call(
        panel_kernel,
        grid_spec=grid_spec,
        out_shape=jax.ShapeDtypeStruct((Y, 8, NCW, 16, 128), jnp.float32),
        compiler_params=pltpu.CompilerParams(vmem_limit_bytes=40 << 20),
        cost_estimate=pl.CostEstimate(flops=2 * 512 * 64 * 64 * 256, bytes_accessed=20 << 20, transcendentals=0),
        name="panel_sums",
    )(kcol, jcol, kohn, dens)


def pack_kernel(slots, g_ref, o_ref):
    def clear(n, _):
        o_ref[pl.ds(n * 16, 16)] = jnp.zeros((16, 16, 128), jnp.float32)
        return 0

    lax.fori_loop(0, 32, clear, 0)

    def place(n, _):
        for m in range(8):
            o_ref[slots[n * 8 + m]] = g_ref[n * 8 + m]
        return 0

    lax.fori_loop(0, 32, place, 0)


def pack(slots, blocks):
    return pl.pallas_call(
        pack_kernel,
        grid_spec=pltpu.PrefetchScalarGridSpec(
            num_scalar_prefetch=1,
            grid=(1,),
            in_specs=[pl.BlockSpec((256, 16, 128), lambda i, *_: (0, 0, 0), pipeline_mode=pl.Buffered(1))],
            out_specs=pl.BlockSpec((512, 16, 128), lambda i, *_: (0, 0, 0), pipeline_mode=pl.Buffered(1)),
        ),
        out_shape=jax.ShapeDtypeStruct((512, 16, 128), jnp.float32),
        compiler_params=pltpu.CompilerParams(vmem_limit_bytes=32 << 20),
        name="pack",
    )(slots, blocks)


def unpack_kernel(r_ref, o_ref, full):
    _, low32 = chunk_masks((16, 128))
    for n in range(16):
        for t in range(2):
            h0 = r_ref[0, 0, n, 0, t]
            h1 = r_ref[0, 1, n, 0, t]
            base = (n * 2 + t) * 32
            full[base:base + 16, :] = jnp.where(low32, h0, pltpu.roll(h1, 32, 1))
            full[base + 16:base + 32, :] = jnp.where(low32, pltpu.roll(h0, 96, 1), h1)
    for p in range(32):
        o_ref[:, p * 128:(p + 1) * 128] = full[pl.ds(p, 32, stride=32), :]


def unpack(received):
    return pl.pallas_call(
        unpack_kernel,
        grid=(X, C),
        in_specs=[pl.BlockSpec((1, C, 16, 1, 2, 16, 128), lambda x, s: (x, 0, 0, s, 0, 0, 0))],
        out_specs=pl.BlockSpec((32, 4096), lambda x, s: (x * 2 + s, 0)),
        out_shape=jax.ShapeDtypeStruct((256, 4096), jnp.float32),
        scratch_shapes=[pltpu.VMEM((32 * 32, 128), jnp.float32)],
        compiler_params=pltpu.CompilerParams(vmem_limit_bytes=32 << 20),
        name="unpack",
    )(received)


def local(kohn_blocks, kohn_columns, density_blocks, density_columns, owner_map):
    x, c, z = lax.axis_index("x"), lax.axis_index("core"), lax.axis_index("z")
    swap = [(0, 1), (1, 0)]

    halves = density_blocks.reshape(8, SP, B, 2, HALF).transpose(3, 0, 2, 1, 4).reshape(2, 8, B, SP * HALF)
    mine = lax.dynamic_index_in_dim(halves, c, 0, keepdims=False)
    theirs = lax.dynamic_index_in_dim(halves, 1 - c, 0, keepdims=False)
    shard = jnp.stack([mine, lax.ppermute(theirs, "core", swap)])
    dens = lax.all_gather(shard, ("z", "x"), axis=0, tiled=True).reshape(Z * 64, B, SP * HALF)

    ints = jnp.concatenate([kohn_columns.reshape(-1), density_columns.reshape(-1), owner_map.reshape(-1)])
    ints = lax.all_gather(ints, ("z", "x", "core")).reshape(Z, X, C, 448)

    def ordered(v, axis):
        return jnp.where(c == 1, jnp.flip(v, axis), v)

    kcol = lax.dynamic_index_in_dim(ints[..., :256], x, 1, keepdims=False).reshape(Z, C, Z, Y, 4, SK)
    kcol = ordered(lax.dynamic_index_in_dim(kcol, z, 2, keepdims=False), 1)
    kcol = (kcol ^ (8 * c)) + 64 * jnp.arange(Z, dtype=jnp.int32).reshape(Z, 1, 1, 1, 1)
    kcol = kcol.transpose(2, 1, 3, 0, 4).reshape(-1)
    jcol = ordered(ints[..., 256:320], 2).reshape(-1)
    owners = lax.dynamic_index_in_dim(ints[..., 320:], z, 0, keepdims=False)
    owners = ordered(lax.dynamic_index_in_dim(owners, x, 0, keepdims=False), 0)
    hit = (owners[..., None] == jnp.arange(128, dtype=jnp.int32)).astype(jnp.int32)
    ranks = jnp.sum(jnp.cumsum(hit, axis=1) * hit, axis=2) - 1
    source = jnp.arange(2, dtype=jnp.int32)[:, None] ^ c
    slots = (owners * 4 + source * 2 + ranks).reshape(-1)

    kohn = kohn_blocks.reshape(Z, 16, SK * 32, 128)
    kohn = lax.all_to_all(kohn, "z", split_axis=0, concat_axis=0, tiled=True)
    kohn = jnp.stack([kohn, lax.ppermute(kohn, "core", swap)]).reshape(2, Z, Y, 4, SK * 32, 128)

    sums = panel_sums(kcol, jcol, kohn, dens)
    gradient = lax.psum_scatter(sums, "y", scatter_dimension=0, tiled=True)
    outgoing = pack(slots, gradient.reshape(256, 16, 128))
    received = lax.all_to_all(outgoing.reshape(128, 4, 16, 128), ALL, split_axis=0, concat_axis=0, tiled=True)
    return unpack(received.reshape(X, C, 16, 2, 2, 16, 128))


def solution(mesh):
    grid = Mesh(mesh.devices.reshape(X, C, Z, Y), ALL)
    row, col = ("x", "core"), ("z", "y")
    return jax.shard_map(
        local,
        mesh=grid,
        in_specs=(
            P(row, col, None, None),
            P(row, col, None),
            P(col, row, None, None),
            P(col, row, None),
            P(ALL, None),
        ),
        out_specs=P(ALL, None),
        check_vma=False,
    )
```

```python
import jax
import jax.numpy as jnp
from jax import lax
from jax.experimental import pallas as pl
from jax.experimental.pallas import tpu as pltpu
from jax.sharding import Mesh, PartitionSpec as P

B = 64
HALF = 32
NCW = 32
SK = 4
SP = 8
X, C, Z, Y = 4, 2, 4, 4
ALL = ("x", "core", "z", "y")
PLANE = ("core", "z", "y")
TOP = 32766.0
MSG = 80


def line_pairs(step, along):
    pairs = []
    for c in range(C):
        for z in range(Z):
            for y in range(Y):
                to = ((z + step) % Z, y) if (c ^ along) == 0 else (z, (y + step) % Y)
                pairs.append(((c * Z + z) * Y + y, (c * Z + to[0]) * Y + to[1]))
    return pairs


def over_line(v, step):
    return lax.ppermute(v, PLANE, line_pairs(step, 0))


def over_cross(v, step):
    return lax.ppermute(v, PLANE, line_pairs(step, 1))


def over_x(v, step):
    return lax.ppermute(v, "x", [(i, (i + step) % X) for i in range(X)])


def over_core(v):
    return lax.ppermute(v, "core", [(0, 1), (1, 0)])


def chunk_masks(shape):
    lane = lax.broadcasted_iota(jnp.int32, shape, len(shape) - 1)
    return (lane & 64) == 0, (lane & 32) == 0


def panel_kernel(n, first, kcol, jcol, *refs):
    kohn, refs = refs[:n], refs[n:]
    halves, refs = refs[:2 * n], refs[2 * n:]
    if not first:
        p_ref, refs = refs[0], refs[1:]
    o_ref, dens, sems = refs
    step = pl.program_id(0)

    @pl.when(step == 0)
    def _():
        copies = [
            pltpu.make_async_copy(halves[h], dens.at[pl.ds(h * 32, 32)], sems.at[h]) for h in range(2 * n)
        ]
        for copy in copies:
            copy.start()
        for copy in copies:
            copy.wait()

    low64, low32 = chunk_masks((16, 128))
    if first:
        o_ref[...] = jnp.zeros_like(o_ref)
    else:
        o_ref[...] = p_ref[...]

    def product(row, s, a):
        k = kcol[((s * 4 + step) * 8 + row) * SK + a] + 64 * s
        blk = kohn[s][0, row // 4, row % 4, a * 32:(a + 1) * 32, :]
        left = jnp.concatenate([blk[:, :B], blk[:, B:]], axis=0)
        return k, jnp.dot(left, dens[k], preferred_element_type=jnp.float32)

    def add(row, k, r):
        us = []
        for t in range(2):
            v = [r[ch * 16:(ch + 1) * 16, t * 128:(t + 1) * 128] for ch in range(4)]
            w = [None] * 4
            for c0 in range(2):
                lo, hi = v[c0], v[2 + c0]
                w[c0] = jnp.where(low64, lo, pltpu.roll(hi, 64, 1))
                w[2 + c0] = jnp.where(low64, pltpu.roll(lo, 64, 1), hi)
            for b1 in range(2):
                lo, hi = w[2 * b1], w[2 * b1 + 1]
                us.append(jnp.where(low32, lo, pltpu.roll(hi, 32, 1)))
                us.append(jnp.where(low32, pltpu.roll(lo, 96, 1), hi))
        js = [jcol[k * SP + b] for b in range(SP)]
        old = [o_ref[0, row, j] for j in js]
        for b in range(SP):
            o_ref[0, row, js[b]] = old[b] + us[b]

    def one_row(row, _):
        todo = [(s, a) for s in range(n) for a in range(SK)]
        held = [product(row, *todo[0]), product(row, *todo[1])]
        for i in range(len(todo)):
            if i + 2 < len(todo):
                held.append(product(row, *todo[i + 2]))
            add(row, *held[i])
        return 0

    lax.fori_loop(0, 8, one_row, 0)


def panel_sums(kcol, jcol, kohn, halves, sums):
    n, first = len(kohn), sums is None
    k_spec = pl.BlockSpec((1, 2, 4, 128, 128), lambda o, *_: (o, 0, 0, 0, 0))
    s_spec = pl.BlockSpec((1, 8, NCW, 16, 128), lambda o, *_: (o, 0, 0, 0, 0))
    any_spec = pl.BlockSpec(memory_space=pl.ANY)
    return pl.pallas_call(
        lambda *refs: panel_kernel(n, first, *refs),
        grid_spec=pltpu.PrefetchScalarGridSpec(
            num_scalar_prefetch=2,
            grid=(4,),
            in_specs=[k_spec] * n + [any_spec] * (2 * n) + [s_spec] * (not first),
            out_specs=s_spec,
            scratch_shapes=[pltpu.VMEM((n * 64, B, SP * HALF), jnp.bfloat16), pltpu.SemaphoreType.DMA((2 * n,))],
        ),
        out_shape=jax.ShapeDtypeStruct((4, 8, NCW, 16, 128), jnp.float32),
        compiler_params=pltpu.CompilerParams(vmem_limit_bytes=40 << 20),
        cost_estimate=pl.CostEstimate(
            flops=2 * n * 128 * 64 * 64 * 256, bytes_accessed=(3 * n + 16) << 20, transcendentals=0
        ),
        name="panel_sums_%d" % n if not first else "panel_sums_first",
    )(kcol, jcol, *kohn, *halves, *(() if first else (sums,)))


def pack_kernel(slots, own, low_p, low_m, high_p, high_m, o_ref, total, codes):
    rows = lax.broadcasted_iota(jnp.int32, (16, 128), 0)

    def clear(n, _):
        for m in range(4):
            o_ref[n * 4 + m] = jnp.zeros((MSG, 128), jnp.int16)
            codes[n * 4 + m] = jnp.zeros((16, 128), jnp.int32)
        return 0

    lax.fori_loop(0, 32, clear, 0)

    def gather(m, p_ref, m_ref):
        def one(row, _):
            top = jnp.zeros((16, 128), jnp.float32)
            for j in range(NCW):
                g = own[0, m * 4 + row, j] + p_ref[row, j] + m_ref[row, j]
                total[j] = g
                top = jnp.maximum(top, jnp.abs(g))
            top = jnp.maximum(jnp.max(top, axis=0, keepdims=True), 2.0 ** -110)
            code = jnp.floor(jnp.log2(top) * 256.0) + 1.0
            scale = jnp.exp2(code * (-1.0 / 256.0)) * TOP
            code = jnp.broadcast_to(code.astype(jnp.int32), (16, 128))
            scale = jnp.broadcast_to(scale, (16, 128))
            for j in range(NCW):
                slot = slots[(m * 4 + row) * NCW + j]
                d, s = slot // 4, slot % 4
                q = jnp.floor(total[j] * scale + 0.5).astype(jnp.int32).astype(jnp.int16)
                o_ref[d, pl.ds(pl.multiple_of(s * 16, 16), 16), :] = q
                codes[d] = jnp.where(rows == s, code, codes[d])
            return 0

        lax.fori_loop(0, 4, one, 0)

    gather(0, low_p, low_m)
    gather(1, high_p, high_m)

    def finish(n, _):
        for m in range(4):
            o_ref[n * 4 + m, 64:80, :] = codes[n * 4 + m].astype(jnp.int16)
        return 0

    lax.fori_loop(0, 32, finish, 0)


def pack(slots, sums, low_p, low_m, high_p, high_m):
    part = pl.BlockSpec((4, NCW, 16, 128), lambda i, *_: (0, 0, 0, 0), pipeline_mode=pl.Buffered(1))
    return pl.pallas_call(
        pack_kernel,
        grid_spec=pltpu.PrefetchScalarGridSpec(
            num_scalar_prefetch=1,
            grid=(1,),
            in_specs=[
                pl.BlockSpec((1, 8, NCW, 16, 128), lambda i, *_: (3, 0, 0, 0, 0), pipeline_mode=pl.Buffered(1))
            ] + [part] * 4,
            out_specs=pl.BlockSpec((128, MSG, 128), lambda i, *_: (0, 0, 0), pipeline_mode=pl.Buffered(1)),
            scratch_shapes=[pltpu.VMEM((NCW, 16, 128), jnp.float32), pltpu.VMEM((128, 16, 128), jnp.int32)],
        ),
        out_shape=jax.ShapeDtypeStruct((128, MSG, 128), jnp.int16),
        compiler_params=pltpu.CompilerParams(vmem_limit_bytes=32 << 20),
        name="pack",
    )(slots, sums, low_p, low_m, high_p, high_m)


def unpack_kernel(r_ref, o_ref, full):
    _, low32 = chunk_masks((16, 128))
    for s in range(2):
        def one(n, _):
            scales = []
            for c in range(2):
                code = r_ref[0, c, n, 64:80, :].astype(jnp.int32).astype(jnp.float32)
                scales.append(jnp.exp2(code * (1.0 / 256.0)) * (1.0 / TOP))
            for t in range(2):
                h = []
                for c in range(2):
                    at = (s * 2 + t) * 16
                    q = r_ref[0, c, n, at:at + 16, :].astype(jnp.int32).astype(jnp.float32)
                    h.append(q * scales[c][s * 2 + t:s * 2 + t + 1, :])
                base = pl.multiple_of(((s * 16 + n) * 2 + t) * 32, 32)
                full[pl.ds(base, 16), :] = jnp.where(low32, h[0], pltpu.roll(h[1], 32, 1))
                full[pl.ds(base + 16, 16), :] = jnp.where(low32, pltpu.roll(h[0], 96, 1), h[1])
            return 0

        lax.fori_loop(0, 16, one, 0)
    for p in range(32):
        o_ref[:, p * 128:(p + 1) * 128] = full[pl.ds(p, 64, stride=32), :]


def unpack(received):
    return pl.pallas_call(
        unpack_kernel,
        grid=(X,),
        in_specs=[pl.BlockSpec((1, C, 16, MSG, 128), lambda x: (x, 0, 0, 0, 0))],
        out_specs=pl.BlockSpec((64, 4096), lambda x: (x, 0)),
        out_shape=jax.ShapeDtypeStruct((256, 4096), jnp.float32),
        scratch_shapes=[pltpu.VMEM((64 * 32, 128), jnp.float32)],
        compiler_params=pltpu.CompilerParams(vmem_limit_bytes=32 << 20),
        name="unpack",
    )(received)


def local(kohn_blocks, kohn_columns, density_blocks, density_columns, owner_map):
    x, c = lax.axis_index("x"), lax.axis_index("core")
    z, y = lax.axis_index("z"), lax.axis_index("y")
    on_line, on_cross = jnp.where(c == 0, z, y), jnp.where(c == 0, y, z)
    targets = (on_cross + jnp.array([2, 1, 3, 0], jnp.int32)) % 4

    def rows_of(t):
        return jnp.where(c == 0, t * Y + targets, targets * Y + t)

    ints = jnp.concatenate([kohn_columns.reshape(-1), density_columns.reshape(-1), owner_map.reshape(-1)])
    other = over_core(ints)
    columns = jnp.concatenate([ints[256:320], other[256:320]])
    columns = jnp.concatenate([columns, over_x(columns, 1), over_x(columns, -1), over_x(columns, 2)])
    words = jnp.concatenate([columns, ints[:256], other[:256]]).reshape(8, 128)
    words = [words, over_line(words, 1), over_line(words, -1), over_line(words, 2)]

    def indices(word):
        word = word.reshape(-1)
        k = word[512:].reshape(2, 16, 4, SK)[:, rows_of(on_line)].transpose(1, 0, 2, 3).reshape(-1)
        away = ((k >> 4) - x) & 3
        slot = jnp.where(away == 0, 0, jnp.where(away == 3, 1, away + 1))
        return slot * 16 + ((k & 15) ^ (8 * c)), word[:512]

    kcols, jcols = zip(*[indices(word) for word in words])

    owners = jnp.stack([ints[320:], other[320:]])
    hit = (owners[..., None] == jnp.arange(128, dtype=jnp.int32)).astype(jnp.int32)
    ranks = jnp.sum(jnp.cumsum(hit, axis=1) * hit, axis=2) - 1
    source = jnp.arange(2, dtype=jnp.int32)[:, None] ^ c
    slots = (owners * 4 + source * 2 + ranks).reshape(-1)

    halves = density_blocks.reshape(8, SP, B, 2, HALF).transpose(3, 0, 2, 1, 4).reshape(2, 8, B, SP * HALF)
    mine = lax.dynamic_index_in_dim(halves, c, 0, keepdims=False)
    theirs = over_core(lax.dynamic_index_in_dim(halves, 1 - c, 0, keepdims=False))
    left0, right0 = over_x(mine, 1), over_x(mine, -1)
    left1, right1 = over_x(theirs, 1), over_x(theirs, -1)
    far0, far1 = over_x(left0, 1), over_x(right1, -1)
    low = jnp.concatenate([mine, theirs, left0, left1])
    high = jnp.concatenate([right0, right1, far0, far1])

    prev_low, prev_high = over_line(low, 1), over_line(high, 1)
    next_high, next_low = over_line(high, -1), over_line(low, -1)
    far_low, far_high = over_line(prev_low, 1), over_line(next_high, -1)

    kohn = kohn_blocks.reshape(16, 4, SK * 32, 128)
    kohn_other = over_core(kohn)

    def rows_for(step):
        rows = rows_of((on_line + step) % 4)
        return jnp.stack([kohn[rows], kohn_other[rows]], axis=1)

    kohn_prev, kohn_next = over_line(rows_for(1), 1), over_line(rows_for(3), -1)
    opposite = rows_for(2)
    opposite0 = over_line(over_line(opposite[:2], 1), 1)
    opposite1 = over_line(over_line(opposite[2:], -1), -1)
    kohn_far = jnp.concatenate([opposite0, opposite1])

    sums = panel_sums(kcols[0], jcols[0], [rows_for(0)], [low, high], None)
    sums = panel_sums(
        jnp.concatenate(kcols[1:3]), jnp.concatenate(jcols[1:3]), [kohn_prev, kohn_next],
        [prev_low, prev_high, next_low, next_high], sums,
    )
    sums = panel_sums(kcols[3], jcols[3], [kohn_far], [far_low, far_high], sums)

    via_next, via_prev = over_cross(sums[0, :4], 1), over_cross(sums[0, 4:], -1)
    high_p, low_m = over_cross(sums[1, 4:], 1), over_cross(sums[2, :4], -1)
    low_p = over_cross(sums[1, :4] + via_next, 1)
    high_m = over_cross(sums[2, 4:] + via_prev, -1)

    outgoing = pack(slots, sums, low_p, low_m, high_p, high_m)
    received = lax.all_to_all(outgoing, ALL, split_axis=0, concat_axis=0, tiled=True)
    return unpack(received.reshape(X, C, 16, MSG, 128))


def solution(mesh):
    grid = Mesh(mesh.devices.reshape(X, C, Z, Y), ALL)
    row, col = ("x", "core"), ("z", "y")
    return jax.shard_map(
        local,
        mesh=grid,
        in_specs=(
            P(row, col, None, None),
            P(row, col, None),
            P(col, row, None, None),
            P(col, row, None),
            P(ALL, None),
        ),
        out_specs=P(ALL, None),
        check_vma=False,
    )
```

```python
import jax
import jax.numpy as jnp
from jax import lax
from jax.experimental import pallas as pl
from jax.experimental.pallas import tpu as pltpu
from jax.sharding import Mesh, PartitionSpec as P

B = 64
HALF = 32
NCW = 32
SK = 4
SP = 8
X, C, Z, Y = 4, 2, 4, 4
ALL = ("x", "core", "z", "y")
PLANE = ("core", "z", "y")
TOP = 32766.0
MSG = 80


def lines(along):
    groups = []
    for c in range(C):
        for fixed in range(4):
            on_z = (c ^ along) == 0
            groups.append([(c * Z + (i if on_z else fixed)) * Y + (fixed if on_z else i) for i in range(4)])
    return groups


LINE, CROSS = lines(0), lines(1)


def over_line(v, step):
    pairs = [(group[i], group[(i + step) % 4]) for group in LINE for i in range(4)]
    return lax.ppermute(v, PLANE, pairs)


def over_x(v, step):
    return lax.ppermute(v, "x", [(i, (i + step) % X) for i in range(X)])


def over_core(v):
    return lax.ppermute(v, "core", [(0, 1), (1, 0)])


def regroup_kernel(core, mine, other, o_ref, sems):
    swapped = core[0] == 1
    copies = []
    for z in range(Z):
        for y in range(Y):
            t, o = jnp.where(swapped, y, z), jnp.where(swapped, z, y)
            for m, src in enumerate((mine, other)):
                copies.append(pltpu.make_async_copy(src.at[z * Y + y], o_ref.at[t, m, o], sems.at[len(copies)]))
    for copy in copies:
        copy.start()
    for copy in copies:
        copy.wait()


def regroup(core, mine, other):
    any_spec = pl.BlockSpec(memory_space=pl.ANY)
    return pl.pallas_call(
        regroup_kernel,
        grid_spec=pltpu.PrefetchScalarGridSpec(
            num_scalar_prefetch=1, grid=(1,), in_specs=[any_spec] * 2, out_specs=any_spec,
            scratch_shapes=[pltpu.SemaphoreType.DMA((32,))],
        ),
        out_shape=jax.ShapeDtypeStruct((4, 2, 4, 4, 128, 128), jnp.bfloat16),
        name="regroup",
    )(core, mine, other)


def encode(values, o_ref, at, write_code):
    top = jnp.zeros((16, 128), jnp.float32)
    for j in range(NCW):
        top = jnp.maximum(top, jnp.abs(values[j]))
    top = jnp.maximum(jnp.max(top, axis=0, keepdims=True), 2.0 ** -110)
    code = jnp.floor(jnp.log2(top) * 256.0) + 1.0
    scale = jnp.broadcast_to(jnp.exp2(code * (-1.0 / 256.0)) * TOP, (16, 128))
    write_code(jnp.broadcast_to(code.astype(jnp.int32), (16, 128)))
    for j in range(NCW):
        q = jnp.floor(values[j] * scale + 0.5).astype(jnp.int32).astype(jnp.int16)
        o_ref[at(j)] = q


def decoded_scale(code):
    return jnp.exp2(code.astype(jnp.int32).astype(jnp.float32) * (1.0 / 256.0)) * (1.0 / TOP)


def panel_kernel(n, first, kcol, jcol, place, *refs):
    kohn, panels, refs = refs[:n], refs[n], refs[n + 1:]
    if not first:
        p_ref, refs = refs[0], refs[1:]
    o_ref, dens, sems, acc = refs
    step = pl.program_id(0)

    @pl.when(step == 0)
    def _():
        copies = []
        for s in range(n):
            src = panels if first else panels.at[(place[0] + 1 + s) % 4]
            copies.append(pltpu.make_async_copy(src, dens.at[pl.ds(s * 64, 64)], sems.at[s]))
        for copy in copies:
            copy.start()
        for copy in copies:
            copy.wait()

    low = (lax.broadcasted_iota(jnp.int32, (32, 128), 1) < 64).astype(jnp.float32).astype(jnp.bfloat16)
    high = 1 - low
    zero = jnp.zeros((128, 128), jnp.bfloat16)

    def twice(blk):
        turned = jnp.concatenate([blk[:, B:], blk[:, :B]], axis=1)
        return jnp.concatenate([blk * low, turned * low, turned * high, blk * high], axis=0)

    def product(row, s, a):
        ks, weights = [], []
        for i in range(2):
            ks.append(kcol[((s * 4 + step) * 8 + row) * SK + a + i] + 64 * s)
            weights.append(twice(kohn[s][0, row // 4, 0, row % 4, (a + i) * 32:(a + i + 1) * 32, :]))
        left = jnp.concatenate([dens[ks[0]], dens[ks[1]]], axis=1)
        right = jnp.concatenate([
            jnp.concatenate([weights[0], zero], axis=1), jnp.concatenate([zero, weights[1]], axis=1)
        ], axis=0)
        r = lax.dot_general(left, right, (((1,), (1,)), ((), ())), preferred_element_type=jnp.float32)
        return ks, r

    def add(sums, ks, r):
        for i in range(2):
            js = [jcol[ks[i] * SP + b] for b in range(SP)]
            old = [sums[j] for j in js]
            for b in range(SP):
                sums[js[b]] = old[b] + r[b * 16:(b + 1) * 16, i * 128:(i + 1) * 128]

    todo = [(s, a) for s in range(n) for a in range(0, SK, 2)]

    def some_rows(row, _):
        rows = [row * 2, row * 2 + 1] if first else [row]
        work = [(q, r, s, a) for q, r in enumerate(rows) for s, a in todo]
        sums = []
        for q, r in enumerate(rows):
            if first:
                o_ref[0, r] = jnp.zeros((NCW, 16, 128), jnp.float32)
                sums.append(o_ref.at[0, r])
            else:
                acc[...] = p_ref[0, r]
                sums.append(acc)
        held = [product(*work[i][1:]) for i in range(2)]
        for i in range(len(work)):
            if i + 2 < len(work):
                held.append(product(*work[i + 2][1:]))
            add(sums[work[i][0]], *held[i])
        if not first:
            def write_code(code):
                o_ref[0, row, NCW] = code.astype(jnp.int16)

            encode(acc, o_ref, lambda j: (0, row, j), write_code)
        return 0

    lax.fori_loop(0, 4 if first else 8, some_rows, 0)


def panel_sums(kcol, jcol, place, kohn, panels, sums):
    first = sums is None
    n = 1 if first else 3
    offset = 0 if first else 1

    def k_spec(s):
        return pl.BlockSpec(
            (1, 2, 1, 4, 128, 128), lambda o, kcol, jcol, place: ((place[0] + s + offset) % 4, 0, o, 0, 0, 0)
        )

    s_spec = pl.BlockSpec((1, 8, NCW, 16, 128), lambda o, *_: (o, 0, 0, 0, 0))
    q_spec = pl.BlockSpec((1, 8, NCW + 1, 16, 128), lambda o, *_: (o, 0, 0, 0, 0))
    any_spec = pl.BlockSpec(memory_space=pl.ANY)
    if first:
        out_spec, out_shape = s_spec, jax.ShapeDtypeStruct((4, 8, NCW, 16, 128), jnp.float32)
    else:
        out_spec, out_shape = q_spec, jax.ShapeDtypeStruct((4, 8, NCW + 1, 16, 128), jnp.int16)
    return pl.pallas_call(
        lambda *refs: panel_kernel(n, first, *refs),
        grid_spec=pltpu.PrefetchScalarGridSpec(
            num_scalar_prefetch=3,
            grid=(4,),
            in_specs=[k_spec(s) for s in range(n)] + [any_spec] + [s_spec] * (not first),
            out_specs=out_spec,
            scratch_shapes=[
                pltpu.VMEM((n * 64, 128, 128), jnp.bfloat16),
                pltpu.SemaphoreType.DMA((n,)),
                pltpu.VMEM((NCW, 16, 128), jnp.float32),
            ],
        ),
        out_shape=out_shape,
        compiler_params=pltpu.CompilerParams(vmem_limit_bytes=40 << 20),
        cost_estimate=pl.CostEstimate(
            flops=2 * n * 128 * 128 * 128 * 128, bytes_accessed=(3 * n + 12) << 20, transcendentals=0
        ),
        name="own_panel" if first else "other_panels",
    )(kcol, jcol, place, *([kohn] * n), panels, *(() if first else (sums,)))


def pack_kernel(slots, r_ref, o_ref, total, codes):
    rows = lax.broadcasted_iota(jnp.int32, (16, 128), 0)
    lane = lax.broadcasted_iota(jnp.int32, (16, 128), 1)

    def clear(n, _):
        for m in range(4):
            o_ref[n * 4 + m] = jnp.zeros((MSG, 128), jnp.int16)
            codes[n * 4 + m] = jnp.zeros((16, 128), jnp.int32)
        return 0

    lax.fori_loop(0, 32, clear, 0)

    def one(row, _):
        scales = [decoded_scale(r_ref[src, row, NCW]) for src in range(4)]
        for group in range(NCW // 8):
            blocks = []
            for j in range(group * 8, group * 8 + 8):
                g = [r_ref[src, row, j].astype(jnp.int32).astype(jnp.float32) * scales[src] for src in range(4)]
                blocks.append((g[0] + g[1]) + (g[2] + g[3]))
            turned = jnp.concatenate(blocks, axis=0).T
            v = []
            for q in range(8):
                par, mh, zh = q // 4, (q // 2) % 2, q % 2
                at = (zh * 4 + par * 2 + mh) * 16
                v.append(turned[at:at + 16, :])
            for bit in (4, 2, 1):
                keep = (lane & (16 * bit)) == 0
                w = [None] * 8
                for i in range(8):
                    if not i & bit:
                        lo, hi = v[i], v[i | bit]
                        w[i] = jnp.where(keep, lo, pltpu.roll(hi, 16 * bit, 1))
                        w[i | bit] = jnp.where(keep, pltpu.roll(lo, 128 - 16 * bit, 1), hi)
                v = w
            for j in range(8):
                total[group * 8 + j] = v[j]

        def where_to(j):
            slot = slots[row * NCW + j]
            return slot // 4, pl.ds(pl.multiple_of((slot % 4) * 16, 16), 16), slice(None)

        def write_code(code):
            for j in range(NCW):
                slot = slots[row * NCW + j]
                codes[slot // 4] = jnp.where(rows == slot % 4, code, codes[slot // 4])

        encode(total, o_ref, where_to, write_code)
        return 0

    lax.fori_loop(0, 8, one, 0)

    def finish(n, _):
        for m in range(4):
            o_ref[n * 4 + m, 64:80, :] = codes[n * 4 + m].astype(jnp.int16)
        return 0

    lax.fori_loop(0, 32, finish, 0)


def pack(slots, parts):
    return pl.pallas_call(
        pack_kernel,
        grid_spec=pltpu.PrefetchScalarGridSpec(
            num_scalar_prefetch=1,
            grid=(1,),
            in_specs=[
                pl.BlockSpec((4, 8, NCW + 1, 16, 128), lambda i, *_: (0, 0, 0, 0, 0), pipeline_mode=pl.Buffered(1))
            ],
            out_specs=pl.BlockSpec((128, MSG, 128), lambda i, *_: (0, 0, 0), pipeline_mode=pl.Buffered(1)),
            scratch_shapes=[pltpu.VMEM((NCW, 16, 128), jnp.float32), pltpu.VMEM((128, 16, 128), jnp.int32)],
        ),
        out_shape=jax.ShapeDtypeStruct((128, MSG, 128), jnp.int16),
        compiler_params=pltpu.CompilerParams(vmem_limit_bytes=32 << 20),
        name="pack",
    )(slots, parts)


def unpack_kernel(r_ref, o_ref, full):
    low32 = (lax.broadcasted_iota(jnp.int32, (16, 128), 1) & 32) == 0
    for s in range(2):
        def one(n, _):
            scales = [decoded_scale(r_ref[0, c, n, 64:80, :]) for c in range(2)]
            for t in range(2):
                h = []
                for c in range(2):
                    at = (s * 2 + t) * 16
                    q = r_ref[0, c, n, at:at + 16, :].astype(jnp.int32).astype(jnp.float32)
                    h.append(q * scales[c][s * 2 + t:s * 2 + t + 1, :])
                base = pl.multiple_of(((s * 16 + n) * 2 + t) * 32, 32)
                full[pl.ds(base, 16), :] = jnp.where(low32, h[0], pltpu.roll(h[1], 32, 1))
                full[pl.ds(base + 16, 16), :] = jnp.where(low32, pltpu.roll(h[0], 96, 1), h[1])
            return 0

        lax.fori_loop(0, 16, one, 0, unroll=4)
    for p in range(32):
        o_ref[:, p * 128:(p + 1) * 128] = full[pl.ds(p, 64, stride=32), :]


def unpack(received):
    return pl.pallas_call(
        unpack_kernel,
        grid=(X,),
        in_specs=[pl.BlockSpec((1, C, 16, MSG, 128), lambda x: (x, 0, 0, 0, 0))],
        out_specs=pl.BlockSpec((64, 4096), lambda x: (x, 0)),
        out_shape=jax.ShapeDtypeStruct((256, 4096), jnp.float32),
        scratch_shapes=[pltpu.VMEM((64 * 32, 128), jnp.float32)],
        compiler_params=pltpu.CompilerParams(vmem_limit_bytes=32 << 20),
        name="unpack",
    )(received)


def local(kohn_blocks, kohn_columns, density_blocks, density_columns, owner_map):
    x, c = lax.axis_index("x"), lax.axis_index("core")
    z, y = lax.axis_index("z"), lax.axis_index("y")
    on_line = jnp.where(c == 0, z, y)
    place = on_line.reshape(1)
    four = jnp.arange(4, dtype=jnp.int32)

    halves = density_blocks.reshape(8, SP, B, C, 2, 16).transpose(3, 0, 1, 5, 4, 2).reshape(C, 8, 128, 128)
    mine = lax.dynamic_index_in_dim(halves, c, 0, keepdims=False)
    theirs = over_core(lax.dynamic_index_in_dim(halves, 1 - c, 0, keepdims=False))
    panel = lax.all_gather(jnp.concatenate([mine, theirs]), "x", axis=0, tiled=True)
    panels = lax.all_gather(panel, PLANE, axis_index_groups=LINE)

    ints = jnp.concatenate([kohn_columns.reshape(-1), density_columns.reshape(-1), owner_map.reshape(-1)])
    other = over_core(ints)
    columns = jnp.concatenate([ints[256:320], other[256:320]])
    columns = jnp.stack([columns, over_x(columns, -1), over_x(columns, 2), over_x(columns, 1)])
    columns = columns[(four - x) & 3].reshape(-1)
    words = jnp.concatenate([columns, ints[:256], other[:256]]).reshape(8, 128)
    words = [words, over_line(words, -1), over_line(words, 2), over_line(words, 1)]

    def indices(word):
        word = word.reshape(-1)
        rows = jnp.where(c == 0, on_line * Y + four, four * Y + on_line)
        k = word[512:].reshape(2, 16, 4, SK)[:, rows].transpose(1, 0, 2, 3).reshape(-1)
        return k ^ (8 * c), word[:512]

    kcols, jcols = zip(*[indices(word) for word in words])

    owners = jnp.stack([ints[320:], other[320:]])
    hit = (owners[..., None] == jnp.arange(128, dtype=jnp.int32)).astype(jnp.int32)
    ranks = jnp.sum(jnp.cumsum(hit, axis=1) * hit, axis=2) - 1
    source = jnp.arange(2, dtype=jnp.int32)[:, None] ^ c
    slots = (owners * 4 + source * 2 + ranks).reshape(-1)

    kohn = kohn_blocks.reshape(16, 4, SK * 32, 128)
    kohn = regroup(c.reshape(1), kohn, over_core(kohn))
    kohn_line = lax.all_to_all(kohn, PLANE, 0, 0, axis_index_groups=LINE, tiled=True)

    sums = panel_sums(kcols[0], jcols[0], place, kohn, panel, None)
    sums = panel_sums(jnp.concatenate(kcols[1:]), jnp.concatenate(jcols[1:]), place, kohn_line, panels, sums)
    parts = lax.all_to_all(sums, PLANE, 0, 0, axis_index_groups=CROSS, tiled=True)
    outgoing = pack(slots, parts)
    received = lax.all_to_all(outgoing, ALL, split_axis=0, concat_axis=0, tiled=True)
    return unpack(received.reshape(X, C, 16, MSG, 128))


def solution(mesh):
    grid = Mesh(mesh.devices.reshape(X, C, Z, Y), ALL)
    row, col = ("x", "core"), ("z", "y")
    return jax.shard_map(
        local,
        mesh=grid,
        in_specs=(
            P(row, col, None, None),
            P(row, col, None),
            P(col, row, None, None),
            P(col, row, None),
            P(ALL, None),
        ),
        out_specs=P(ALL, None),
        check_vma=False,
    )
```

```python
import jax
import jax.numpy as jnp
from jax import lax
from jax.experimental import pallas as pl
from jax.experimental.pallas import tpu as pltpu
from jax.sharding import Mesh, PartitionSpec as P

B = 64
HALF = 32
NCW = 32
SK = 4
SP = 8
X, C, Z, Y = 4, 2, 4, 4
ALL = ("x", "core", "z", "y")
PLANE = ("core", "z", "y")
TOP = 32766.0
MSG = 80
ORDER = (2, 1, 3, 0)


def lines(along):
    groups = []
    for c in range(C):
        for fixed in range(4):
            on_z = (c ^ along) == 0
            groups.append([(c * Z + (i if on_z else fixed)) * Y + (fixed if on_z else i) for i in range(4)])
    return groups


LINE, CROSS = lines(0), lines(1)


def over(groups, v, step):
    return lax.ppermute(v, PLANE, [(group[i], group[(i + step) % 4]) for group in groups for i in range(4)])


def over_line(v, step):
    return over(LINE, v, step)


def over_cross(v, step):
    return over(CROSS, v, step)


def over_x(v, step):
    return lax.ppermute(v, "x", [(i, (i + step) % X) for i in range(X)])


def over_core(v):
    return lax.ppermute(v, "core", [(0, 1), (1, 0)])


def split_kernel(core, d_ref, mine, theirs, flat, wide):
    lane32 = lax.broadcasted_iota(jnp.int32, (32, 128), 1)
    lane64 = lax.broadcasted_iota(jnp.int32, (64, 128), 1)

    def one(k, _):
        rows = d_ref[k].astype(jnp.float32)
        for p in range(32):
            flat[p * 8:(p + 1) * 8, :] = rows[:, p * 128:(p + 1) * 128]
        v = []
        for b in range(4):
            lo, hi = flat[pl.ds(b, 32, stride=8), :], flat[pl.ds(b + 4, 32, stride=8), :]
            wide[b, pl.ds(0, 32, stride=2), :] = jnp.where(lane32 < 64, lo, pltpu.roll(hi, 64, 1))
            wide[b, pl.ds(1, 32, stride=2), :] = jnp.where(lane32 < 64, pltpu.roll(lo, 64, 1), hi)
        v = [wide[b] for b in range(4)]
        for bit in (2, 1):
            keep = (lane64 & (16 * bit)) == 0
            w = [None] * 4
            for i in range(4):
                if not i & bit:
                    lo, hi = v[i], v[i | bit]
                    w[i] = jnp.where(keep, lo, pltpu.roll(hi, 16 * bit, 1))
                    w[i | bit] = jnp.where(keep, pltpu.roll(lo, 128 - 16 * bit, 1), hi)
            v = w
        first = jnp.concatenate([v[0], v[1]], axis=0).T
        second = jnp.concatenate([v[2], v[3]], axis=0).T
        swapped = core[0] == 1
        mine[k] = jnp.where(swapped, second, first).astype(jnp.bfloat16)
        theirs[k] = jnp.where(swapped, first, second).astype(jnp.bfloat16)
        return 0

    lax.fori_loop(0, 8, one, 0)


def split(core, dens):
    half = jax.ShapeDtypeStruct((8, 128, 128), jnp.bfloat16)
    whole = pl.BlockSpec((8, 128, 128), lambda i, *_: (0, 0, 0))
    return pl.pallas_call(
        split_kernel,
        grid_spec=pltpu.PrefetchScalarGridSpec(
            num_scalar_prefetch=1, grid=(1,),
            in_specs=[pl.BlockSpec((8, SP, B * B), lambda i, *_: (0, 0, 0))],
            out_specs=[whole, whole],
            scratch_shapes=[pltpu.VMEM((256, 128), jnp.float32), pltpu.VMEM((4, B, 128), jnp.float32)],
        ),
        out_shape=[half, half],
        name="split",
    )(core, dens)


def regroup_kernel(at, mine, other, own, after, before, far0, far1, sems):
    swapped, line, cross = at[0] == 1, at[1], at[2]
    copies = []
    for step, dst in enumerate((own, after, None, before)):
        t = (line + step) % 4
        for i, rel in enumerate(ORDER):
            o = (cross + rel) % 4
            row = jnp.where(swapped, o * 4 + t, t * 4 + o)
            for m, src in enumerate((mine, other)):
                to = (far0, far1)[m].at[i] if dst is None else dst.at[m, i]
                copies.append(pltpu.make_async_copy(src.at[row], to, sems.at[len(copies)]))
    for copy in copies:
        copy.start()
    for copy in copies:
        copy.wait()


def regroup(at, mine, other):
    two, one = (2, 4, 4, 128, 128), (4, 4, 128, 128)
    shapes = [two, two, two, one, one]
    return pl.pallas_call(
        regroup_kernel,
        grid_spec=pltpu.PrefetchScalarGridSpec(
            num_scalar_prefetch=1, grid=(1,), in_specs=[pl.BlockSpec(memory_space=pl.ANY)] * 2,
            out_specs=[pl.BlockSpec(shape, lambda i, *_, n=len(shape): (0,) * n) for shape in shapes],
            scratch_shapes=[pltpu.SemaphoreType.DMA((32,))],
        ),
        out_shape=[jax.ShapeDtypeStruct(shape, jnp.bfloat16) for shape in shapes],
        compiler_params=pltpu.CompilerParams(vmem_limit_bytes=24 << 20),
        name="regroup",
    )(at, mine, other)


def encode(values, put, write_code):
    top = jnp.zeros((16, 128), jnp.float32)
    for j in range(NCW):
        top = jnp.maximum(top, jnp.abs(values[j]))
    top = jnp.maximum(jnp.max(top, axis=0, keepdims=True), 2.0 ** -110)
    code = jnp.floor(jnp.log2(top) * 256.0) + 1.0
    scale = jnp.broadcast_to(jnp.exp2(code * (-1.0 / 256.0)) * TOP, (16, 128))
    write_code(jnp.broadcast_to(code.astype(jnp.int32), (16, 128)))
    for j in range(NCW):
        put(j, jnp.floor(values[j] * scale + 0.5).astype(jnp.int32).astype(jnp.int16))


def decoded_scale(code):
    return jnp.exp2(code.astype(jnp.int32).astype(jnp.float32) * (1.0 / 256.0)) * (1.0 / TOP)


def panel_kernel(n, rows_of_block, has_sums, coded, kcol, jcol, *refs):
    kohn, refs = refs[:2 * n], refs[2 * n:]
    panels, refs = refs[:2 * n], refs[2 * n:]
    if has_sums:
        p_ref, refs = refs[0], refs[1:]
    outs, (dens, sems, acc) = refs[:-3], refs[-3:]
    step = pl.program_id(0) + rows_of_block

    @pl.when(pl.program_id(0) == 0)
    def _():
        copies = [pltpu.make_async_copy(panels[s], dens.at[pl.ds(s * 32, 32)], sems.at[s]) for s in range(2 * n)]
        for copy in copies:
            copy.start()
        for copy in copies:
            copy.wait()

    low = (lax.broadcasted_iota(jnp.int32, (32, 128), 1) < 64).astype(jnp.float32).astype(jnp.bfloat16)
    high = 1 - low
    zero = jnp.zeros((128, 128), jnp.bfloat16)

    def twice(blk):
        turned = jnp.concatenate([blk[:, B:], blk[:, :B]], axis=1)
        return jnp.concatenate([blk * low, turned * low, turned * high, blk * high], axis=0)

    def product(m, r, s, a):
        ks, weights = [], []
        for i in range(2):
            ks.append(kcol[(((s * 4 + step) * 2 + m) * 4 + r) * SK + a + i] + 64 * s)
            weights.append(twice(kohn[2 * s + m][0, 0, r, (a + i) * 32:(a + i + 1) * 32, :]))
        left = jnp.concatenate([dens[ks[0]], dens[ks[1]]], axis=1)
        right = jnp.concatenate([
            jnp.concatenate([weights[0], zero], axis=1), jnp.concatenate([zero, weights[1]], axis=1)
        ], axis=0)
        r = lax.dot_general(left, right, (((1,), (1,)), ((), ())), preferred_element_type=jnp.float32)
        return ks, r

    def add(sums, ks, r):
        for i in range(2):
            js = [jcol[ks[i] * SP + b] for b in range(SP)]
            old = [sums[j] for j in js]
            for b in range(SP):
                sums[js[b]] = old[b] + r[b * 16:(b + 1) * 16, i * 128:(i + 1) * 128]

    def two_rows(m, pair):
        work, sums = [], []
        for q in range(2):
            r = pair * 2 + q
            work += [(q, r, s, a) for s in range(n) for a in range(0, SK, 2)]
            place = acc.at[q] if coded else outs[0].at[0, m * 4 + r]
            place[...] = p_ref[0, m * 4 + r] if has_sums else jnp.zeros((NCW, 16, 128), jnp.float32)
            sums.append(place)
        held = [product(m, *work[i][1:]) for i in range(2)]
        for i in range(len(work)):
            if i + 2 < len(work):
                held.append(product(m, *work[i + 2][1:]))
            add(sums[work[i][0]], *held[i])
        if coded:
            for q in range(2):
                r = pair * 2 + q
                out, row = (outs[m], r) if len(outs) == 2 else (outs[0], m * 4 + r)

                def put(j, value, out=out, row=row):
                    out[row, j] = value

                encode(sums[q], put, lambda code, put=put: put(NCW, code.astype(jnp.int16)))

    for m in range(2):
        lax.fori_loop(0, 2, lambda pair, _, m=m: (two_rows(m, pair), 0)[1], 0)


def panel_sums(name, kcol, jcol, kohn, panels, sums, target=None, coded=False):
    n = len(panels) // 2
    base = 0 if target is None else target
    k_specs = [
        pl.BlockSpec((1, 1, 4, 128, 128), lambda o, *_, m=m: (m, o + base, 0, 0, 0)) for _, m in kohn
    ]
    s_shape = (1, 8, NCW, 16, 128)
    s_spec = pl.BlockSpec(s_shape, lambda o, *_: (o + base, 0, 0, 0, 0))
    o_specs = [pl.BlockSpec(s_shape, lambda o, *_: (o, 0, 0, 0, 0))]
    shapes = [jax.ShapeDtypeStruct((4 if target is None else 1,) + s_shape[1:], jnp.float32)]
    if coded:
        parts = 2 if target == 0 else 1
        o_specs = [pl.BlockSpec((8 // parts, NCW + 1, 16, 128), lambda o, *_: (0, 0, 0, 0))] * parts
        shapes = [jax.ShapeDtypeStruct((8 // parts, NCW + 1, 16, 128), jnp.int16)] * parts
    any_spec = pl.BlockSpec(memory_space=pl.ANY)
    steps = 4 if target is None else 1
    return pl.pallas_call(
        lambda *refs: panel_kernel(n, base, sums is not None, coded, *refs),
        grid_spec=pltpu.PrefetchScalarGridSpec(
            num_scalar_prefetch=2,
            grid=(steps,),
            in_specs=k_specs + [any_spec] * (2 * n) + [s_spec] * (sums is not None),
            out_specs=o_specs,
            scratch_shapes=[
                pltpu.VMEM((n * 64, 128, 128), jnp.bfloat16),
                pltpu.SemaphoreType.DMA((2 * n,)),
                pltpu.VMEM((2, NCW, 16, 128), jnp.float32),
            ],
        ),
        out_shape=shapes,
        compiler_params=pltpu.CompilerParams(vmem_limit_bytes=40 << 20),
        cost_estimate=pl.CostEstimate(
            flops=2 * n * 32 * steps * 128 * 128 * 128, bytes_accessed=(2 * n + 5 * steps) << 20, transcendentals=0
        ),
        name=name,
    )(kcol, jcol, *[array for array, _ in kohn], *panels, *(() if sums is None else (sums,)))


def pack_kernel(slots, own, after, before, far0, far1, o_ref, total, codes):
    rows = lax.broadcasted_iota(jnp.int32, (16, 128), 0)
    lane = lax.broadcasted_iota(jnp.int32, (16, 128), 1)

    def clear(n, _):
        for m in range(4):
            o_ref[n * 4 + m] = jnp.zeros((MSG, 128), jnp.int16)
            codes[n * 4 + m] = jnp.zeros((16, 128), jnp.int32)
        return 0

    lax.fori_loop(0, 32, clear, 0)

    def one(m, r):
        row = m * 4 + r
        coded = [(before, row), (after, row), ((far0, far1)[m], r)]
        scales = [decoded_scale(ref[at, NCW]) for ref, at in coded]
        for group in range(NCW // 8):
            blocks = []
            for j in range(group * 8, group * 8 + 8):
                g = [ref[at, j].astype(jnp.int32).astype(jnp.float32) * scale for (ref, at), scale in zip(coded, scales)]
                blocks.append((own[0, row, j] + g[0]) + (g[1] + g[2]))
            turned = jnp.concatenate(blocks, axis=0).T
            v = []
            for q in range(8):
                par, mh, zh = q // 4, (q // 2) % 2, q % 2
                at = (zh * 4 + par * 2 + mh) * 16
                v.append(turned[at:at + 16, :])
            for bit in (4, 2, 1):
                keep = (lane & (16 * bit)) == 0
                w = [None] * 8
                for i in range(8):
                    if not i & bit:
                        lo, hi = v[i], v[i | bit]
                        w[i] = jnp.where(keep, lo, pltpu.roll(hi, 16 * bit, 1))
                        w[i | bit] = jnp.where(keep, pltpu.roll(lo, 128 - 16 * bit, 1), hi)
                v = w
            for j in range(8):
                total[group * 8 + j] = v[j]

        def put(j, value):
            slot = slots[row * NCW + j]
            o_ref[slot // 4, pl.ds(pl.multiple_of((slot % 4) * 16, 16), 16), :] = value

        def write_code(code):
            for j in range(NCW):
                slot = slots[row * NCW + j]
                codes[slot // 4] = jnp.where(rows == slot % 4, code, codes[slot // 4])

        encode(total, put, write_code)

    for m in range(2):
        lax.fori_loop(0, 4, lambda r, _, m=m: (one(m, r), 0)[1], 0)

    def finish(n, _):
        for m in range(4):
            o_ref[n * 4 + m, 64:80, :] = codes[n * 4 + m].astype(jnp.int16)
        return 0

    lax.fori_loop(0, 32, finish, 0)


def pack(slots, own, after, before, far0, far1):
    def whole(array):
        return pl.BlockSpec(
            array.shape, lambda i, *_, n=array.ndim: (0,) * n, pipeline_mode=pl.Buffered(1)
        )

    return pl.pallas_call(
        pack_kernel,
        grid_spec=pltpu.PrefetchScalarGridSpec(
            num_scalar_prefetch=1,
            grid=(1,),
            in_specs=[whole(array) for array in (own, after, before, far0, far1)],
            out_specs=pl.BlockSpec((128, MSG, 128), lambda i, *_: (0, 0, 0), pipeline_mode=pl.Buffered(1)),
            scratch_shapes=[pltpu.VMEM((NCW, 16, 128), jnp.float32), pltpu.VMEM((128, 16, 128), jnp.int32)],
        ),
        out_shape=jax.ShapeDtypeStruct((128, MSG, 128), jnp.int16),
        compiler_params=pltpu.CompilerParams(vmem_limit_bytes=32 << 20),
        name="pack",
    )(slots, own, after, before, far0, far1)


def unpack_kernel(r_ref, o_ref, full):
    low32 = (lax.broadcasted_iota(jnp.int32, (16, 128), 1) & 32) == 0
    for s in range(2):
        def one(n, _):
            scales = [decoded_scale(r_ref[0, c, n, 64:80, :]) for c in range(2)]
            for t in range(2):
                h = []
                for c in range(2):
                    at = (s * 2 + t) * 16
                    q = r_ref[0, c, n, at:at + 16, :].astype(jnp.int32).astype(jnp.float32)
                    h.append(q * scales[c][s * 2 + t:s * 2 + t + 1, :])
                base = pl.multiple_of(((s * 16 + n) * 2 + t) * 32, 32)
                full[pl.ds(base, 16), :] = jnp.where(low32, h[0], pltpu.roll(h[1], 32, 1))
                full[pl.ds(base + 16, 16), :] = jnp.where(low32, pltpu.roll(h[0], 96, 1), h[1])
            return 0

        lax.fori_loop(0, 16, one, 0, unroll=4)
    for p in range(32):
        o_ref[:, p * 128:(p + 1) * 128] = full[pl.ds(p, 64, stride=32), :]


def unpack(received):
    return pl.pallas_call(
        unpack_kernel,
        grid=(X,),
        in_specs=[pl.BlockSpec((1, C, 16, MSG, 128), lambda x: (x, 0, 0, 0, 0))],
        out_specs=pl.BlockSpec((64, 4096), lambda x: (x, 0)),
        out_shape=jax.ShapeDtypeStruct((256, 4096), jnp.float32),
        scratch_shapes=[pltpu.VMEM((64 * 32, 128), jnp.float32)],
        compiler_params=pltpu.CompilerParams(vmem_limit_bytes=32 << 20),
        name="unpack",
    )(received)


def local(kohn_blocks, kohn_columns, density_blocks, density_columns, owner_map):
    x, c = lax.axis_index("x"), lax.axis_index("core")
    z, y = lax.axis_index("z"), lax.axis_index("y")
    on_line, on_cross = jnp.where(c == 0, z, y), jnp.where(c == 0, y, z)
    four = jnp.arange(4, dtype=jnp.int32)

    mine, theirs = split(c.reshape(1), density_blocks[0])
    theirs = over_core(theirs)
    left0, right0 = over_x(mine, 1), over_x(mine, -1)
    left1, right1 = over_x(theirs, 1), over_x(theirs, -1)
    far0, far1 = over_x(left0, 1), over_x(right1, -1)
    low = jnp.concatenate([mine, theirs, left0, left1])
    high = jnp.concatenate([right0, right1, far0, far1])

    prev_low, prev_high = over_line(low, 1), over_line(high, 1)
    next_high, next_low = over_line(high, -1), over_line(low, -1)
    far_low, far_high = over_line(prev_low, 1), over_line(next_high, -1)

    ints = jnp.concatenate([kohn_columns.reshape(-1), density_columns.reshape(-1), owner_map.reshape(-1)])
    other = over_core(ints)
    columns = jnp.concatenate([ints[256:320], other[256:320]])
    columns = jnp.concatenate([columns, over_x(columns, 1), over_x(columns, -1), over_x(columns, 2)])
    words = jnp.concatenate([columns, ints[:256], other[:256]]).reshape(8, 128)
    words = [words, over_line(words, 1), over_line(words, -1), over_line(words, 2)]

    def indices(word):
        word = word.reshape(-1)
        targets = (on_cross + jnp.array(ORDER, jnp.int32)) % 4
        rows = jnp.where(c == 0, on_line * Y + targets, targets * Y + on_line)
        k = word[512:].reshape(2, 16, 4, SK)[:, rows].transpose(1, 0, 2, 3).reshape(-1)
        away = ((k >> 4) - x) & 3
        slot = jnp.where(away == 0, 0, jnp.where(away == 3, 1, away + 1))
        return slot * 16 + ((k & 15) ^ (8 * c)), word[:512]

    kcols, jcols = zip(*[indices(word) for word in words])

    owners = jnp.stack([ints[320:], other[320:]])
    hit = (owners[..., None] == jnp.arange(128, dtype=jnp.int32)).astype(jnp.int32)
    ranks = jnp.sum(jnp.cumsum(hit, axis=1) * hit, axis=2) - 1
    source = jnp.arange(2, dtype=jnp.int32)[:, None] ^ c
    slots = (owners * 4 + source * 2 + ranks).reshape(-1)

    kohn = kohn_blocks.reshape(16, 4, SK * 32, 128)
    kohn, after, before, opposite0, opposite1 = regroup(
        jnp.stack([c, on_line, on_cross]), kohn, over_core(kohn)
    )
    before, after = over_line(after, 1), over_line(before, -1)
    opposite0 = over_line(over_line(opposite0, 1), 1)
    opposite1 = over_line(over_line(opposite1, -1), -1)

    def both(array):
        return [(array, 0), (array, 1)]

    sums, = panel_sums("own_panel", kcols[0], jcols[0], both(kohn), [low, high], None)
    sums, = panel_sums(
        "near_panels", jnp.concatenate(kcols[1:3]), jnp.concatenate(jcols[1:3]), both(before) + both(after),
        [prev_low, prev_high, next_low, next_high], sums,
    )
    opposite = [(opposite0[None], 0), (opposite1[None], 0)]

    def last(target, coded):
        return panel_sums(
            "last_panel", kcols[3], jcols[3], opposite, [far_low, far_high], sums, target=target, coded=coded
        )

    sums0, sums1 = last(0, True)
    sums0, sums1 = over_cross(sums0, 1), over_cross(sums1, -1)
    to_next, = last(1, True)
    from_prev = over_cross(to_next, 1)
    to_prev, = last(2, True)
    from_next = over_cross(to_prev, -1)
    sums0, sums1 = over_cross(sums0, 1), over_cross(sums1, -1)
    own, = last(3, False)

    outgoing = pack(slots, own, from_next, from_prev, sums0, sums1)
    received = lax.all_to_all(outgoing, ALL, split_axis=0, concat_axis=0, tiled=True)
    return unpack(received.reshape(X, C, 16, MSG, 128))


def solution(mesh):
    grid = Mesh(mesh.devices.reshape(X, C, Z, Y), ALL)
    row, col = ("x", "core"), ("z", "y")
    return jax.shard_map(
        local,
        mesh=grid,
        in_specs=(
            P(row, col, None, None),
            P(row, col, None),
            P(col, row, None, None),
            P(col, row, None),
            P(ALL, None),
        ),
        out_specs=P(ALL, None),
        check_vma=False,
    )
```

```python
import jax
import jax.numpy as jnp
from jax import lax
from jax.experimental import pallas as pl
from jax.experimental.pallas import tpu as pltpu
from jax.sharding import Mesh, PartitionSpec as P

B = 64
HALF = 32
NCW = 32
SK = 4
SP = 8
X, C, Z, Y = 4, 2, 4, 4
ALL = ("x", "core", "z", "y")
PLANE = ("core", "z", "y")
TOP = 32766.0
MSG = 80
PART = 8 * 128 + 16
ORDER = (2, 1, 3, 0)


def lines(along):
    groups = []
    for c in range(C):
        for fixed in range(4):
            on_z = (c ^ along) == 0
            groups.append([(c * Z + (i if on_z else fixed)) * Y + (fixed if on_z else i) for i in range(4)])
    return groups


LINE, CROSS = lines(0), lines(1)


def over(groups, v, step):
    return lax.ppermute(v, PLANE, [(group[i], group[(i + step) % 4]) for group in groups for i in range(4)])


def over_line(v, step):
    return over(LINE, v, step)


def over_cross(v, step):
    return over(CROSS, v, step)


def over_x(v, step):
    return lax.ppermute(v, "x", [(i, (i + step) % X) for i in range(X)])


def over_core(v):
    return lax.ppermute(v, "core", [(0, 1), (1, 0)])


def split_kernel(core, d_ref, i_ref, mine, theirs, flat, wide):
    lane32 = lax.broadcasted_iota(jnp.int32, (32, 128), 1)
    lane64 = lax.broadcasted_iota(jnp.int32, (64, 128), 1)

    def one(k, _):
        rows = d_ref[k].astype(jnp.float32)
        for p in range(32):
            flat[p * 8:(p + 1) * 8, :] = rows[:, p * 128:(p + 1) * 128]
        v = []
        for b in range(4):
            lo, hi = flat[pl.ds(b, 32, stride=8), :], flat[pl.ds(b + 4, 32, stride=8), :]
            wide[b, pl.ds(0, 32, stride=2), :] = jnp.where(lane32 < 64, lo, pltpu.roll(hi, 64, 1))
            wide[b, pl.ds(1, 32, stride=2), :] = jnp.where(lane32 < 64, pltpu.roll(lo, 64, 1), hi)
        v = [wide[b] for b in range(4)]
        for bit in (2, 1):
            keep = (lane64 & (16 * bit)) == 0
            w = [None] * 4
            for i in range(4):
                if not i & bit:
                    lo, hi = v[i], v[i | bit]
                    w[i] = jnp.where(keep, lo, pltpu.roll(hi, 16 * bit, 1))
                    w[i | bit] = jnp.where(keep, pltpu.roll(lo, 128 - 16 * bit, 1), hi)
            v = w
        first = jnp.concatenate([v[0], v[1]], axis=0).T
        second = jnp.concatenate([v[2], v[3]], axis=0).T
        swapped = core[0] == 1
        at = pl.ds(pl.multiple_of(k * 128, 128), 128)
        mine[at, :] = jnp.where(swapped, second, first).astype(jnp.bfloat16)
        theirs[at, :] = jnp.where(swapped, first, second).astype(jnp.bfloat16)
        return 0

    lax.fori_loop(0, 8, one, 0)
    ints = i_ref[...].astype(jnp.float32).astype(jnp.bfloat16)
    mine[8 * 128:, :] = ints
    theirs[8 * 128:, :] = ints


def split(core, dens, ints):
    half = jax.ShapeDtypeStruct((PART, 128), jnp.bfloat16)
    whole = pl.BlockSpec((PART, 128), lambda i, *_: (0, 0))
    return pl.pallas_call(
        split_kernel,
        grid_spec=pltpu.PrefetchScalarGridSpec(
            num_scalar_prefetch=1, grid=(1,),
            in_specs=[
                pl.BlockSpec((8, SP, B * B), lambda i, *_: (0, 0, 0)), pl.BlockSpec((16, 128), lambda i, *_: (0, 0))
            ],
            out_specs=[whole, whole],
            scratch_shapes=[pltpu.VMEM((256, 128), jnp.float32), pltpu.VMEM((4, B, 128), jnp.float32)],
        ),
        out_shape=[half, half],
        name="split",
    )(core, dens, ints)


def regroup_kernel(at, mine, other, own, after, before, far0, far1, sems):
    swapped, line, cross = at[0] == 1, at[1], at[2]
    copies = []
    for step, dst in enumerate((own, after, None, before)):
        t = (line + step) % 4
        for i, rel in enumerate(ORDER):
            o = (cross + rel) % 4
            row = jnp.where(swapped, o * 4 + t, t * 4 + o)
            for m, src in enumerate((mine, other)):
                to = (far0, far1)[m].at[i] if dst is None else dst.at[m, i]
                copies.append(pltpu.make_async_copy(src.at[row], to, sems.at[len(copies)]))
    for copy in copies:
        copy.start()
    for copy in copies:
        copy.wait()


def regroup(at, mine, other):
    two, one = (2, 4, 4, 128, 128), (4, 4, 128, 128)
    shapes = [two, two, two, one, one]
    return pl.pallas_call(
        regroup_kernel,
        grid_spec=pltpu.PrefetchScalarGridSpec(
            num_scalar_prefetch=1, grid=(1,), in_specs=[pl.BlockSpec(memory_space=pl.ANY)] * 2,
            out_specs=[pl.BlockSpec(shape, lambda i, *_, n=len(shape): (0,) * n) for shape in shapes],
            scratch_shapes=[pltpu.SemaphoreType.DMA((32,))],
        ),
        out_shape=[jax.ShapeDtypeStruct(shape, jnp.bfloat16) for shape in shapes],
        compiler_params=pltpu.CompilerParams(vmem_limit_bytes=24 << 20),
        name="regroup",
    )(at, mine, other)


def encode(values, put, write_code):
    top = jnp.zeros((16, 128), jnp.float32)
    for j in range(NCW):
        top = jnp.maximum(top, jnp.abs(values[j]))
    top = jnp.maximum(jnp.max(top, axis=0, keepdims=True), 2.0 ** -110)
    code = jnp.floor(jnp.log2(top) * 256.0) + 1.0
    scale = jnp.broadcast_to(jnp.exp2(code * (-1.0 / 256.0)) * TOP, (16, 128))
    write_code(jnp.broadcast_to(code.astype(jnp.int32), (16, 128)))
    for j in range(NCW):
        put(j, jnp.floor(values[j] * scale + 0.5).astype(jnp.int32).astype(jnp.int16))


def decoded_scale(code):
    return jnp.exp2(code.astype(jnp.int32).astype(jnp.float32) * (1.0 / 256.0)) * (1.0 / TOP)


def panel_kernel(n, pieces, target, has_sums, coded, ints, at, *refs):
    kohn, refs = refs[:2 * n], refs[2 * n:]
    panels, refs = refs[:pieces], refs[pieces:]
    if has_sums:
        p_ref, refs = refs[0], refs[1:]
    outs, (dens, sems, acc) = refs[:-3], refs[-3:]
    size = n * 8 * PART // pieces
    core, line, cross, x = at[0], at[1], at[2], at[3]
    if target is None:
        step = pl.program_id(0)
        ahead = jnp.where(step == 0, ORDER[0], jnp.where(step == 1, ORDER[1], jnp.where(step == 2, ORDER[2], ORDER[3])))
    else:
        ahead = ORDER[target]
    goal = (cross + ahead) & 3
    block_row = jnp.where(core == 1, goal * 4 + line, line * 4 + goal)

    @pl.when(pl.program_id(0) == 0)
    def _():
        copies = [
            pltpu.make_async_copy(panels[s], dens.at[pl.ds(s * size, size)], sems.at[s]) for s in range(pieces)
        ]
        for copy in copies:
            copy.start()
        for copy in copies:
            copy.wait()

    low = (lax.broadcasted_iota(jnp.int32, (32, 128), 1) < 64).astype(jnp.float32).astype(jnp.bfloat16)
    high = 1 - low

    def twice(blk):
        turned = jnp.concatenate([blk[:, B:], blk[:, :B]], axis=1)
        return jnp.concatenate([blk * low, turned * low, turned * high, blk * high], axis=0)

    def product(m, r, s, a):
        k = ints[(s * 8 + m) * 8 + (block_row >> 3), (block_row & 7) * 16 + r * 4 + a]
        slot = (120 >> (2 * (((k >> 4) - x) & 3))) & 3
        k = slot * 16 + ((k & 15) ^ (8 * core))
        part = s * 8 + (k >> 3)
        left = dens[pl.ds(pl.multiple_of(part * PART + (k & 7) * 128, 16), 128), :]
        right = twice(kohn[2 * s + m][0, 0, r, a * 32:(a + 1) * 32, :])
        r = lax.dot_general(left, right, (((1,), (1,)), ((), ())), preferred_element_type=jnp.float32)
        return part, (k & 7) * SP, r

    def add(sums, part, first, r):
        js = [ints[part * 8 + 2, first + b] for b in range(SP)]
        old = [sums[j] for j in js]
        for b in range(SP):
            sums[js[b]] = old[b] + r[b * 16:(b + 1) * 16, :]

    def two_rows(m, pair):
        work, sums = [], []
        for q in range(2):
            r = pair * 2 + q
            work += [(q, r, s, a) for s in range(n) for a in range(SK)]
            place = acc.at[q] if coded else outs[0].at[0, m * 4 + r]
            place[...] = p_ref[0, m * 4 + r] if has_sums else jnp.zeros((NCW, 16, 128), jnp.float32)
            sums.append(place)
        held = [product(m, *work[i][1:]) for i in range(3)]
        for i in range(len(work)):
            if i + 3 < len(work):
                held.append(product(m, *work[i + 3][1:]))
            add(sums[work[i][0]], *held[i])
        if coded:
            for q in range(2):
                r = pair * 2 + q
                out, row = (outs[m], r) if len(outs) == 2 else (outs[0], m * 4 + r)

                def put(j, value, out=out, row=row):
                    out[row, j] = value

                encode(sums[q], put, lambda code, put=put: put(NCW, code.astype(jnp.int16)))

    for m in range(2):
        lax.fori_loop(0, 2, lambda pair, _, m=m: (two_rows(m, pair), 0)[1], 0)


def panel_sums(name, ints, at, kohn, panels, sums, target=None, coded=False):
    n, pieces = len(kohn) // 2, len(panels)
    base = 0 if target is None else target
    k_specs = [
        pl.BlockSpec((1, 1, 4, 128, 128), lambda o, *_, m=m: (m, o + base, 0, 0, 0)) for _, m in kohn
    ]
    s_shape = (1, 8, NCW, 16, 128)
    s_spec = pl.BlockSpec(s_shape, lambda o, *_: (o + base, 0, 0, 0, 0))
    o_specs = [pl.BlockSpec(s_shape, lambda o, *_: (o, 0, 0, 0, 0))]
    shapes = [jax.ShapeDtypeStruct((4 if target is None else 1,) + s_shape[1:], jnp.float32)]
    if coded:
        parts = 2 if target == 0 else 1
        o_specs = [pl.BlockSpec((8 // parts, NCW + 1, 16, 128), lambda o, *_: (0, 0, 0, 0))] * parts
        shapes = [jax.ShapeDtypeStruct((8 // parts, NCW + 1, 16, 128), jnp.int16)] * parts
    any_spec = pl.BlockSpec(memory_space=pl.ANY)
    steps = 4 if target is None else 1
    return pl.pallas_call(
        lambda *refs: panel_kernel(n, pieces, target, sums is not None, coded, *refs),
        grid_spec=pltpu.PrefetchScalarGridSpec(
            num_scalar_prefetch=2,
            grid=(steps,),
            in_specs=k_specs + [any_spec] * pieces + [s_spec] * (sums is not None),
            out_specs=o_specs,
            scratch_shapes=[
                pltpu.VMEM((n * 8 * PART, 128), jnp.bfloat16),
                pltpu.SemaphoreType.DMA((pieces,)),
                pltpu.VMEM((2, NCW, 16, 128), jnp.float32),
            ],
        ),
        out_shape=shapes,
        compiler_params=pltpu.CompilerParams(vmem_limit_bytes=44 << 20),
        cost_estimate=pl.CostEstimate(
            flops=2 * n * 32 * steps * 128 * 128 * 128, bytes_accessed=(2 * n + 5 * steps) << 20, transcendentals=0
        ),
        name=name,
    )(ints, at, *[array for array, _ in kohn], *panels, *(() if sums is None else (sums,)))


def pack_kernel(slots, own, after, before, far0, far1, o_ref, total, codes):
    rows = lax.broadcasted_iota(jnp.int32, (16, 128), 0)
    lane = lax.broadcasted_iota(jnp.int32, (16, 128), 1)

    def clear(n, _):
        for m in range(4):
            o_ref[n * 4 + m] = jnp.zeros((MSG, 128), jnp.int16)
            codes[n * 4 + m] = jnp.zeros((16, 128), jnp.int32)
        return 0

    lax.fori_loop(0, 32, clear, 0)

    def one(m, r):
        row = m * 4 + r
        coded = [(before, row), (after, row), ((far0, far1)[m], r)]
        scales = [decoded_scale(ref[at, NCW]) for ref, at in coded]
        for group in range(NCW // 8):
            blocks = []
            for j in range(group * 8, group * 8 + 8):
                g = [ref[at, j].astype(jnp.int32).astype(jnp.float32) * scale for (ref, at), scale in zip(coded, scales)]
                blocks.append((own[0, row, j] + g[0]) + (g[1] + g[2]))
            turned = jnp.concatenate(blocks, axis=0).T
            v = []
            for q in range(8):
                par, mh, zh = q // 4, (q // 2) % 2, q % 2
                at = (zh * 4 + par * 2 + mh) * 16
                v.append(turned[at:at + 16, :])
            for bit in (4, 2, 1):
                keep = (lane & (16 * bit)) == 0
                w = [None] * 8
                for i in range(8):
                    if not i & bit:
                        lo, hi = v[i], v[i | bit]
                        w[i] = jnp.where(keep, lo, pltpu.roll(hi, 16 * bit, 1))
                        w[i | bit] = jnp.where(keep, pltpu.roll(lo, 128 - 16 * bit, 1), hi)
                v = w
            for j in range(8):
                total[group * 8 + j] = v[j]

        def put(j, value):
            slot = slots[row * NCW + j]
            o_ref[slot // 4, pl.ds(pl.multiple_of((slot % 4) * 16, 16), 16), :] = value

        def write_code(code):
            for j in range(NCW):
                slot = slots[row * NCW + j]
                codes[slot // 4] = jnp.where(rows == slot % 4, code, codes[slot // 4])

        encode(total, put, write_code)

    for m in range(2):
        lax.fori_loop(0, 4, lambda r, _, m=m: (one(m, r), 0)[1], 0)

    def finish(n, _):
        for m in range(4):
            o_ref[n * 4 + m, 64:80, :] = codes[n * 4 + m].astype(jnp.int16)
        return 0

    lax.fori_loop(0, 32, finish, 0)


def pack(slots, own, after, before, far0, far1):
    def whole(array):
        return pl.BlockSpec(
            array.shape, lambda i, *_, n=array.ndim: (0,) * n, pipeline_mode=pl.Buffered(1)
        )

    return pl.pallas_call(
        pack_kernel,
        grid_spec=pltpu.PrefetchScalarGridSpec(
            num_scalar_prefetch=1,
            grid=(1,),
            in_specs=[whole(array) for array in (own, after, before, far0, far1)],
            out_specs=pl.BlockSpec((128, MSG, 128), lambda i, *_: (0, 0, 0), pipeline_mode=pl.Buffered(1)),
            scratch_shapes=[pltpu.VMEM((NCW, 16, 128), jnp.float32), pltpu.VMEM((128, 16, 128), jnp.int32)],
        ),
        out_shape=jax.ShapeDtypeStruct((128, MSG, 128), jnp.int16),
        compiler_params=pltpu.CompilerParams(vmem_limit_bytes=32 << 20),
        name="pack",
    )(slots, own, after, before, far0, far1)


def unpack_kernel(r_ref, o_ref, full):
    low32 = (lax.broadcasted_iota(jnp.int32, (16, 128), 1) & 32) == 0
    for s in range(2):
        def one(n, _):
            scales = [decoded_scale(r_ref[0, c, n, 64:80, :]) for c in range(2)]
            for t in range(2):
                h = []
                for c in range(2):
                    at = (s * 2 + t) * 16
                    q = r_ref[0, c, n, at:at + 16, :].astype(jnp.int32).astype(jnp.float32)
                    h.append(q * scales[c][s * 2 + t:s * 2 + t + 1, :])
                base = pl.multiple_of(((s * 16 + n) * 2 + t) * 32, 32)
                full[pl.ds(base, 16), :] = jnp.where(low32, h[0], pltpu.roll(h[1], 32, 1))
                full[pl.ds(base + 16, 16), :] = jnp.where(low32, pltpu.roll(h[0], 96, 1), h[1])
            return 0

        lax.fori_loop(0, 16, one, 0, unroll=4)
    for p in range(32):
        o_ref[:, p * 128:(p + 1) * 128] = full[pl.ds(p, 64, stride=32), :]


def unpack(received):
    return pl.pallas_call(
        unpack_kernel,
        grid=(X,),
        in_specs=[pl.BlockSpec((1, C, 16, MSG, 128), lambda x: (x, 0, 0, 0, 0))],
        out_specs=pl.BlockSpec((64, 4096), lambda x: (x, 0)),
        out_shape=jax.ShapeDtypeStruct((256, 4096), jnp.float32),
        scratch_shapes=[pltpu.VMEM((64 * 32, 128), jnp.float32)],
        compiler_params=pltpu.CompilerParams(vmem_limit_bytes=32 << 20),
        name="unpack",
    )(received)


def local(kohn_blocks, kohn_columns, density_blocks, density_columns, owner_map):
    x, c = lax.axis_index("x"), lax.axis_index("core")
    z, y = lax.axis_index("z"), lax.axis_index("y")
    on_line, on_cross = jnp.where(c == 0, z, y), jnp.where(c == 0, y, z)
    at = jnp.stack([c, on_line, on_cross, x])

    kohn = kohn_blocks.reshape(16, 4, SK * 32, 128)
    kohn_other = over_core(kohn)

    ints = jnp.concatenate([
        kohn_columns.reshape(2, 128), jnp.pad(density_columns.reshape(1, 64), ((0, 0), (0, 64))),
        owner_map.reshape(1, 128), jnp.zeros((12, 128), jnp.int32),
    ])
    dens, kohn = lax.optimization_barrier((density_blocks[0], kohn))

    mine, theirs = split(at, dens, ints)
    shard = jnp.concatenate([mine, over_core(theirs)])
    left, right = over_x(shard, 1), over_x(shard, -1)

    kohn, after, before, opposite0, opposite1 = regroup(at, kohn, kohn_other)
    left, right, _ = lax.optimization_barrier((left, right, opposite0))
    kohn_before, kohn_after = over_line(after, 1), over_line(before, -1)
    opposite0, opposite1 = over_line(opposite0, 1), over_line(opposite1, -1)

    panel = jnp.concatenate([shard, left, right, over_x(left[:PART], 1), over_x(right[PART:], -1)])
    sent, kohn_before, kohn_after = lax.optimization_barrier((panel, kohn_before, kohn_after))
    prev, after = over_line(sent, 1), over_line(sent, -1)
    opposite0, opposite1 = over_line(opposite0, 1), over_line(opposite1, -1)
    far_low, far_high = over_line(prev[:4 * PART], 1), over_line(after[4 * PART:], -1)

    def words(*arrays):
        parts = jnp.concatenate([array.reshape(-1, PART, 128)[:, 8 * 128:8 * 128 + 8] for array in arrays])
        return parts.astype(jnp.int32).reshape(-1, 128)

    owners = jnp.stack([owner_map.reshape(128), shard[PART + 8 * 128 + 3].astype(jnp.int32)])
    hit = (owners[..., None] == jnp.arange(128, dtype=jnp.int32)).astype(jnp.int32)
    ranks = jnp.sum(jnp.cumsum(hit, axis=1) * hit, axis=2) - 1
    source = jnp.arange(2, dtype=jnp.int32)[:, None] ^ c
    slots = (owners * 4 + source * 2 + ranks).reshape(-1)

    def both(array):
        return [(array, 0), (array, 1)]

    sums, = panel_sums("own_panel", words(panel), at, both(kohn), [panel], None)
    sums, = panel_sums(
        "near_panels", words(prev, after), at, both(kohn_before) + both(kohn_after), [prev, after], sums
    )
    opposite = [(opposite0[None], 0), (opposite1[None], 0)]
    far_words = words(far_low, far_high)

    def last(target, coded):
        return panel_sums(
            "last_panel", far_words, at, opposite, [far_low, far_high], sums, target=target, coded=coded
        )

    sums0, sums1 = last(0, True)
    sums0, sums1 = over_cross(sums0, 1), over_cross(sums1, -1)
    to_next, = last(1, True)
    from_prev = over_cross(to_next, 1)
    to_prev, = last(2, True)
    from_next = over_cross(to_prev, -1)
    sums0, sums1 = over_cross(sums0, 1), over_cross(sums1, -1)
    own, = last(3, False)

    outgoing = pack(slots, own, from_next, from_prev, sums0, sums1)
    received = lax.all_to_all(outgoing, ALL, split_axis=0, concat_axis=0, tiled=True)
    return unpack(received.reshape(X, C, 16, MSG, 128))


def solution(mesh):
    grid = Mesh(mesh.devices.reshape(X, C, Z, Y), ALL)
    row, col = ("x", "core"), ("z", "y")
    return jax.shard_map(
        local,
        mesh=grid,
        in_specs=(
            P(row, col, None, None),
            P(row, col, None),
            P(col, row, None, None),
            P(col, row, None),
            P(ALL, None),
        ),
        out_specs=P(ALL, None),
        check_vma=False,
    )
```

```python
import jax
import jax.numpy as jnp
from jax import lax
from jax.experimental import pallas as pl
from jax.experimental.pallas import tpu as pltpu
from jax.sharding import Mesh, PartitionSpec as P

B = 64
HALF = 32
NCW = 32
SK = 4
SP = 8
X, C, Z, Y = 4, 2, 4, 4
ALL = ("x", "core", "z", "y")
PLANE = ("core", "z", "y")
TOP = 32766.0
MSG = 80
PART = 8 * 128 + 16
ORDER = (2, 1, 3, 0)


def lines(along):
    groups = []
    for c in range(C):
        for fixed in range(4):
            on_z = (c ^ along) == 0
            groups.append([(c * Z + (i if on_z else fixed)) * Y + (fixed if on_z else i) for i in range(4)])
    return groups


LINE, CROSS = lines(0), lines(1)


def over(groups, v, step):
    return lax.ppermute(v, PLANE, [(group[i], group[(i + step) % 4]) for group in groups for i in range(4)])


def over_line(v, step):
    return over(LINE, v, step)


def over_cross(v, step):
    return over(CROSS, v, step)


def over_x(v, step):
    return lax.ppermute(v, "x", [(i, (i + step) % X) for i in range(X)])


def over_core(v):
    return lax.ppermute(v, "core", [(0, 1), (1, 0)])


def split_kernel(core, d_ref, i_ref, mine, theirs, flat, wide):
    lane32 = lax.broadcasted_iota(jnp.int32, (32, 128), 1)
    lane64 = lax.broadcasted_iota(jnp.int32, (64, 128), 1)

    def one(k, _):
        rows = d_ref[k].astype(jnp.float32)
        for p in range(32):
            flat[p * 8:(p + 1) * 8, :] = rows[:, p * 128:(p + 1) * 128]
        v = []
        for b in range(4):
            lo, hi = flat[pl.ds(b, 32, stride=8), :], flat[pl.ds(b + 4, 32, stride=8), :]
            wide[b, pl.ds(0, 32, stride=2), :] = jnp.where(lane32 < 64, lo, pltpu.roll(hi, 64, 1))
            wide[b, pl.ds(1, 32, stride=2), :] = jnp.where(lane32 < 64, pltpu.roll(lo, 64, 1), hi)
        v = [wide[b] for b in range(4)]
        for bit in (2, 1):
            keep = (lane64 & (16 * bit)) == 0
            w = [None] * 4
            for i in range(4):
                if not i & bit:
                    lo, hi = v[i], v[i | bit]
                    w[i] = jnp.where(keep, lo, pltpu.roll(hi, 16 * bit, 1))
                    w[i | bit] = jnp.where(keep, pltpu.roll(lo, 128 - 16 * bit, 1), hi)
            v = w
        first = jnp.concatenate([v[0], v[1]], axis=0).T
        second = jnp.concatenate([v[2], v[3]], axis=0).T
        swapped = core[0] == 1
        at = pl.ds(pl.multiple_of(k * 128, 128), 128)
        mine[at, :] = jnp.where(swapped, second, first).astype(jnp.bfloat16)
        theirs[at, :] = jnp.where(swapped, first, second).astype(jnp.bfloat16)
        return 0

    lax.fori_loop(0, 8, one, 0)
    ints = i_ref[...].astype(jnp.float32).astype(jnp.bfloat16)
    mine[8 * 128:, :] = ints
    theirs[8 * 128:, :] = ints


def split(core, dens, ints):
    half = jax.ShapeDtypeStruct((PART, 128), jnp.bfloat16)
    whole = pl.BlockSpec((PART, 128), lambda i, *_: (0, 0))
    return pl.pallas_call(
        split_kernel,
        grid_spec=pltpu.PrefetchScalarGridSpec(
            num_scalar_prefetch=1, grid=(1,),
            in_specs=[
                pl.BlockSpec((8, SP, B * B), lambda i, *_: (0, 0, 0)), pl.BlockSpec((16, 128), lambda i, *_: (0, 0))
            ],
            out_specs=[whole, whole],
            scratch_shapes=[pltpu.VMEM((256, 128), jnp.float32), pltpu.VMEM((4, B, 128), jnp.float32)],
        ),
        out_shape=[half, half],
        name="split",
    )(core, dens, ints)


def regroup_kernel(at, mine, other, own, ahead, back, sems):
    swapped, line, cross = at[0] == 1, at[1], at[2]
    copies = []
    for step in range(4):
        t = (line + step) % 4
        for i, rel in enumerate(ORDER):
            o = (cross + rel) % 4
            row = jnp.where(swapped, o * 4 + t, t * 4 + o)
            for m, src in enumerate((mine, other)):
                dst = (own.at[m, i], ahead.at[m, i], (ahead, back)[m].at[2, i], back.at[m, i])[step]
                copies.append(pltpu.make_async_copy(src.at[row], dst, sems.at[len(copies)]))
    for copy in copies:
        copy.start()
    for copy in copies:
        copy.wait()


def regroup(at, mine, other):
    shapes = [(2, 4, 4, 128, 128), (3, 4, 4, 128, 128), (3, 4, 4, 128, 128)]
    return pl.pallas_call(
        regroup_kernel,
        grid_spec=pltpu.PrefetchScalarGridSpec(
            num_scalar_prefetch=1, grid=(1,), in_specs=[pl.BlockSpec(memory_space=pl.ANY)] * 2,
            out_specs=[pl.BlockSpec(shape, lambda i, *_, n=len(shape): (0,) * n) for shape in shapes],
            scratch_shapes=[pltpu.SemaphoreType.DMA((32,))],
        ),
        out_shape=[jax.ShapeDtypeStruct(shape, jnp.bfloat16) for shape in shapes],
        compiler_params=pltpu.CompilerParams(vmem_limit_bytes=24 << 20),
        name="regroup",
    )(at, mine, other)


def encode(values, put, write_code):
    top = jnp.zeros((16, 128), jnp.float32)
    for j in range(NCW):
        top = jnp.maximum(top, jnp.abs(values[j]))
    top = jnp.maximum(jnp.max(top, axis=0, keepdims=True), 2.0 ** -110)
    code = jnp.floor(jnp.log2(top) * 256.0) + 1.0
    scale = jnp.broadcast_to(jnp.exp2(code * (-1.0 / 256.0)) * TOP, (16, 128))
    write_code(jnp.broadcast_to(code.astype(jnp.int32), (16, 128)))
    for j in range(NCW):
        put(j, jnp.floor(values[j] * scale + 0.5).astype(jnp.int32).astype(jnp.int16))


def decoded_scale(code):
    return jnp.exp2(code.astype(jnp.int32).astype(jnp.float32) * (1.0 / 256.0)) * (1.0 / TOP)


def panel_kernel(n, pieces, halves, form, at, *refs):
    kohn, refs = refs[:2 * n], refs[2 * n:]
    panels, refs = refs[:pieces], refs[pieces:]
    if form != "first":
        sums_in, refs = refs[:2], refs[2:]
    if form == "sent":
        received, refs = refs[:2], refs[2:]
    outs, (dens, sems, acc, staged, ints) = refs[:-5], refs[-5:]
    size = n * 8 * PART // pieces
    core, line, cross, x = at[0], at[1], at[2], at[3]

    @pl.when(pl.program_id(0) == 0)
    def _():
        copies = [
            pltpu.make_async_copy(panels[s], dens.at[pl.ds(s * size, size)], sems.at[s]) for s in range(pieces)
        ]
        for copy in copies:
            copy.start()
        for copy in copies:
            copy.wait()
        for s in range(n):
            rows = [dens[pl.ds((s * 8 + p) * PART + 8 * 128, 16), :].astype(jnp.float32) for p in range(8)]
            rows = [row[2:3] for row in rows] + [rows[0][0:2], rows[1][0:2], jnp.zeros((4, 128), jnp.float32)]
            staged[s * 16:(s + 1) * 16, :] = jnp.concatenate(rows, axis=0).astype(jnp.int32)
        copy = pltpu.make_async_copy(staged, ints, sems.at[pieces])
        copy.start()
        copy.wait()

    def place_of(target):
        if target is None:
            step = pl.program_id(0)
            ahead = jnp.where(step < 2, ORDER[0] - step, ORDER[2] * (3 - step))
        else:
            ahead = ORDER[target]
        goal = (cross + ahead) & 3
        return jnp.where(core == 1, goal * 4 + line, line * 4 + goal)

    low = (lax.broadcasted_iota(jnp.int32, (32, 128), 1) < 64).astype(jnp.float32).astype(jnp.bfloat16)
    high = 1 - low

    def twice(blk):
        turned = jnp.concatenate([blk[:, B:], blk[:, :B]], axis=1)
        return jnp.concatenate([blk * low, turned * low, turned * high, blk * high], axis=0)

    def product(h, place, r, s, a):
        k = ints[s * 16 + 8 + halves[h][1] * 2 + (place >> 3), (place & 7) * 16 + r * 4 + a]
        slot = (120 >> (2 * (((k >> 4) - x) & 3))) & 3
        k = slot * 16 + ((k & 15) ^ (8 * core))
        part = s * 8 + (k >> 3)
        left = dens[pl.ds(pl.multiple_of(part * PART + (k & 7) * 128, 16), 128), :]
        right = twice(kohn[2 * s + h][0, 0, r, a * 32:(a + 1) * 32, :])
        r = lax.dot_general(left, right, (((1,), (1,)), ((), ())), preferred_element_type=jnp.float32)
        return s * 16 + (k >> 3), (k & 7) * SP, r

    def add(sums, word, first, r):
        js = [ints[word, first + b] for b in range(SP)]
        old = [sums[j] for j in js]
        for b in range(SP):
            sums[js[b]] = old[b] + r[b * 16:(b + 1) * 16, :]

    def two_rows(h, place, pair):
        work, sums = [], []
        for q in range(2):
            r = pair * 2 + q
            work += [(q, r, s, a) for s in range(n) for a in range(SK)]
            total = acc.at[q] if form in ("coded", "sent") else outs[0].at[0, h * 4 + r]
            if form == "first":
                total[...] = jnp.zeros((NCW, 16, 128), jnp.float32)
            elif form == "sent":
                scale = decoded_scale(received[h][r, NCW])
                for j in range(NCW):
                    total[j] = sums_in[h][0, r, j] + received[h][r, j].astype(jnp.int32).astype(jnp.float32) * scale
            else:
                total[...] = sums_in[h][0, r]
            sums.append(total)
        held = [product(h, place, *work[i][1:]) for i in range(3)]
        for i in range(len(work)):
            if i + 3 < len(work):
                held.append(product(h, place, *work[i + 3][1:]))
            add(sums[work[i][0]], *held[i])
        if form in ("coded", "sent"):
            for q in range(2):
                r = pair * 2 + q

                def put(j, value, r=r):
                    outs[h][r, j] = value

                encode(sums[q], put, lambda code, put=put: put(NCW, code.astype(jnp.int16)))

    for h in range(2):
        place = place_of(halves[h][0])
        lax.fori_loop(0, 2, lambda pair, _, h=h, place=place: (two_rows(h, place, pair), 0)[1], 0)


def panel_sums(name, form, at, kohn, panels, halves, sums=None, received=(), us=4.0):
    n, pieces = len(kohn) // 2, len(panels)
    steps = 4 if halves[0][0] is None else 1

    def at_target(h, lead):
        target = halves[h][0]
        return lambda o, *_: (lead, o if target is None else target, 0, 0, 0)

    k_specs = [pl.BlockSpec((1, 1, 4, 128, 128), at_target(i % 2, place)) for i, (_, place) in enumerate(kohn)]

    def s_spec(h):
        target, m = halves[h]
        return pl.BlockSpec((1, 4, NCW, 16, 128), lambda o, *_: (o if target is None else target, m, 0, 0, 0))

    coded = pl.BlockSpec((4, NCW + 1, 16, 128), lambda o, *_: (0, 0, 0, 0))
    if form in ("coded", "sent"):
        o_specs = [coded] * 2
        shapes = [jax.ShapeDtypeStruct((4, NCW + 1, 16, 128), jnp.int16)] * 2
    else:
        o_specs = [pl.BlockSpec((1, 8, NCW, 16, 128), lambda o, *_: (o, 0, 0, 0, 0))]
        shapes = [jax.ShapeDtypeStruct((steps, 8, NCW, 16, 128), jnp.float32)]
    any_spec = pl.BlockSpec(memory_space=pl.ANY)
    return pl.pallas_call(
        lambda *refs: panel_kernel(n, pieces, halves, form, *refs),
        grid_spec=pltpu.PrefetchScalarGridSpec(
            num_scalar_prefetch=1,
            grid=(steps,),
            in_specs=(
                k_specs + [any_spec] * pieces + ([] if sums is None else [s_spec(0), s_spec(1)]) + [coded] * len(received)
            ),
            out_specs=o_specs,
            scratch_shapes=[
                pltpu.VMEM((n * 8 * PART, 128), jnp.bfloat16),
                pltpu.SemaphoreType.DMA((pieces + 1,)),
                pltpu.VMEM((2, NCW, 16, 128), jnp.float32),
                pltpu.VMEM((n * 16, 128), jnp.int32),
                pltpu.SMEM((n * 16, 128), jnp.int32),
            ],
        ),
        out_shape=shapes,
        compiler_params=pltpu.CompilerParams(vmem_limit_bytes=44 << 20),
        cost_estimate=pl.CostEstimate(flops=int(us * 1.1e9), bytes_accessed=int(us * 2e6), transcendentals=0),
        name=name,
    )(at, *[array for array, _ in kohn], *panels, *([] if sums is None else [sums, sums]), *received)


def pack_kernel(slots, own, prev0, prev1, next0, next1, o_ref, total, codes):
    rows = lax.broadcasted_iota(jnp.int32, (16, 128), 0)
    lane = lax.broadcasted_iota(jnp.int32, (16, 128), 1)

    def clear(n, _):
        for m in range(4):
            o_ref[n * 4 + m] = jnp.zeros((MSG, 128), jnp.int16)
            codes[n * 4 + m] = jnp.zeros((16, 128), jnp.int32)
        return 0

    lax.fori_loop(0, 32, clear, 0)

    def one(m, r):
        row = m * 4 + r
        coded = [((prev0, prev1)[m], r), ((next0, next1)[m], r)]
        scales = [decoded_scale(ref[at, NCW]) for ref, at in coded]
        for group in range(NCW // 8):
            blocks = []
            for j in range(group * 8, group * 8 + 8):
                g = [ref[at, j].astype(jnp.int32).astype(jnp.float32) * scale for (ref, at), scale in zip(coded, scales)]
                blocks.append(own[0, row, j] + g[0] + g[1])
            turned = jnp.concatenate(blocks, axis=0).T
            v = []
            for q in range(8):
                par, mh, zh = q // 4, (q // 2) % 2, q % 2
                at = (zh * 4 + par * 2 + mh) * 16
                v.append(turned[at:at + 16, :])
            for bit in (4, 2, 1):
                keep = (lane & (16 * bit)) == 0
                w = [None] * 8
                for i in range(8):
                    if not i & bit:
                        lo, hi = v[i], v[i | bit]
                        w[i] = jnp.where(keep, lo, pltpu.roll(hi, 16 * bit, 1))
                        w[i | bit] = jnp.where(keep, pltpu.roll(lo, 128 - 16 * bit, 1), hi)
                v = w
            for j in range(8):
                total[group * 8 + j] = v[j]

        def put(j, value):
            slot = slots[row * NCW + j]
            o_ref[slot // 4, pl.ds(pl.multiple_of((slot % 4) * 16, 16), 16), :] = value

        def write_code(code):
            for j in range(NCW):
                slot = slots[row * NCW + j]
                codes[slot // 4] = jnp.where(rows == slot % 4, code, codes[slot // 4])

        encode(total, put, write_code)

    for m in range(2):
        lax.fori_loop(0, 4, lambda r, _, m=m: (one(m, r), 0)[1], 0)

    def finish(n, _):
        for m in range(4):
            o_ref[n * 4 + m, 64:80, :] = codes[n * 4 + m].astype(jnp.int16)
        return 0

    lax.fori_loop(0, 32, finish, 0)


def pack(slots, *parts):
    def whole(array):
        return pl.BlockSpec(
            array.shape, lambda i, *_, n=array.ndim: (0,) * n, pipeline_mode=pl.Buffered(1)
        )

    return pl.pallas_call(
        pack_kernel,
        grid_spec=pltpu.PrefetchScalarGridSpec(
            num_scalar_prefetch=1,
            grid=(1,),
            in_specs=[whole(array) for array in parts],
            out_specs=pl.BlockSpec((128, MSG, 128), lambda i, *_: (0, 0, 0), pipeline_mode=pl.Buffered(1)),
            scratch_shapes=[pltpu.VMEM((NCW, 16, 128), jnp.float32), pltpu.VMEM((128, 16, 128), jnp.int32)],
        ),
        out_shape=jax.ShapeDtypeStruct((128, MSG, 128), jnp.int16),
        compiler_params=pltpu.CompilerParams(vmem_limit_bytes=32 << 20),
        name="pack",
    )(slots, *parts)


def unpack_kernel(r_ref, o_ref, full):
    low32 = (lax.broadcasted_iota(jnp.int32, (16, 128), 1) & 32) == 0
    for s in range(2):
        def one(n, _):
            scales = [decoded_scale(r_ref[0, c, n, 64:80, :]) for c in range(2)]
            for t in range(2):
                h = []
                for c in range(2):
                    at = (s * 2 + t) * 16
                    q = r_ref[0, c, n, at:at + 16, :].astype(jnp.int32).astype(jnp.float32)
                    h.append(q * scales[c][s * 2 + t:s * 2 + t + 1, :])
                base = pl.multiple_of(((s * 16 + n) * 2 + t) * 32, 32)
                full[pl.ds(base, 16), :] = jnp.where(low32, h[0], pltpu.roll(h[1], 32, 1))
                full[pl.ds(base + 16, 16), :] = jnp.where(low32, pltpu.roll(h[0], 96, 1), h[1])
            return 0

        lax.fori_loop(0, 16, one, 0, unroll=4)
    for p in range(32):
        o_ref[:, p * 128:(p + 1) * 128] = full[pl.ds(p, 64, stride=32), :]


def unpack(received):
    return pl.pallas_call(
        unpack_kernel,
        grid=(X,),
        in_specs=[pl.BlockSpec((1, C, 16, MSG, 128), lambda x: (x, 0, 0, 0, 0))],
        out_specs=pl.BlockSpec((64, 4096), lambda x: (x, 0)),
        out_shape=jax.ShapeDtypeStruct((256, 4096), jnp.float32),
        scratch_shapes=[pltpu.VMEM((64 * 32, 128), jnp.float32)],
        compiler_params=pltpu.CompilerParams(vmem_limit_bytes=32 << 20),
        name="unpack",
    )(received)


def local(kohn_blocks, kohn_columns, density_blocks, density_columns, owner_map):
    x, c = lax.axis_index("x"), lax.axis_index("core")
    z, y = lax.axis_index("z"), lax.axis_index("y")
    on_line, on_cross = jnp.where(c == 0, z, y), jnp.where(c == 0, y, z)
    at = jnp.stack([c, on_line, on_cross, x])

    kohn = kohn_blocks.reshape(16, 4, SK * 32, 128)
    kohn_other = over_core(kohn)

    ints = jnp.concatenate([
        kohn_columns.reshape(2, 128), jnp.pad(density_columns.reshape(1, 64), ((0, 0), (0, 64))),
        owner_map.reshape(1, 128), jnp.zeros((12, 128), jnp.int32),
    ])
    dens, kohn = lax.optimization_barrier((density_blocks[0], kohn))

    mine, theirs = split(at, dens, ints)
    shard = jnp.concatenate([mine, over_core(theirs)])
    shard, kohn, kohn_other = lax.optimization_barrier((shard, kohn, kohn_other))
    left, right = over_x(shard, 1), over_x(shard, -1)

    kohn, ahead, back = regroup(at, kohn, kohn_other)
    kohn_prev, kohn_next = over_line(ahead, 1), over_line(back, -1)
    left, right, kohn_prev, kohn_next = lax.optimization_barrier((left, right, kohn_prev, kohn_next))
    opposite0, opposite1 = over_line(kohn_prev[2:], 1), over_line(kohn_next[2:], -1)

    panel = jnp.concatenate([shard, left, right, over_x(left[:PART], 1), over_x(right[PART:], -1)])
    sent, opposite0, opposite1 = lax.optimization_barrier((panel, opposite0, opposite1))
    prev, after = over_line(sent, 1), over_line(sent, -1)

    owners = jnp.stack([owner_map.reshape(128), shard[PART + 8 * 128 + 3].astype(jnp.int32)])
    hit = (owners[..., None] == jnp.arange(128, dtype=jnp.int32)).astype(jnp.int32)
    ranks = jnp.sum(jnp.cumsum(hit, axis=1) * hit, axis=2) - 1
    source = jnp.arange(2, dtype=jnp.int32)[:, None] ^ c
    slots = (owners * 4 + source * 2 + ranks).reshape(-1)

    def both(array):
        return [(array, 0), (array, 1)]

    everything = ((None, 0), (None, 1))
    sums, = panel_sums("own_panel", "first", at, both(kohn), [panel], everything, us=9.0)
    prev, after, sums = lax.optimization_barrier((prev, after, sums))
    far_low, far_high = over_line(prev[:4 * PART], 1), over_line(after[4 * PART:], -1)
    sums, = panel_sums(
        "near_panels", "more", at, both(kohn_prev) + both(kohn_next), [prev, after], everything, sums, us=16.0
    )

    def last(form, halves, received=()):
        kohn = [((opposite0, opposite1)[m], 0) for _, m in halves]
        return panel_sums("last_" + form, form, at, kohn, [far_low, far_high], halves, sums, received)

    via_next, via_prev = last("coded", ((0, 0), (0, 1)))
    via_next, via_prev = over_cross(via_next, 1), over_cross(via_prev, -1)
    next1, prev0 = last("coded", ((1, 1), (2, 0)))
    prev_1, next_0 = over_cross(next1, 1), over_cross(prev0, -1)
    next0, prev1 = last("sent", ((1, 0), (2, 1)), (via_next, via_prev))
    prev_0, next_1 = over_cross(next0, 1), over_cross(prev1, -1)
    own, = last("more", ((3, 0), (3, 1)))

    outgoing = pack(slots, own, prev_0, prev_1, next_0, next_1)
    received = lax.all_to_all(outgoing, ALL, split_axis=0, concat_axis=0, tiled=True)
    return unpack(received.reshape(X, C, 16, MSG, 128))


def solution(mesh):
    grid = Mesh(mesh.devices.reshape(X, C, Z, Y), ALL)
    row, col = ("x", "core"), ("z", "y")
    return jax.shard_map(
        local,
        mesh=grid,
        in_specs=(
            P(row, col, None, None),
            P(row, col, None),
            P(col, row, None, None),
            P(col, row, None),
            P(ALL, None),
        ),
        out_specs=P(ALL, None),
        check_vma=False,
    )
```

```python
import jax
import jax.numpy as jnp
from jax import lax
from jax.experimental import pallas as pl
from jax.experimental.pallas import tpu as pltpu
from jax.sharding import Mesh, PartitionSpec as P

B = 64
HALF = 32
NCW = 32
SK = 4
SP = 8
X, C, Z, Y = 4, 2, 4, 4
ALL = ("x", "core", "z", "y")
PLANE = ("core", "z", "y")
TOP = 32766.0
MSG = 80
PART = 8 * 128 + 16
ORDER = (2, 1, 3, 0)


def lines(along):
    groups = []
    for c in range(C):
        for fixed in range(4):
            on_z = (c ^ along) == 0
            groups.append([(c * Z + (i if on_z else fixed)) * Y + (fixed if on_z else i) for i in range(4)])
    return groups


LINE, CROSS = lines(0), lines(1)


def over(groups, v, step):
    return lax.ppermute(v, PLANE, [(group[i], group[(i + step) % 4]) for group in groups for i in range(4)])


def over_line(v, step):
    return over(LINE, v, step)


def over_cross(v, step):
    return over(CROSS, v, step)


def over_x(v, step):
    return lax.ppermute(v, "x", [(i, (i + step) % X) for i in range(X)])


def over_core(v):
    return lax.ppermute(v, "core", [(0, 1), (1, 0)])


def split_kernel(core, d_ref, i_ref, mine, theirs, flat, wide):
    lane32 = lax.broadcasted_iota(jnp.int32, (32, 128), 1)
    lane64 = lax.broadcasted_iota(jnp.int32, (64, 128), 1)

    def one(k, _):
        rows = d_ref[k].astype(jnp.float32)
        for p in range(32):
            flat[p * 8:(p + 1) * 8, :] = rows[:, p * 128:(p + 1) * 128]
        v = []
        for b in range(4):
            lo, hi = flat[pl.ds(b, 32, stride=8), :], flat[pl.ds(b + 4, 32, stride=8), :]
            wide[b, pl.ds(0, 32, stride=2), :] = jnp.where(lane32 < 64, lo, pltpu.roll(hi, 64, 1))
            wide[b, pl.ds(1, 32, stride=2), :] = jnp.where(lane32 < 64, pltpu.roll(lo, 64, 1), hi)
        v = [wide[b] for b in range(4)]
        for bit in (2, 1):
            keep = (lane64 & (16 * bit)) == 0
            w = [None] * 4
            for i in range(4):
                if not i & bit:
                    lo, hi = v[i], v[i | bit]
                    w[i] = jnp.where(keep, lo, pltpu.roll(hi, 16 * bit, 1))
                    w[i | bit] = jnp.where(keep, pltpu.roll(lo, 128 - 16 * bit, 1), hi)
            v = w
        first = jnp.concatenate([v[0], v[1]], axis=0).T
        second = jnp.concatenate([v[2], v[3]], axis=0).T
        swapped = core[0] == 1
        at = pl.ds(pl.multiple_of(k * 128, 128), 128)
        mine[at, :] = jnp.where(swapped, second, first).astype(jnp.bfloat16)
        theirs[at, :] = jnp.where(swapped, first, second).astype(jnp.bfloat16)
        return 0

    lax.fori_loop(0, 8, one, 0)
    ints = i_ref[...].astype(jnp.float32).astype(jnp.bfloat16)
    mine[8 * 128:, :] = ints
    theirs[8 * 128:, :] = ints


def split(core, dens, ints):
    half = jax.ShapeDtypeStruct((PART, 128), jnp.bfloat16)
    whole = pl.BlockSpec((PART, 128), lambda i, *_: (0, 0))
    return pl.pallas_call(
        split_kernel,
        grid_spec=pltpu.PrefetchScalarGridSpec(
            num_scalar_prefetch=1, grid=(1,),
            in_specs=[
                pl.BlockSpec((8, SP, B * B), lambda i, *_: (0, 0, 0)), pl.BlockSpec((16, 128), lambda i, *_: (0, 0))
            ],
            out_specs=[whole, whole],
            scratch_shapes=[pltpu.VMEM((256, 128), jnp.float32), pltpu.VMEM((4, B, 128), jnp.float32)],
        ),
        out_shape=[half, half],
        name="split",
    )(core, dens, ints)


def regroup_kernel(at, mine, other, own, ahead, back, sems):
    swapped, line, cross = at[0] == 1, at[1], at[2]
    copies = []
    for step in range(4):
        t = (line + step) % 4
        for i, rel in enumerate(ORDER):
            o = (cross + rel) % 4
            row = jnp.where(swapped, o * 4 + t, t * 4 + o)
            for m, src in enumerate((mine, other)):
                dst = (own.at[m, i], ahead.at[m, i], (ahead, back)[m].at[2, i], back.at[m, i])[step]
                copies.append(pltpu.make_async_copy(src.at[row], dst, sems.at[len(copies)]))
    for copy in copies:
        copy.start()
    for copy in copies:
        copy.wait()


def regroup(at, mine, other):
    shapes = [(2, 4, 4, 128, 128), (3, 4, 4, 128, 128), (3, 4, 4, 128, 128)]
    return pl.pallas_call(
        regroup_kernel,
        grid_spec=pltpu.PrefetchScalarGridSpec(
            num_scalar_prefetch=1, grid=(1,), in_specs=[pl.BlockSpec(memory_space=pl.ANY)] * 2,
            out_specs=[pl.BlockSpec(shape, lambda i, *_, n=len(shape): (0,) * n) for shape in shapes],
            scratch_shapes=[pltpu.SemaphoreType.DMA((32,))],
        ),
        out_shape=[jax.ShapeDtypeStruct(shape, jnp.bfloat16) for shape in shapes],
        compiler_params=pltpu.CompilerParams(vmem_limit_bytes=24 << 20),
        name="regroup",
    )(at, mine, other)


def encode(values, put, write_code):
    top = jnp.zeros((16, 128), jnp.float32)
    for j in range(NCW):
        top = jnp.maximum(top, jnp.abs(values[j]))
    top = jnp.maximum(jnp.max(top, axis=0, keepdims=True), 2.0 ** -110)
    code = jnp.floor(jnp.log2(top) * 256.0) + 1.0
    scale = jnp.broadcast_to(jnp.exp2(code * (-1.0 / 256.0)) * TOP, (16, 128))
    write_code(jnp.broadcast_to(code.astype(jnp.int32), (16, 128)))
    for j in range(NCW):
        put(j, jnp.floor(values[j] * scale + 0.5).astype(jnp.int32).astype(jnp.int16))


def decoded_scale(code):
    return jnp.exp2(code.astype(jnp.int32).astype(jnp.float32) * (1.0 / 256.0)) * (1.0 / TOP)


def panel_kernel(n, pieces, halves, form, kcol, jcol, *refs):
    whole = halves[0][0] is None
    kohn, refs = refs[:2 * n], refs[2 * n:]
    panels, refs = refs[:pieces], refs[pieces:]
    if form != "first":
        sums_in, refs = refs[0], refs[1:]
    if form == "sent":
        received, refs = refs[:2], refs[2:]
    outs, (dens, sems, acc) = refs[:-3], refs[-3:]
    size = n * 8 * PART // pieces

    @pl.when(pl.program_id(0) == 0)
    def _():
        copies = [
            pltpu.make_async_copy(panels[s], dens.at[pl.ds(s * size, size)], sems.at[s]) for s in range(pieces)
        ]
        if not whole:
            for h, (target, m) in enumerate(halves):
                into = outs[0].at[0] if form == "own" else acc
                copies.append(pltpu.make_async_copy(
                    sums_in.at[target, pl.ds(m * 4, 4)], into.at[pl.ds(h * 4, 4)], sems.at[pieces + h]
                ))
        for copy in copies:
            copy.start()
        for copy in copies:
            copy.wait()

    low = (lax.broadcasted_iota(jnp.int32, (32, 128), 1) < 64).astype(jnp.float32).astype(jnp.bfloat16)
    high = 1 - low

    def twice(blk):
        turned = jnp.concatenate([blk[:, B:], blk[:, :B]], axis=1)
        return jnp.concatenate([blk * low, turned * low, turned * high, blk * high], axis=0)

    def product(h, r, s, a):
        target, m = halves[h]
        step = pl.program_id(0) if whole else target
        k = kcol[(((s * 4 + step) * 2 + m) * 4 + r) * SK + a]
        at = s * 8 * PART + k * 128 + (k >> 3) * 16
        left = dens[pl.ds(pl.multiple_of(at, 16), 128), :]
        right = twice(kohn[2 * s + h][0, 0, r, a * 32:(a + 1) * 32, :])
        r = lax.dot_general(left, right, (((1,), (1,)), ((), ())), preferred_element_type=jnp.float32)
        return s * 512 + k * SP, r

    def add(sums, first, r):
        js = [jcol[first + b] for b in range(SP)]
        old = [sums[j] for j in js]
        for b in range(SP):
            sums[js[b]] = old[b] + r[b * 16:(b + 1) * 16, :]

    def two_rows(h, pair):
        work, sums = [], []
        for q in range(2):
            r = pair * 2 + q
            work += [(q, r, s, a) for s in range(n) for a in range(SK)]
            total = acc.at[h * 4 + r] if form in ("coded", "sent") else outs[0].at[0, h * 4 + r]
            if form == "first":
                total[...] = jnp.zeros((NCW, 16, 128), jnp.float32)
            elif form == "more":
                total[...] = sums_in[0, h * 4 + r]
            elif form == "sent":
                scale = decoded_scale(received[h][r, NCW])
                for j in range(NCW):
                    total[j] = total[j] + received[h][r, j].astype(jnp.int32).astype(jnp.float32) * scale
            sums.append(total)
        held = [product(h, *work[i][1:]) for i in range(3)]
        for i in range(len(work)):
            if i + 3 < len(work):
                held.append(product(h, *work[i + 3][1:]))
            add(sums[work[i][0]], *held[i])
        if form in ("coded", "sent"):
            for q in range(2):
                r = pair * 2 + q

                def put(j, value, r=r):
                    outs[h][r, j] = value

                encode(sums[q], put, lambda code, put=put: put(NCW, code.astype(jnp.int16)))

    for h in range(2):
        lax.fori_loop(0, 2, lambda pair, _, h=h: (two_rows(h, pair), 0)[1], 0)


def panel_sums(name, form, kcol, jcol, kohn, panels, halves, sums=None, received=(), us=3.0):
    n, pieces = len(kohn) // 2, len(panels)
    whole = halves[0][0] is None
    steps = 4 if whole else 1

    def at_target(h, lead):
        target = halves[h][0]
        return lambda o, *_: (lead, o if target is None else target, 0, 0, 0)

    k_specs = [pl.BlockSpec((1, 1, 4, 128, 128), at_target(i % 2, place)) for i, (_, place) in enumerate(kohn)]
    any_spec = pl.BlockSpec(memory_space=pl.ANY)
    s_spec = pl.BlockSpec((1, 8, NCW, 16, 128), lambda o, *_: (o, 0, 0, 0, 0))
    coded = pl.BlockSpec((4, NCW + 1, 16, 128), lambda o, *_: (0, 0, 0, 0))
    if form in ("coded", "sent"):
        o_specs = [coded] * 2
        shapes = [jax.ShapeDtypeStruct((4, NCW + 1, 16, 128), jnp.int16)] * 2
    else:
        o_specs = [s_spec]
        shapes = [jax.ShapeDtypeStruct((steps, 8, NCW, 16, 128), jnp.float32)]
    return pl.pallas_call(
        lambda *refs: panel_kernel(n, pieces, halves, form, *refs),
        grid_spec=pltpu.PrefetchScalarGridSpec(
            num_scalar_prefetch=2,
            grid=(steps,),
            in_specs=(
                k_specs + [any_spec] * pieces + ([] if sums is None else [s_spec if whole else any_spec])
                + [coded] * len(received)
            ),
            out_specs=o_specs,
            scratch_shapes=[
                pltpu.VMEM((n * 8 * PART, 128), jnp.bfloat16),
                pltpu.SemaphoreType.DMA((pieces + 2,)),
                pltpu.VMEM((8 if form in ("coded", "sent") else 1, NCW, 16, 128), jnp.float32),
            ],
        ),
        out_shape=shapes,
        compiler_params=pltpu.CompilerParams(vmem_limit_bytes=44 << 20),
        cost_estimate=pl.CostEstimate(flops=int(us * 1.1e9), bytes_accessed=int(us * 2e6), transcendentals=0),
        name=name,
    )(kcol, jcol, *[array for array, _ in kohn], *panels, *([] if sums is None else [sums]), *received)


def pack_kernel(slots, own, prev0, prev1, next0, next1, o_ref, total, codes):
    rows = lax.broadcasted_iota(jnp.int32, (16, 128), 0)
    lane = lax.broadcasted_iota(jnp.int32, (16, 128), 1)

    def clear(n, _):
        for m in range(4):
            o_ref[n * 4 + m] = jnp.zeros((MSG, 128), jnp.int16)
            codes[n * 4 + m] = jnp.zeros((16, 128), jnp.int32)
        return 0

    lax.fori_loop(0, 32, clear, 0)

    def one(m, r):
        row = m * 4 + r
        coded = [((prev0, prev1)[m], r), ((next0, next1)[m], r)]
        scales = [decoded_scale(ref[at, NCW]) for ref, at in coded]
        for group in range(NCW // 8):
            blocks = []
            for j in range(group * 8, group * 8 + 8):
                g = [ref[at, j].astype(jnp.int32).astype(jnp.float32) * scale for (ref, at), scale in zip(coded, scales)]
                blocks.append(own[0, row, j] + g[0] + g[1])
            turned = jnp.concatenate(blocks, axis=0).T
            v = []
            for q in range(8):
                par, mh, zh = q // 4, (q // 2) % 2, q % 2
                at = (zh * 4 + par * 2 + mh) * 16
                v.append(turned[at:at + 16, :])
            for bit in (4, 2, 1):
                keep = (lane & (16 * bit)) == 0
                w = [None] * 8
                for i in range(8):
                    if not i & bit:
                        lo, hi = v[i], v[i | bit]
                        w[i] = jnp.where(keep, lo, pltpu.roll(hi, 16 * bit, 1))
                        w[i | bit] = jnp.where(keep, pltpu.roll(lo, 128 - 16 * bit, 1), hi)
                v = w
            for j in range(8):
                total[group * 8 + j] = v[j]

        def put(j, value):
            slot = slots[row * NCW + j]
            o_ref[slot // 4, pl.ds(pl.multiple_of((slot % 4) * 16, 16), 16), :] = value

        def write_code(code):
            for j in range(NCW):
                slot = slots[row * NCW + j]
                codes[slot // 4] = jnp.where(rows == slot % 4, code, codes[slot // 4])

        encode(total, put, write_code)

    for m in range(2):
        lax.fori_loop(0, 4, lambda r, _, m=m: (one(m, r), 0)[1], 0)

    def finish(n, _):
        for m in range(4):
            o_ref[n * 4 + m, 64:80, :] = codes[n * 4 + m].astype(jnp.int16)
        return 0

    lax.fori_loop(0, 32, finish, 0)


def pack(slots, *parts):
    def whole(array):
        return pl.BlockSpec(
            array.shape, lambda i, *_, n=array.ndim: (0,) * n, pipeline_mode=pl.Buffered(1)
        )

    return pl.pallas_call(
        pack_kernel,
        grid_spec=pltpu.PrefetchScalarGridSpec(
            num_scalar_prefetch=1,
            grid=(1,),
            in_specs=[whole(array) for array in parts],
            out_specs=pl.BlockSpec((128, MSG, 128), lambda i, *_: (0, 0, 0), pipeline_mode=pl.Buffered(1)),
            scratch_shapes=[pltpu.VMEM((NCW, 16, 128), jnp.float32), pltpu.VMEM((128, 16, 128), jnp.int32)],
        ),
        out_shape=jax.ShapeDtypeStruct((128, MSG, 128), jnp.int16),
        compiler_params=pltpu.CompilerParams(vmem_limit_bytes=32 << 20),
        name="pack",
    )(slots, *parts)


def unpack_kernel(r_ref, o_ref, full):
    low32 = (lax.broadcasted_iota(jnp.int32, (16, 128), 1) & 32) == 0
    for s in range(2):
        def one(n, _):
            scales = [decoded_scale(r_ref[0, c, n, 64:80, :]) for c in range(2)]
            for t in range(2):
                h = []
                for c in range(2):
                    at = (s * 2 + t) * 16
                    q = r_ref[0, c, n, at:at + 16, :].astype(jnp.int32).astype(jnp.float32)
                    h.append(q * scales[c][s * 2 + t:s * 2 + t + 1, :])
                base = pl.multiple_of(((s * 16 + n) * 2 + t) * 32, 32)
                full[pl.ds(base, 16), :] = jnp.where(low32, h[0], pltpu.roll(h[1], 32, 1))
                full[pl.ds(base + 16, 16), :] = jnp.where(low32, pltpu.roll(h[0], 96, 1), h[1])
            return 0

        lax.fori_loop(0, 16, one, 0, unroll=4)
    for p in range(32):
        o_ref[:, p * 128:(p + 1) * 128] = full[pl.ds(p, 64, stride=32), :]


def unpack(received):
    return pl.pallas_call(
        unpack_kernel,
        grid=(X,),
        in_specs=[pl.BlockSpec((1, C, 16, MSG, 128), lambda x: (x, 0, 0, 0, 0))],
        out_specs=pl.BlockSpec((64, 4096), lambda x: (x, 0)),
        out_shape=jax.ShapeDtypeStruct((256, 4096), jnp.float32),
        scratch_shapes=[pltpu.VMEM((64 * 32, 128), jnp.float32)],
        compiler_params=pltpu.CompilerParams(vmem_limit_bytes=32 << 20),
        name="unpack",
    )(received)


def local(kohn_blocks, kohn_columns, density_blocks, density_columns, owner_map):
    x, c = lax.axis_index("x"), lax.axis_index("core")
    z, y = lax.axis_index("z"), lax.axis_index("y")
    on_line, on_cross = jnp.where(c == 0, z, y), jnp.where(c == 0, y, z)
    at = jnp.stack([c, on_line, on_cross, x])

    kohn = kohn_blocks.reshape(16, 4, SK * 32, 128)
    kohn_other = over_core(kohn)

    ints = jnp.concatenate([
        kohn_columns.reshape(2, 128), jnp.pad(density_columns.reshape(1, 64), ((0, 0), (0, 64))),
        owner_map.reshape(1, 128), jnp.zeros((12, 128), jnp.int32),
    ])
    dens, kohn = lax.optimization_barrier((density_blocks[0], kohn))

    mine, theirs = split(at, dens, ints)
    shard = jnp.concatenate([mine, over_core(theirs)])
    shard, kohn, kohn_other = lax.optimization_barrier((shard, kohn, kohn_other))
    left, right = over_x(shard, 1), over_x(shard, -1)

    kohn, ahead, back = regroup(at, kohn, kohn_other)
    kohn_prev, kohn_next = over_line(ahead, 1), over_line(back, -1)
    opposite0, opposite1 = over_line(kohn_prev[2:], 1), over_line(kohn_next[2:], -1)

    far0, far1 = over_x(left[:PART], 1), over_x(right[PART:], -1)
    panel = jnp.concatenate([shard, left, right, far0, far1])
    sent, kohn_prev, kohn_next = lax.optimization_barrier((panel, kohn_prev, kohn_next))
    prev, after = over_line(sent, 1), over_line(sent, -1)

    rows = panel.reshape(8, PART, 128)[:, 8 * 128:8 * 128 + 8].astype(jnp.int32)
    words = jnp.concatenate([rows[:, 2, :64].reshape(4, 128), rows[:2, :2].reshape(4, 128)])

    def indices(word):
        targets = (on_cross + jnp.array(ORDER, jnp.int32)) % 4
        places = jnp.where(c == 0, on_line * Y + targets, targets * Y + on_line)
        k = word[4:].reshape(2, 16, 4, SK)[:, places].transpose(1, 0, 2, 3).reshape(-1)
        away = ((k >> 4) - x) & 3
        slot = jnp.where(away == 0, 0, jnp.where(away == 3, 1, away + 1))
        return slot * 16 + ((k & 15) ^ (8 * c)), word[:4].reshape(-1)

    def both(array):
        return [(array, 0), (array, 1)]

    everything = ((None, 0), (None, 1))
    sums, = panel_sums("own_panel", "first", *indices(words), both(kohn), [panel], everything, us=9.0)
    words, sums = lax.optimization_barrier((words, sums))
    near = tuple(jnp.concatenate(pair) for pair in zip(indices(over_line(words, 1)), indices(over_line(words, -1))))
    far = indices(over_line(words, 2))

    owners = jnp.stack([owner_map.reshape(128), shard[PART + 8 * 128 + 3].astype(jnp.int32)])
    hit = (owners[..., None] == jnp.arange(128, dtype=jnp.int32)).astype(jnp.int32)
    ranks = jnp.sum(jnp.cumsum(hit, axis=1) * hit, axis=2) - 1
    source = jnp.arange(2, dtype=jnp.int32)[:, None] ^ c
    slots = (owners * 4 + source * 2 + ranks).reshape(-1)

    prev, after, sums, near, far, opposite0, opposite1 = lax.optimization_barrier(
        (prev, after, sums, near, far, opposite0, opposite1)
    )
    far_low, far_high = over_line(prev[:4 * PART], 1), over_line(after[4 * PART:], -1)
    sums, = panel_sums(
        "near_panels", "more", *near, both(kohn_prev) + both(kohn_next), [prev, after], everything, sums, us=16.0
    )

    def last(form, halves, received=()):
        kohn = [((opposite0, opposite1)[m], 0) for _, m in halves]
        return panel_sums("last_" + form, form, *far, kohn, [far_low, far_high], halves, sums, received)

    via_next, via_prev = last("coded", ((0, 0), (0, 1)))
    via_next, via_prev = over_cross(via_next, 1), over_cross(via_prev, -1)
    next1, prev0 = last("coded", ((1, 1), (2, 0)))
    prev_1, next_0 = over_cross(next1, 1), over_cross(prev0, -1)
    next0, prev1 = last("sent", ((1, 0), (2, 1)), (via_next, via_prev))
    prev_0, next_1 = over_cross(next0, 1), over_cross(prev1, -1)
    own, = last("own", ((3, 0), (3, 1)))

    outgoing = pack(slots, own, prev_0, prev_1, next_0, next_1)
    received = lax.all_to_all(outgoing, ALL, split_axis=0, concat_axis=0, tiled=True)
    return unpack(received.reshape(X, C, 16, MSG, 128))


def solution(mesh):
    grid = Mesh(mesh.devices.reshape(X, C, Z, Y), ALL)
    row, col = ("x", "core"), ("z", "y")
    return jax.shard_map(
        local,
        mesh=grid,
        in_specs=(
            P(row, col, None, None),
            P(row, col, None),
            P(col, row, None, None),
            P(col, row, None),
            P(ALL, None),
        ),
        out_specs=P(ALL, None),
        check_vma=False,
    )
```

```python
import jax
import jax.numpy as jnp
from jax import lax
from jax.experimental import pallas as pl
from jax.experimental.pallas import tpu as pltpu
from jax.sharding import Mesh, PartitionSpec as P

B = 64
HALF = 32
NCW = 32
SK = 4
SP = 8
X, C, Z, Y = 4, 2, 4, 4
ALL = ("x", "core", "z", "y")
PLANE = ("core", "z", "y")
TOP = 32766.0
MSG = 80
LIMIT = 16
PART = 8 * 128 + 16
ORDER = (2, 1, 3, 0)


def lines(along):
    groups = []
    for c in range(C):
        for fixed in range(4):
            on_z = (c ^ along) == 0
            groups.append([(c * Z + (i if on_z else fixed)) * Y + (fixed if on_z else i) for i in range(4)])
    return groups


LINE, CROSS = lines(0), lines(1)


def over(groups, v, step):
    return lax.ppermute(v, PLANE, [(group[i], group[(i + step) % 4]) for group in groups for i in range(4)])


def over_line(v, step):
    return over(LINE, v, step)


def over_cross(v, step):
    return over(CROSS, v, step)


def over_x(v, step):
    return lax.ppermute(v, "x", [(i, (i + step) % X) for i in range(X)])


def over_core(v):
    return lax.ppermute(v, "core", [(0, 1), (1, 0)])


def split_kernel(core, d_ref, i_ref, mine, theirs, flat, wide):
    lane32 = lax.broadcasted_iota(jnp.int32, (32, 128), 1)
    lane64 = lax.broadcasted_iota(jnp.int32, (64, 128), 1)

    def one(k, _):
        rows = d_ref[k].astype(jnp.float32)
        for p in range(32):
            flat[p * 8:(p + 1) * 8, :] = rows[:, p * 128:(p + 1) * 128]
        v = []
        for b in range(4):
            lo, hi = flat[pl.ds(b, 32, stride=8), :], flat[pl.ds(b + 4, 32, stride=8), :]
            wide[b, pl.ds(0, 32, stride=2), :] = jnp.where(lane32 < 64, lo, pltpu.roll(hi, 64, 1))
            wide[b, pl.ds(1, 32, stride=2), :] = jnp.where(lane32 < 64, pltpu.roll(lo, 64, 1), hi)
        v = [wide[b] for b in range(4)]
        for bit in (2, 1):
            keep = (lane64 & (16 * bit)) == 0
            w = [None] * 4
            for i in range(4):
                if not i & bit:
                    lo, hi = v[i], v[i | bit]
                    w[i] = jnp.where(keep, lo, pltpu.roll(hi, 16 * bit, 1))
                    w[i | bit] = jnp.where(keep, pltpu.roll(lo, 128 - 16 * bit, 1), hi)
            v = w
        first = jnp.concatenate([v[0], v[1]], axis=0).T
        second = jnp.concatenate([v[2], v[3]], axis=0).T
        swapped = core[0] == 1
        at = pl.ds(pl.multiple_of(k * 128, 128), 128)
        mine[at, :] = jnp.where(swapped, second, first).astype(jnp.bfloat16)
        theirs[at, :] = jnp.where(swapped, first, second).astype(jnp.bfloat16)
        return 0

    lax.fori_loop(0, 8, one, 0)
    ints = i_ref[...].astype(jnp.float32).astype(jnp.bfloat16)
    mine[8 * 128:, :] = ints
    theirs[8 * 128:, :] = ints


def split(core, dens, ints):
    half = jax.ShapeDtypeStruct((PART, 128), jnp.bfloat16)
    whole = pl.BlockSpec((PART, 128), lambda i, *_: (0, 0))
    return pl.pallas_call(
        split_kernel,
        grid_spec=pltpu.PrefetchScalarGridSpec(
            num_scalar_prefetch=1, grid=(1,),
            in_specs=[
                pl.BlockSpec((8, SP, B * B), lambda i, *_: (0, 0, 0)), pl.BlockSpec((16, 128), lambda i, *_: (0, 0))
            ],
            out_specs=[whole, whole],
            scratch_shapes=[pltpu.VMEM((256, 128), jnp.float32), pltpu.VMEM((4, B, 128), jnp.float32)],
        ),
        out_shape=[half, half],
        name="split",
    )(core, dens, ints)


def regroup_kernel(at, mine, other, own, ahead, back, far0, far1, sems):
    swapped, line, cross = at[0] == 1, at[1], at[2]
    copies = []
    for step in range(4):
        t = (line + step) % 4
        for i, rel in enumerate(ORDER):
            o = (cross + rel) % 4
            row = jnp.where(swapped, o * 4 + t, t * 4 + o)
            for m, src in enumerate((mine, other)):
                dst = (own.at[m, i], ahead.at[m, i], (far0, far1)[m].at[0, i], back.at[m, i])[step]
                copies.append(pltpu.make_async_copy(src.at[row], dst, sems.at[len(copies)]))
    for copy in copies:
        copy.start()
    for copy in copies:
        copy.wait()


def regroup(at, mine, other):
    shapes = [(2, 4, 4, 128, 128)] * 3 + [(1, 4, 4, 128, 128)] * 2
    return pl.pallas_call(
        regroup_kernel,
        grid_spec=pltpu.PrefetchScalarGridSpec(
            num_scalar_prefetch=1, grid=(1,),
            in_specs=[pl.BlockSpec((16, 4, 128, 128), lambda i, *_: (0, 0, 0, 0), pipeline_mode=pl.Buffered(1))] * 2,
            out_specs=[pl.BlockSpec(memory_space=pl.ANY)] * 5,
            scratch_shapes=[pltpu.SemaphoreType.DMA((32,))],
        ),
        out_shape=[jax.ShapeDtypeStruct(shape, jnp.bfloat16) for shape in shapes],
        compiler_params=pltpu.CompilerParams(vmem_limit_bytes=12 << 20),
        name="regroup",
    )(at, mine, other)


def encode(values, put, write_code):
    top = jnp.zeros((16, 128), jnp.float32)
    for j in range(NCW):
        top = jnp.maximum(top, jnp.abs(values[j]))
    top = jnp.maximum(jnp.max(top, axis=0, keepdims=True), 2.0 ** -110)
    code = jnp.floor(jnp.log2(top) * 256.0) + 1.0
    scale = jnp.broadcast_to(jnp.exp2(code * (-1.0 / 256.0)) * TOP, (16, 128))
    write_code(jnp.broadcast_to(code.astype(jnp.int32), (16, 128)))
    for j in range(NCW):
        put(j, jnp.floor(values[j] * scale + 0.5).astype(jnp.int32).astype(jnp.int16))


def decoded_scale(code):
    return jnp.exp2(code.astype(jnp.int32).astype(jnp.float32) * (1.0 / 256.0)) * (1.0 / TOP)


def panel_kernel(n, pieces, halves, form, at, *refs):
    kohn, refs = refs[:2 * n], refs[2 * n:]
    panels, refs = refs[:pieces], refs[pieces:]
    if form != "first":
        sums_in, refs = refs[0], refs[1:]
    if form == "sent":
        received, refs = refs[:2], refs[2:]
    outs, (dens, sems, acc, in_sems, out_sems, staged, ints) = refs[:-7], refs[-7:]
    size = n * 8 * PART // pieces
    core, line, cross, x = at[0], at[1], at[2], at[3]

    loads = [pltpu.make_async_copy(panels[s], dens.at[pl.ds(s * size, size)], sems.at[s]) for s in range(pieces)]
    sums = []
    if form != "first":
        for h, (target, m) in enumerate(halves):
            src = sums_in.at[target, pl.ds(m * 4, 4)]
            sums.append(pltpu.make_async_copy(src, acc.at[h], in_sems.at[h]))
    stores = []
    if form in ("first", "more"):
        for h, (target, m) in enumerate(halves):
            dst = outs[0].at[target if len(halves) > 2 else 0, pl.ds(m * 4, 4)]
            stores.append(pltpu.make_async_copy(acc.at[h], dst, out_sems.at[h]))
    for copy in loads + sums:
        copy.start()
    for copy in loads:
        copy.wait()
    for s in range(n):
        rows = [dens[pl.ds((s * 8 + p) * PART + 8 * 128, 16), :].astype(jnp.float32) for p in range(8)]
        rows = [row[2:3] for row in rows] + [rows[0][0:2], rows[1][0:2], jnp.zeros((4, 128), jnp.float32)]
        staged[s * 16:(s + 1) * 16, :] = jnp.concatenate(rows, axis=0).astype(jnp.int32)
    copy = pltpu.make_async_copy(staged, ints, sems.at[pieces])
    copy.start()
    copy.wait()

    low = (lax.broadcasted_iota(jnp.int32, (32, 128), 1) < 64).astype(jnp.float32).astype(jnp.bfloat16)
    high = 1 - low

    def twice(blk):
        turned = jnp.concatenate([blk[:, B:], blk[:, :B]], axis=1)
        return jnp.concatenate([blk * low, turned * low, turned * high, blk * high], axis=0)

    def product(h, r, s, a):
        target, m = halves[h]
        goal = (cross + ORDER[target]) & 3
        place = jnp.where(core == 1, goal * 4 + line, line * 4 + goal)
        k = ints[s * 16 + 8 + m * 2 + (place >> 3), (place & 7) * 16 + r * 4 + a]
        slot = (120 >> (2 * (((k >> 4) - x) & 3))) & 3
        k = slot * 16 + ((k & 15) ^ (8 * core))
        part = s * 8 + (k >> 3)
        left = dens[pl.ds(pl.multiple_of(part * PART + (k & 7) * 128, 16), 128), :]
        ref, index = kohn[2 * s + m], target if kohn[2 * s + m].shape[1] == 4 else 0
        right = twice(ref[0, index, r, a * 32:(a + 1) * 32, :])
        r = lax.dot_general(left, right, (((1,), (1,)), ((), ())), preferred_element_type=jnp.float32)
        return s * 16 + (k >> 3), (k & 7) * SP, r

    def add(total, word, first, r):
        js = [ints[word, first + b] for b in range(SP)]
        old = [total[j] for j in js]
        for b in range(SP):
            total[js[b]] = old[b] + r[b * 16:(b + 1) * 16, :]

    def two_rows(h, pair):
        work, totals = [], []
        for q in range(2):
            r = pair * 2 + q
            work += [(q, r, s, a) for s in range(n) for a in range(SK)]
            total = acc.at[h, r]
            if form == "first":
                total[...] = jnp.zeros((NCW, 16, 128), jnp.float32)
            elif form == "sent":
                scale = decoded_scale(received[h][r, NCW])
                for j in range(NCW):
                    total[j] = total[j] + received[h][r, j].astype(jnp.int32).astype(jnp.float32) * scale
            totals.append(total)
        held = [product(h, *work[i][1:]) for i in range(3)]
        for i in range(len(work)):
            if i + 3 < len(work):
                held.append(product(h, *work[i + 3][1:]))
            add(totals[work[i][0]], *held[i])
        if form in ("coded", "sent"):
            for q in range(2):
                r = pair * 2 + q

                def put(j, value, r=r):
                    outs[h][r, j] = value

                encode(totals[q], put, lambda code, put=put: put(NCW, code.astype(jnp.int16)))

    for h in range(len(halves)):
        if sums:
            sums[h].wait()
        lax.fori_loop(0, 2, lambda pair, _, h=h: (two_rows(h, pair), 0)[1], 0)
        if stores:
            stores[h].start()
    for copy in stores:
        copy.wait()


def panel_sums(name, form, at, kohn, panels, halves, sums=None, received=(), us=4.0):
    n, pieces, groups = len(kohn) // 2, len(panels), len(halves)

    def k_spec(i, place):
        if groups > 2:
            return pl.BlockSpec((1, 4, 4, 128, 128), lambda *_: (place, 0, 0, 0, 0), pipeline_mode=pl.Buffered(1))
        target = {m: t for t, m in halves}[i % 2]
        return pl.BlockSpec((1, 1, 4, 128, 128), lambda *_: (place, target, 0, 0, 0), pipeline_mode=pl.Buffered(1))

    any_spec = pl.BlockSpec(memory_space=pl.ANY)
    sums_spec = pl.BlockSpec(memory_space=pltpu.HBM)
    coded = pl.BlockSpec((4, NCW + 1, 16, 128), lambda *_: (0, 0, 0, 0), pipeline_mode=pl.Buffered(1))
    if form in ("coded", "sent"):
        o_specs = [coded] * 2
        shapes = [jax.ShapeDtypeStruct((4, NCW + 1, 16, 128), jnp.int16)] * 2
    else:
        o_specs = [sums_spec if groups > 2 else any_spec]
        shapes = [jax.ShapeDtypeStruct((max(groups // 2, 1), 8, NCW, 16, 128), jnp.float32)]
    return pl.pallas_call(
        lambda *refs: panel_kernel(n, pieces, halves, form, *refs),
        grid_spec=pltpu.PrefetchScalarGridSpec(
            num_scalar_prefetch=1,
            grid=(1,),
            in_specs=(
                [k_spec(i, place) for i, (_, place) in enumerate(kohn)] + [any_spec] * pieces
                + ([] if sums is None else [sums_spec]) + [coded] * len(received)
            ),
            out_specs=o_specs,
            scratch_shapes=[
                pltpu.VMEM((n * 8 * PART, 128), jnp.bfloat16),
                pltpu.SemaphoreType.DMA((pieces + 1,)),
                pltpu.VMEM((groups, 4, NCW, 16, 128), jnp.float32),
                pltpu.SemaphoreType.DMA((groups,)),
                pltpu.SemaphoreType.DMA((groups,)),
                pltpu.VMEM((n * 16, 128), jnp.int32),
                pltpu.SMEM((n * 16, 128), jnp.int32),
            ],
        ),
        out_shape=shapes,
        compiler_params=pltpu.CompilerParams(vmem_limit_bytes=LIMIT << 20),
        cost_estimate=pl.CostEstimate(flops=int(us * 1.1e9), bytes_accessed=int(us * 2e6), transcendentals=0),
        name=name,
    )(at, *[array for array, _ in kohn], *panels, *([] if sums is None else [sums]), *received)


def pack_kernel(slots, own, prev0, prev1, next0, next1, o_ref, total, codes):
    rows = lax.broadcasted_iota(jnp.int32, (16, 128), 0)
    lane = lax.broadcasted_iota(jnp.int32, (16, 128), 1)

    def clear(n, _):
        for m in range(4):
            o_ref[n * 4 + m] = jnp.zeros((MSG, 128), jnp.int16)
            codes[n * 4 + m] = jnp.zeros((16, 128), jnp.int32)
        return 0

    lax.fori_loop(0, 32, clear, 0)

    def one(m, r):
        row = m * 4 + r
        coded = [((prev0, prev1)[m], r), ((next0, next1)[m], r)]
        scales = [decoded_scale(ref[at, NCW]) for ref, at in coded]
        for group in range(NCW // 8):
            blocks = []
            for j in range(group * 8, group * 8 + 8):
                g = [ref[at, j].astype(jnp.int32).astype(jnp.float32) * scale for (ref, at), scale in zip(coded, scales)]
                blocks.append(own[0, row, j] + g[0] + g[1])
            turned = jnp.concatenate(blocks, axis=0).T
            v = []
            for q in range(8):
                par, mh, zh = q // 4, (q // 2) % 2, q % 2
                at = (zh * 4 + par * 2 + mh) * 16
                v.append(turned[at:at + 16, :])
            for bit in (4, 2, 1):
                keep = (lane & (16 * bit)) == 0
                w = [None] * 8
                for i in range(8):
                    if not i & bit:
                        lo, hi = v[i], v[i | bit]
                        w[i] = jnp.where(keep, lo, pltpu.roll(hi, 16 * bit, 1))
                        w[i | bit] = jnp.where(keep, pltpu.roll(lo, 128 - 16 * bit, 1), hi)
                v = w
            for j in range(8):
                total[group * 8 + j] = v[j]

        def put(j, value):
            slot = slots[row * NCW + j]
            o_ref[slot // 4, pl.ds(pl.multiple_of((slot % 4) * 16, 16), 16), :] = value

        def write_code(code):
            for j in range(NCW):
                slot = slots[row * NCW + j]
                codes[slot // 4] = jnp.where(rows == slot % 4, code, codes[slot // 4])

        encode(total, put, write_code)

    for m in range(2):
        lax.fori_loop(0, 4, lambda r, _, m=m: (one(m, r), 0)[1], 0)

    def finish(n, _):
        for m in range(4):
            o_ref[n * 4 + m, 64:80, :] = codes[n * 4 + m].astype(jnp.int16)
        return 0

    lax.fori_loop(0, 32, finish, 0)


def pack(slots, *parts):
    def whole(array):
        return pl.BlockSpec(
            array.shape, lambda i, *_, n=array.ndim: (0,) * n, pipeline_mode=pl.Buffered(1)
        )

    return pl.pallas_call(
        pack_kernel,
        grid_spec=pltpu.PrefetchScalarGridSpec(
            num_scalar_prefetch=1,
            grid=(1,),
            in_specs=[whole(array) for array in parts],
            out_specs=pl.BlockSpec((128, MSG, 128), lambda i, *_: (0, 0, 0), pipeline_mode=pl.Buffered(1)),
            scratch_shapes=[pltpu.VMEM((NCW, 16, 128), jnp.float32), pltpu.VMEM((128, 16, 128), jnp.int32)],
        ),
        out_shape=jax.ShapeDtypeStruct((128, MSG, 128), jnp.int16),
        compiler_params=pltpu.CompilerParams(vmem_limit_bytes=32 << 20),
        name="pack",
    )(slots, *parts)


def unpack_kernel(r_ref, o_ref, full):
    low32 = (lax.broadcasted_iota(jnp.int32, (16, 128), 1) & 32) == 0
    for s in range(2):
        def one(n, _):
            scales = [decoded_scale(r_ref[0, c, n, 64:80, :]) for c in range(2)]
            for t in range(2):
                h = []
                for c in range(2):
                    at = (s * 2 + t) * 16
                    q = r_ref[0, c, n, at:at + 16, :].astype(jnp.int32).astype(jnp.float32)
                    h.append(q * scales[c][s * 2 + t:s * 2 + t + 1, :])
                base = pl.multiple_of(((s * 16 + n) * 2 + t) * 32, 32)
                full[pl.ds(base, 16), :] = jnp.where(low32, h[0], pltpu.roll(h[1], 32, 1))
                full[pl.ds(base + 16, 16), :] = jnp.where(low32, pltpu.roll(h[0], 96, 1), h[1])
            return 0

        lax.fori_loop(0, 16, one, 0, unroll=4)
    for p in range(32):
        o_ref[:, p * 128:(p + 1) * 128] = full[pl.ds(p, 64, stride=32), :]


def unpack(received):
    return pl.pallas_call(
        unpack_kernel,
        grid=(X,),
        in_specs=[pl.BlockSpec((1, C, 16, MSG, 128), lambda x: (x, 0, 0, 0, 0))],
        out_specs=pl.BlockSpec((64, 4096), lambda x: (x, 0)),
        out_shape=jax.ShapeDtypeStruct((256, 4096), jnp.float32),
        scratch_shapes=[pltpu.VMEM((64 * 32, 128), jnp.float32)],
        compiler_params=pltpu.CompilerParams(vmem_limit_bytes=32 << 20),
        name="unpack",
    )(received)


def local(kohn_blocks, kohn_columns, density_blocks, density_columns, owner_map):
    x, c = lax.axis_index("x"), lax.axis_index("core")
    z, y = lax.axis_index("z"), lax.axis_index("y")
    on_line, on_cross = jnp.where(c == 0, z, y), jnp.where(c == 0, y, z)
    at = jnp.stack([c, on_line, on_cross, x])

    kohn = kohn_blocks.reshape(16, 4, SK * 32, 128)
    kohn_other = over_core(kohn)

    ints = jnp.concatenate([
        kohn_columns.reshape(2, 128), jnp.pad(density_columns.reshape(1, 64), ((0, 0), (0, 64))),
        owner_map.reshape(1, 128), jnp.zeros((12, 128), jnp.int32),
    ])
    dens, kohn = lax.optimization_barrier((density_blocks[0], kohn))

    mine, theirs = split(at, dens, ints)
    shard = jnp.concatenate([mine, over_core(theirs)])
    shard, kohn, kohn_other = lax.optimization_barrier((shard, kohn, kohn_other))
    left, right = over_x(shard, 1), over_x(shard, -1)

    kohn, ahead, back, opposite0, opposite1 = regroup(at, kohn, kohn_other)
    opposite0, opposite1 = over_line(opposite0, 1), over_line(opposite1, -1)
    kohn_prev, kohn_next = over_line(ahead, 1), over_line(back, -1)
    opposite0, opposite1 = over_line(opposite0, 1), over_line(opposite1, -1)

    panel = jnp.concatenate([shard, left, right, over_x(left[:PART], 1), over_x(right[PART:], -1)])
    sent, kohn_prev, kohn_next, opposite0, opposite1 = lax.optimization_barrier(
        (panel, kohn_prev, kohn_next, opposite0, opposite1)
    )
    prev, after = over_line(sent, 1), over_line(sent, -1)

    owners = jnp.stack([owner_map.reshape(128), shard[PART + 8 * 128 + 3].astype(jnp.int32)])
    hit = (owners[..., None] == jnp.arange(128, dtype=jnp.int32)).astype(jnp.int32)
    ranks = jnp.sum(jnp.cumsum(hit, axis=1) * hit, axis=2) - 1
    source = jnp.arange(2, dtype=jnp.int32)[:, None] ^ c
    slots = (owners * 4 + source * 2 + ranks).reshape(-1)

    def both(array):
        return [(array, 0), (array, 1)]

    everything = tuple((target, m) for target in range(4) for m in range(2))
    sums, = panel_sums("own_panel", "first", at, both(kohn), [panel], everything, us=9.0)
    prev, after, sums = lax.optimization_barrier((prev, after, sums))
    far_low, far_high = over_line(prev[:4 * PART], 1), over_line(after[4 * PART:], -1)
    sums, = panel_sums(
        "near_panels", "more", at, both(kohn_prev) + both(kohn_next), [prev, after], everything, sums, us=16.0
    )

    def last(form, halves, received=()):
        kohn = [(opposite0, 0), (opposite1, 0)]
        return panel_sums("last_" + form, form, at, kohn, [far_low, far_high], halves, sums, received)

    via_next, via_prev = last("coded", ((0, 0), (0, 1)))
    via_next, via_prev = over_cross(via_next, 1), over_cross(via_prev, -1)
    next1, prev0 = last("coded", ((1, 1), (2, 0)))
    prev_1, next_0 = over_cross(next1, 1), over_cross(prev0, -1)
    next0, prev1 = last("sent", ((1, 0), (2, 1)), (via_next, via_prev))
    prev_0, next_1 = over_cross(next0, 1), over_cross(prev1, -1)
    own, = last("more", ((3, 0), (3, 1)))

    outgoing = pack(slots, own, prev_0, prev_1, next_0, next_1)
    received = lax.all_to_all(outgoing, ALL, split_axis=0, concat_axis=0, tiled=True)
    return unpack(received.reshape(X, C, 16, MSG, 128))


def solution(mesh):
    grid = Mesh(mesh.devices.reshape(X, C, Z, Y), ALL)
    row, col = ("x", "core"), ("z", "y")
    return jax.shard_map(
        local,
        mesh=grid,
        in_specs=(
            P(row, col, None, None),
            P(row, col, None),
            P(col, row, None, None),
            P(col, row, None),
            P(ALL, None),
        ),
        out_specs=P(ALL, None),
        check_vma=False,
    )
```

```python
import jax
import jax.numpy as jnp
from jax import lax
from jax.experimental import pallas as pl
from jax.experimental.pallas import tpu as pltpu
from jax.sharding import Mesh, PartitionSpec as P

B = 64
HALF = 32
NCW = 32
SK = 4
SP = 8
X, C, Z, Y = 4, 2, 4, 4
ALL = ("x", "core", "z", "y")
PLANE = ("core", "z", "y")
TOP = 32766.0
MSG = 80
LIMIT = 16
PART = 8 * 128 + 16
ORDER = (2, 1, 3, 0)


def lines(along):
    groups = []
    for c in range(C):
        for fixed in range(4):
            on_z = (c ^ along) == 0
            groups.append([(c * Z + (i if on_z else fixed)) * Y + (fixed if on_z else i) for i in range(4)])
    return groups


LINE, CROSS = lines(0), lines(1)


def over(groups, v, step):
    return lax.ppermute(v, PLANE, [(group[i], group[(i + step) % 4]) for group in groups for i in range(4)])


def over_line(v, step):
    return over(LINE, v, step)


def over_cross(v, step):
    return over(CROSS, v, step)


def over_x(v, step):
    return lax.ppermute(v, "x", [(i, (i + step) % X) for i in range(X)])


def over_core(v):
    return lax.ppermute(v, "core", [(0, 1), (1, 0)])


def split_kernel(core, d_ref, i_ref, mine, theirs, flat, wide):
    lane32 = lax.broadcasted_iota(jnp.int32, (32, 128), 1)
    lane64 = lax.broadcasted_iota(jnp.int32, (64, 128), 1)

    def one(k, _):
        rows = d_ref[k].astype(jnp.float32)
        for p in range(32):
            flat[p * 8:(p + 1) * 8, :] = rows[:, p * 128:(p + 1) * 128]
        v = []
        for b in range(4):
            lo, hi = flat[pl.ds(b, 32, stride=8), :], flat[pl.ds(b + 4, 32, stride=8), :]
            wide[b, pl.ds(0, 32, stride=2), :] = jnp.where(lane32 < 64, lo, pltpu.roll(hi, 64, 1))
            wide[b, pl.ds(1, 32, stride=2), :] = jnp.where(lane32 < 64, pltpu.roll(lo, 64, 1), hi)
        v = [wide[b] for b in range(4)]
        for bit in (2, 1):
            keep = (lane64 & (16 * bit)) == 0
            w = [None] * 4
            for i in range(4):
                if not i & bit:
                    lo, hi = v[i], v[i | bit]
                    w[i] = jnp.where(keep, lo, pltpu.roll(hi, 16 * bit, 1))
                    w[i | bit] = jnp.where(keep, pltpu.roll(lo, 128 - 16 * bit, 1), hi)
            v = w
        first = jnp.concatenate([v[0], v[1]], axis=0).T
        second = jnp.concatenate([v[2], v[3]], axis=0).T
        swapped = core[0] == 1
        at = pl.ds(pl.multiple_of(k * 128, 128), 128)
        mine[at, :] = jnp.where(swapped, second, first).astype(jnp.bfloat16)
        theirs[at, :] = jnp.where(swapped, first, second).astype(jnp.bfloat16)
        return 0

    lax.fori_loop(0, 8, one, 0)
    ints = i_ref[...].astype(jnp.float32).astype(jnp.bfloat16)
    mine[8 * 128:, :] = ints
    theirs[8 * 128:, :] = ints


def split(core, dens, ints):
    half = jax.ShapeDtypeStruct((PART, 128), jnp.bfloat16)
    whole = pl.BlockSpec((PART, 128), lambda i, *_: (0, 0))
    return pl.pallas_call(
        split_kernel,
        grid_spec=pltpu.PrefetchScalarGridSpec(
            num_scalar_prefetch=1, grid=(1,),
            in_specs=[
                pl.BlockSpec((8, SP, B * B), lambda i, *_: (0, 0, 0)), pl.BlockSpec((16, 128), lambda i, *_: (0, 0))
            ],
            out_specs=[whole, whole],
            scratch_shapes=[pltpu.VMEM((256, 128), jnp.float32), pltpu.VMEM((4, B, 128), jnp.float32)],
        ),
        out_shape=[half, half],
        name="split",
    )(core, dens, ints)


def regroup_kernel(at, mine, other, own, ahead, back, far0, far1, sems):
    swapped, line, cross = at[0] == 1, at[1], at[2]
    copies = []
    for step in range(4):
        t = (line + step) % 4
        for i, rel in enumerate(ORDER):
            o = (cross + rel) % 4
            row = jnp.where(swapped, o * 4 + t, t * 4 + o)
            for m, src in enumerate((mine, other)):
                dst = (own.at[m, i], ahead.at[m, i], (far0, far1)[m].at[0, i], back.at[m, i])[step]
                copies.append(pltpu.make_async_copy(src.at[row], dst, sems.at[len(copies)]))
    for copy in copies:
        copy.start()
    for copy in copies:
        copy.wait()


def regroup(at, mine, other):
    shapes = [(2, 4, 4, 128, 128)] * 3 + [(1, 4, 4, 128, 128)] * 2
    return pl.pallas_call(
        regroup_kernel,
        grid_spec=pltpu.PrefetchScalarGridSpec(
            num_scalar_prefetch=1, grid=(1,),
            in_specs=[pl.BlockSpec(memory_space=pl.ANY)] * 2,
            out_specs=[pl.BlockSpec(s, lambda i, *_: (0,) * 5, pipeline_mode=pl.Buffered(1)) for s in shapes],
            scratch_shapes=[pltpu.SemaphoreType.DMA((32,))],
        ),
        out_shape=[jax.ShapeDtypeStruct(shape, jnp.bfloat16) for shape in shapes],
        compiler_params=pltpu.CompilerParams(vmem_limit_bytes=12 << 20),
        name="regroup",
    )(at, mine, other)


def encode(values, put, write_code):
    top = jnp.zeros((16, 128), jnp.float32)
    for j in range(NCW):
        top = jnp.maximum(top, jnp.abs(values[j]))
    top = jnp.maximum(jnp.max(top, axis=0, keepdims=True), 2.0 ** -110)
    code = jnp.floor(jnp.log2(top) * 256.0) + 1.0
    scale = jnp.broadcast_to(jnp.exp2(code * (-1.0 / 256.0)) * TOP, (16, 128))
    write_code(jnp.broadcast_to(code.astype(jnp.int32), (16, 128)))
    for j in range(NCW):
        put(j, jnp.floor(values[j] * scale + 0.5).astype(jnp.int32).astype(jnp.int16))


def decoded_scale(code):
    return jnp.exp2(code.astype(jnp.int32).astype(jnp.float32) * (1.0 / 256.0)) * (1.0 / TOP)


def panel_kernel(n, pieces, halves, form, at, *refs):
    kohn, refs = refs[:2 * n], refs[2 * n:]
    panels, refs = refs[:pieces], refs[pieces:]
    if form != "first":
        sums_in, refs = refs[0], refs[1:]
    if form == "sent":
        received, refs = refs[:2], refs[2:]
    outs, (dens, sems, acc, in_sems, out_sems, staged, ints) = refs[:-7], refs[-7:]
    size = n * 8 * PART // pieces
    core, line, cross, x = at[0], at[1], at[2], at[3]

    loads = [pltpu.make_async_copy(panels[s], dens.at[pl.ds(s * size, size)], sems.at[s]) for s in range(pieces)]
    sums = []
    if form != "first":
        for h, (target, m) in enumerate(halves):
            src = sums_in.at[target, pl.ds(m * 4, 4)]
            sums.append(pltpu.make_async_copy(src, acc.at[h], in_sems.at[h]))
    stores = []
    if form in ("first", "more"):
        for h, (target, m) in enumerate(halves):
            dst = outs[0].at[target if len(halves) > 2 else 0, pl.ds(m * 4, 4)]
            stores.append(pltpu.make_async_copy(acc.at[h], dst, out_sems.at[h]))
    for copy in loads + sums:
        copy.start()
    for copy in loads:
        copy.wait()
    for s in range(n):
        rows = [dens[pl.ds((s * 8 + p) * PART + 8 * 128, 16), :].astype(jnp.float32) for p in range(8)]
        rows = [row[2:3] for row in rows] + [rows[0][0:2], rows[1][0:2], jnp.zeros((4, 128), jnp.float32)]
        staged[s * 16:(s + 1) * 16, :] = jnp.concatenate(rows, axis=0).astype(jnp.int32)
    copy = pltpu.make_async_copy(staged, ints, sems.at[pieces])
    copy.start()
    copy.wait()

    low = (lax.broadcasted_iota(jnp.int32, (32, 128), 1) < 64).astype(jnp.float32).astype(jnp.bfloat16)
    high = 1 - low

    def twice(blk):
        turned = jnp.concatenate([blk[:, B:], blk[:, :B]], axis=1)
        return jnp.concatenate([blk * low, turned * low, turned * high, blk * high], axis=0)

    def product(h, r, s, a):
        target, m = halves[h]
        goal = (cross + ORDER[target]) & 3
        place = jnp.where(core == 1, goal * 4 + line, line * 4 + goal)
        k = ints[s * 16 + 8 + m * 2 + (place >> 3), (place & 7) * 16 + r * 4 + a]
        slot = (120 >> (2 * (((k >> 4) - x) & 3))) & 3
        k = slot * 16 + ((k & 15) ^ (8 * core))
        part = s * 8 + (k >> 3)
        left = dens[pl.ds(pl.multiple_of(part * PART + (k & 7) * 128, 16), 128), :]
        ref, index = kohn[2 * s + m], target if kohn[2 * s + m].shape[1] == 4 else 0
        right = twice(ref[0, index, r, a * 32:(a + 1) * 32, :])
        r = lax.dot_general(left, right, (((1,), (1,)), ((), ())), preferred_element_type=jnp.float32)
        return s * 16 + (k >> 3), (k & 7) * SP, r

    def add(total, word, first, r):
        js = [ints[word, first + b] for b in range(SP)]
        old = [total[j] for j in js]
        for b in range(SP):
            total[js[b]] = old[b] + r[b * 16:(b + 1) * 16, :]

    def two_rows(h, pair):
        work, totals = [], []
        for q in range(2):
            r = pair * 2 + q
            work += [(q, r, s, a) for s in range(n) for a in range(SK)]
            total = acc.at[h, r]
            if form == "first":
                total[...] = jnp.zeros((NCW, 16, 128), jnp.float32)
            elif form == "sent":
                scale = decoded_scale(received[h][r, NCW])
                for j in range(NCW):
                    total[j] = total[j] + received[h][r, j].astype(jnp.int32).astype(jnp.float32) * scale
            totals.append(total)
        held = [product(h, *work[i][1:]) for i in range(3)]
        for i in range(len(work)):
            if i + 3 < len(work):
                held.append(product(h, *work[i + 3][1:]))
            add(totals[work[i][0]], *held[i])
        if form in ("coded", "sent"):
            for q in range(2):
                r = pair * 2 + q

                def put(j, value, r=r):
                    outs[h][r, j] = value

                encode(totals[q], put, lambda code, put=put: put(NCW, code.astype(jnp.int16)))

    for h in range(len(halves)):
        if sums:
            sums[h].wait()
        lax.fori_loop(0, 2, lambda pair, _, h=h: (two_rows(h, pair), 0)[1], 0)
        if stores:
            stores[h].start()
    for copy in stores:
        copy.wait()


def panel_sums(name, form, at, kohn, panels, halves, sums=None, received=(), us=4.0):
    n, pieces, groups = len(kohn) // 2, len(panels), len(halves)

    def k_spec(i, place):
        if groups > 2:
            return pl.BlockSpec((1, 4, 4, 128, 128), lambda *_: (place, 0, 0, 0, 0), pipeline_mode=pl.Buffered(1))
        target = {m: t for t, m in halves}[i % 2]
        return pl.BlockSpec((1, 1, 4, 128, 128), lambda *_: (place, target, 0, 0, 0), pipeline_mode=pl.Buffered(1))

    any_spec = pl.BlockSpec(memory_space=pl.ANY)
    sums_spec = pl.BlockSpec(memory_space=pltpu.HBM)
    coded = pl.BlockSpec((4, NCW + 1, 16, 128), lambda *_: (0, 0, 0, 0), pipeline_mode=pl.Buffered(1))
    if form in ("coded", "sent"):
        o_specs = [coded] * 2
        shapes = [jax.ShapeDtypeStruct((4, NCW + 1, 16, 128), jnp.int16)] * 2
    else:
        o_specs = [sums_spec if groups > 2 else any_spec]
        shapes = [jax.ShapeDtypeStruct((max(groups // 2, 1), 8, NCW, 16, 128), jnp.float32)]
    return pl.pallas_call(
        lambda *refs: panel_kernel(n, pieces, halves, form, *refs),
        grid_spec=pltpu.PrefetchScalarGridSpec(
            num_scalar_prefetch=1,
            grid=(1,),
            in_specs=(
                [k_spec(i, place) for i, (_, place) in enumerate(kohn)] + [any_spec] * pieces
                + ([] if sums is None else [sums_spec]) + [coded] * len(received)
            ),
            out_specs=o_specs,
            scratch_shapes=[
                pltpu.VMEM((n * 8 * PART, 128), jnp.bfloat16),
                pltpu.SemaphoreType.DMA((pieces + 1,)),
                pltpu.VMEM((groups, 4, NCW, 16, 128), jnp.float32),
                pltpu.SemaphoreType.DMA((groups,)),
                pltpu.SemaphoreType.DMA((groups,)),
                pltpu.VMEM((n * 16, 128), jnp.int32),
                pltpu.SMEM((n * 16, 128), jnp.int32),
            ],
        ),
        out_shape=shapes,
        compiler_params=pltpu.CompilerParams(vmem_limit_bytes=LIMIT << 20),
        cost_estimate=pl.CostEstimate(flops=int(us * 1.1e9), bytes_accessed=int(us * 2e6), transcendentals=0),
        name=name,
    )(at, *[array for array, _ in kohn], *panels, *([] if sums is None else [sums]), *received)


def pack_kernel(slots, own, prev0, prev1, next0, next1, o_ref, total, codes):
    rows = lax.broadcasted_iota(jnp.int32, (16, 128), 0)
    lane = lax.broadcasted_iota(jnp.int32, (16, 128), 1)

    def clear(n, _):
        for m in range(4):
            o_ref[n * 4 + m] = jnp.zeros((MSG, 128), jnp.int16)
            codes[n * 4 + m] = jnp.zeros((16, 128), jnp.int32)
        return 0

    lax.fori_loop(0, 32, clear, 0)

    def one(m, r):
        row = m * 4 + r
        coded = [((prev0, prev1)[m], r), ((next0, next1)[m], r)]
        scales = [decoded_scale(ref[at, NCW]) for ref, at in coded]
        for group in range(NCW // 8):
            blocks = []
            for j in range(group * 8, group * 8 + 8):
                g = [ref[at, j].astype(jnp.int32).astype(jnp.float32) * scale for (ref, at), scale in zip(coded, scales)]
                blocks.append(own[0, row, j] + g[0] + g[1])
            turned = jnp.concatenate(blocks, axis=0).T
            v = []
            for q in range(8):
                par, mh, zh = q // 4, (q // 2) % 2, q % 2
                at = (zh * 4 + par * 2 + mh) * 16
                v.append(turned[at:at + 16, :])
            for bit in (4, 2, 1):
                keep = (lane & (16 * bit)) == 0
                w = [None] * 8
                for i in range(8):
                    if not i & bit:
                        lo, hi = v[i], v[i | bit]
                        w[i] = jnp.where(keep, lo, pltpu.roll(hi, 16 * bit, 1))
                        w[i | bit] = jnp.where(keep, pltpu.roll(lo, 128 - 16 * bit, 1), hi)
                v = w
            for j in range(8):
                total[group * 8 + j] = v[j]

        def put(j, value):
            slot = slots[row * NCW + j]
            o_ref[slot // 4, pl.ds(pl.multiple_of((slot % 4) * 16, 16), 16), :] = value

        def write_code(code):
            for j in range(NCW):
                slot = slots[row * NCW + j]
                codes[slot // 4] = jnp.where(rows == slot % 4, code, codes[slot // 4])

        encode(total, put, write_code)

    for m in range(2):
        lax.fori_loop(0, 4, lambda r, _, m=m: (one(m, r), 0)[1], 0)

    def finish(n, _):
        for m in range(4):
            o_ref[n * 4 + m, 64:80, :] = codes[n * 4 + m].astype(jnp.int16)
        return 0

    lax.fori_loop(0, 32, finish, 0)


def pack(slots, *parts):
    def whole(array):
        return pl.BlockSpec(
            array.shape, lambda i, *_, n=array.ndim: (0,) * n, pipeline_mode=pl.Buffered(1)
        )

    return pl.pallas_call(
        pack_kernel,
        grid_spec=pltpu.PrefetchScalarGridSpec(
            num_scalar_prefetch=1,
            grid=(1,),
            in_specs=[whole(array) for array in parts],
            out_specs=pl.BlockSpec((128, MSG, 128), lambda i, *_: (0, 0, 0), pipeline_mode=pl.Buffered(1)),
            scratch_shapes=[pltpu.VMEM((NCW, 16, 128), jnp.float32), pltpu.VMEM((128, 16, 128), jnp.int32)],
        ),
        out_shape=jax.ShapeDtypeStruct((128, MSG, 128), jnp.int16),
        compiler_params=pltpu.CompilerParams(vmem_limit_bytes=32 << 20),
        name="pack",
    )(slots, *parts)


def unpack_kernel(r_ref, o_ref, full, scales):
    low32 = (lax.broadcasted_iota(jnp.int32, (16, 128), 1) & 32) == 0
    for n in range(16):
        for c in range(2):
            scales[n * 2 + c] = decoded_scale(r_ref[0, c, n, 64:80, :])[:8]

    def one(n, _):
        for s in range(2):
            for t in range(2):
                h = []
                for c in range(2):
                    at = (s * 2 + t) * 16
                    q = r_ref[0, c, n, at:at + 16, :].astype(jnp.int32).astype(jnp.float32)
                    h.append(q * scales[n * 2 + c, s * 2 + t:s * 2 + t + 1, :])
                base = pl.multiple_of(((s * 16 + n) * 2 + t) * 32, 32)
                full[pl.ds(base, 16), :] = jnp.where(low32, h[0], pltpu.roll(h[1], 32, 1))
                full[pl.ds(base + 16, 16), :] = jnp.where(low32, pltpu.roll(h[0], 96, 1), h[1])
        return 0

    lax.fori_loop(0, 16, one, 0, unroll=4)
    for p in range(32):
        o_ref[:, p * 128:(p + 1) * 128] = full[pl.ds(p, 64, stride=32), :]


def unpack(received):
    return pl.pallas_call(
        unpack_kernel,
        grid=(X,),
        in_specs=[pl.BlockSpec((1, C, 16, MSG, 128), lambda x: (x, 0, 0, 0, 0))],
        out_specs=pl.BlockSpec((64, 4096), lambda x: (x, 0)),
        out_shape=jax.ShapeDtypeStruct((256, 4096), jnp.float32),
        scratch_shapes=[pltpu.VMEM((64 * 32, 128), jnp.float32), pltpu.VMEM((32, 8, 128), jnp.float32)],
        compiler_params=pltpu.CompilerParams(vmem_limit_bytes=32 << 20),
        name="unpack",
    )(received)


def local(kohn_blocks, kohn_columns, density_blocks, density_columns, owner_map):
    x, c = lax.axis_index("x"), lax.axis_index("core")
    z, y = lax.axis_index("z"), lax.axis_index("y")
    on_line, on_cross = jnp.where(c == 0, z, y), jnp.where(c == 0, y, z)
    at = jnp.stack([c, on_line, on_cross, x])

    kohn = kohn_blocks.reshape(16, 4, SK * 32, 128)
    kohn_other = over_core(kohn)

    ints = jnp.concatenate([
        kohn_columns.reshape(2, 128), jnp.pad(density_columns.reshape(1, 64), ((0, 0), (0, 64))),
        owner_map.reshape(1, 128), jnp.zeros((12, 128), jnp.int32),
    ])
    dens, kohn = lax.optimization_barrier((density_blocks[0], kohn))

    mine, theirs = split(at, dens, ints)
    shard = jnp.concatenate([mine, over_core(theirs)])
    shard, kohn, kohn_other = lax.optimization_barrier((shard, kohn, kohn_other))
    left, right, far = over_x(shard, 1), over_x(shard, -1), over_x(shard, 2)

    kohn, ahead, back, opposite0, opposite1 = regroup(at, kohn, kohn_other)
    opposite0, opposite1 = over_line(opposite0, 1), over_line(opposite1, -1)
    kohn_prev, kohn_next = over_line(ahead, 1), over_line(back, -1)
    opposite0, opposite1 = over_line(opposite0, 1), over_line(opposite1, -1)

    owners = jnp.stack([owner_map.reshape(128), shard[PART + 8 * 128 + 3].astype(jnp.int32)])
    hit = (owners[..., None] == jnp.arange(128, dtype=jnp.int32)).astype(jnp.int32)
    ranks = jnp.sum(jnp.cumsum(hit, axis=1) * hit, axis=2) - 1
    source = jnp.arange(2, dtype=jnp.int32)[:, None] ^ c
    slots = (owners * 4 + source * 2 + ranks).reshape(-1)

    low, high = jnp.concatenate([shard, left]), jnp.concatenate([right, far])
    low_sent, high_sent, kohn_prev, kohn_next, slots = lax.optimization_barrier((low, high, kohn_prev, kohn_next, slots))
    prev_low, next_high = over_line(low_sent, 1), over_line(high_sent, -1)
    prev_high, next_low = over_line(high_sent, 1), over_line(low_sent, -1)

    def both(array):
        return [(array, 0), (array, 1)]

    everything = tuple((target, m) for target in range(4) for m in range(2))
    sums, = panel_sums("own_panel", "first", at, both(kohn), [low, high], everything, us=9.0)
    prev_low, next_high, opposite0, opposite1, sums = lax.optimization_barrier(
        (prev_low, next_high, opposite0, opposite1, sums)
    )
    far_low, far_high = over_line(prev_low, 1), over_line(next_high, -1)
    sums, = panel_sums(
        "near_panels", "more", at, both(kohn_prev) + both(kohn_next), [prev_low, prev_high, next_low, next_high],
        everything, sums, us=16.0,
    )

    def last(form, halves, received=()):
        kohn = [(opposite0, 0), (opposite1, 0)]
        return panel_sums("last_" + form, form, at, kohn, [far_low, far_high], halves, sums, received)

    via_next, via_prev = last("coded", ((0, 0), (0, 1)))
    via_next, via_prev = over_cross(via_next, 1), over_cross(via_prev, -1)
    next1, prev0 = last("coded", ((1, 1), (2, 0)))
    prev_1, next_0 = over_cross(next1, 1), over_cross(prev0, -1)
    next0, prev1 = last("sent", ((1, 0), (2, 1)), (via_next, via_prev))
    prev_0, next_1 = over_cross(next0, 1), over_cross(prev1, -1)
    own, = last("more", ((3, 0), (3, 1)))

    outgoing = pack(slots, own, prev_0, prev_1, next_0, next_1)
    received = lax.all_to_all(outgoing, ALL, split_axis=0, concat_axis=0, tiled=True)
    return unpack(received.reshape(X, C, 16, MSG, 128))


def solution(mesh):
    grid = Mesh(mesh.devices.reshape(X, C, Z, Y), ALL)
    row, col = ("x", "core"), ("z", "y")
    return jax.shard_map(
        local,
        mesh=grid,
        in_specs=(
            P(row, col, None, None),
            P(row, col, None),
            P(col, row, None, None),
            P(col, row, None),
            P(ALL, None),
        ),
        out_specs=P(ALL, None),
        check_vma=False,
    )
```

```python
import jax
import jax.numpy as jnp
from jax import lax
from jax.experimental import pallas as pl
from jax.experimental.pallas import tpu as pltpu
from jax.sharding import Mesh, PartitionSpec as P

B = 64
HALF = 32
NCW = 32
SK = 4
SP = 8
X, C, Z, Y = 4, 2, 4, 4
ALL = ("x", "core", "z", "y")
PLANE = ("core", "z", "y")
TOP = 32766.0
MSG = 80
LIMIT = 16
PART = 8 * 128 + 16
ORDER = (2, 1, 3, 0)


def lines(along):
    groups = []
    for c in range(C):
        for fixed in range(4):
            on_z = (c ^ along) == 0
            groups.append([(c * Z + (i if on_z else fixed)) * Y + (fixed if on_z else i) for i in range(4)])
    return groups


LINE, CROSS = lines(0), lines(1)


def over(groups, v, step):
    return lax.ppermute(v, PLANE, [(group[i], group[(i + step) % 4]) for group in groups for i in range(4)])


def over_line(v, step):
    return over(LINE, v, step)


def over_cross(v, step):
    return over(CROSS, v, step)


def over_x(v, step):
    return lax.ppermute(v, "x", [(i, (i + step) % X) for i in range(X)])


def over_core(v):
    return lax.ppermute(v, "core", [(0, 1), (1, 0)])


def split_kernel(core, d_ref, i_ref, mine, theirs, flat, wide):
    lane32 = lax.broadcasted_iota(jnp.int32, (32, 128), 1)
    lane64 = lax.broadcasted_iota(jnp.int32, (64, 128), 1)

    def one(k, _):
        rows = d_ref[k].astype(jnp.float32)
        for p in range(32):
            flat[p * 8:(p + 1) * 8, :] = rows[:, p * 128:(p + 1) * 128]
        v = []
        for b in range(4):
            lo, hi = flat[pl.ds(b, 32, stride=8), :], flat[pl.ds(b + 4, 32, stride=8), :]
            wide[b, pl.ds(0, 32, stride=2), :] = jnp.where(lane32 < 64, lo, pltpu.roll(hi, 64, 1))
            wide[b, pl.ds(1, 32, stride=2), :] = jnp.where(lane32 < 64, pltpu.roll(lo, 64, 1), hi)
        v = [wide[b] for b in range(4)]
        for bit in (2, 1):
            keep = (lane64 & (16 * bit)) == 0
            w = [None] * 4
            for i in range(4):
                if not i & bit:
                    lo, hi = v[i], v[i | bit]
                    w[i] = jnp.where(keep, lo, pltpu.roll(hi, 16 * bit, 1))
                    w[i | bit] = jnp.where(keep, pltpu.roll(lo, 128 - 16 * bit, 1), hi)
            v = w
        first = jnp.concatenate([v[0], v[1]], axis=0).T
        second = jnp.concatenate([v[2], v[3]], axis=0).T
        swapped = core[0] == 1
        at = pl.ds(pl.multiple_of(k * 128, 128), 128)
        mine[at, :] = jnp.where(swapped, second, first).astype(jnp.bfloat16)
        theirs[at, :] = jnp.where(swapped, first, second).astype(jnp.bfloat16)
        return 0

    lax.fori_loop(0, 8, one, 0)
    ints = i_ref[...].astype(jnp.float32).astype(jnp.bfloat16)
    mine[8 * 128:, :] = ints
    theirs[8 * 128:, :] = ints


def split(core, dens, ints):
    half = jax.ShapeDtypeStruct((PART, 128), jnp.bfloat16)
    whole = pl.BlockSpec((PART, 128), lambda i, *_: (0, 0))
    return pl.pallas_call(
        split_kernel,
        grid_spec=pltpu.PrefetchScalarGridSpec(
            num_scalar_prefetch=1, grid=(1,),
            in_specs=[
                pl.BlockSpec((8, SP, B * B), lambda i, *_: (0, 0, 0)), pl.BlockSpec((16, 128), lambda i, *_: (0, 0))
            ],
            out_specs=[whole, whole],
            scratch_shapes=[pltpu.VMEM((256, 128), jnp.float32), pltpu.VMEM((4, B, 128), jnp.float32)],
        ),
        out_shape=[half, half],
        name="split",
    )(core, dens, ints)


def regroup_kernel(at, mine, other, own, ahead, back, sems):
    swapped, line, cross = at[0] == 1, at[1], at[2]
    copies = []
    for step in range(4):
        t = (line + step) % 4
        for i, rel in enumerate(ORDER):
            o = (cross + rel) % 4
            row = jnp.where(swapped, o * 4 + t, t * 4 + o)
            for m, src in enumerate((mine, other)):
                dst = (own.at[m, i], ahead.at[m, i], (ahead, back)[m].at[2, i], back.at[m, i])[step]
                copies.append(pltpu.make_async_copy(src.at[row], dst, sems.at[len(copies)]))
    for copy in copies:
        copy.start()
    for copy in copies:
        copy.wait()


def regroup(at, mine, other):
    shapes = [(2, 4, 4, 128, 128), (3, 4, 4, 128, 128), (3, 4, 4, 128, 128)]
    return pl.pallas_call(
        regroup_kernel,
        grid_spec=pltpu.PrefetchScalarGridSpec(
            num_scalar_prefetch=1, grid=(1,),
            in_specs=[pl.BlockSpec(memory_space=pl.ANY)] * 2,
            out_specs=[pl.BlockSpec(s, lambda i, *_: (0,) * 5, pipeline_mode=pl.Buffered(1)) for s in shapes],
            scratch_shapes=[pltpu.SemaphoreType.DMA((32,))],
        ),
        out_shape=[jax.ShapeDtypeStruct(shape, jnp.bfloat16) for shape in shapes],
        compiler_params=pltpu.CompilerParams(vmem_limit_bytes=12 << 20),
        name="regroup",
    )(at, mine, other)


def encode(values, put, write_code):
    top = jnp.zeros((16, 128), jnp.float32)
    for j in range(NCW):
        top = jnp.maximum(top, jnp.abs(values[j]))
    top = jnp.maximum(jnp.max(top, axis=0, keepdims=True), 2.0 ** -110)
    code = jnp.floor(jnp.log2(top) * 256.0) + 1.0
    scale = jnp.broadcast_to(jnp.exp2(code * (-1.0 / 256.0)) * TOP, (16, 128))
    write_code(jnp.broadcast_to(code.astype(jnp.int32), (16, 128)))
    for j in range(NCW):
        put(j, jnp.floor(values[j] * scale + 0.5).astype(jnp.int32).astype(jnp.int16))


def decoded_scale(code):
    return jnp.exp2(code.astype(jnp.int32).astype(jnp.float32) * (1.0 / 256.0)) * (1.0 / TOP)


def panel_kernel(n, pieces, halves, form, at, *refs):
    kohn, refs = refs[:2 * n], refs[2 * n:]
    panels, refs = refs[:pieces], refs[pieces:]
    if form != "first":
        sums_in, refs = refs[0], refs[1:]
    if form == "sent":
        received, refs = refs[:2], refs[2:]
    outs, (dens, sems, acc, in_sems, out_sems, staged, ints) = refs[:-7], refs[-7:]
    size = n * 8 * PART // pieces
    core, line, cross, x = at[0], at[1], at[2], at[3]

    loads = [pltpu.make_async_copy(panels[s], dens.at[pl.ds(s * size, size)], sems.at[s]) for s in range(pieces)]
    sums = []
    if form != "first":
        for h, (target, m) in enumerate(halves):
            src = sums_in.at[target, pl.ds(m * 4, 4)]
            sums.append(pltpu.make_async_copy(src, acc.at[h], in_sems.at[h]))
    stores = []
    if form in ("first", "more"):
        for h, (target, m) in enumerate(halves):
            dst = outs[0].at[target if len(halves) > 2 else 0, pl.ds(m * 4, 4)]
            stores.append(pltpu.make_async_copy(acc.at[h], dst, out_sems.at[h]))
    for copy in loads + sums:
        copy.start()
    for copy in loads:
        copy.wait()
    for s in range(n):
        rows = [dens[pl.ds((s * 8 + p) * PART + 8 * 128, 16), :].astype(jnp.float32) for p in range(8)]
        rows = [row[2:3] for row in rows] + [rows[0][0:2], rows[1][0:2], jnp.zeros((4, 128), jnp.float32)]
        staged[s * 16:(s + 1) * 16, :] = jnp.concatenate(rows, axis=0).astype(jnp.int32)
    copy = pltpu.make_async_copy(staged, ints, sems.at[pieces])
    copy.start()
    copy.wait()

    low = (lax.broadcasted_iota(jnp.int32, (32, 128), 1) < 64).astype(jnp.float32).astype(jnp.bfloat16)
    high = 1 - low

    def twice(blk):
        turned = jnp.concatenate([blk[:, B:], blk[:, :B]], axis=1)
        return jnp.concatenate([blk * low, turned * low, turned * high, blk * high], axis=0)

    def product(h, r, s, a):
        target, m = halves[h]
        goal = (cross + ORDER[target]) & 3
        place = jnp.where(core == 1, goal * 4 + line, line * 4 + goal)
        k = ints[s * 16 + 8 + m * 2 + (place >> 3), (place & 7) * 16 + r * 4 + a]
        slot = (120 >> (2 * (((k >> 4) - x) & 3))) & 3
        k = slot * 16 + ((k & 15) ^ (8 * core))
        part = s * 8 + (k >> 3)
        left = dens[pl.ds(pl.multiple_of(part * PART + (k & 7) * 128, 16), 128), :]
        ref, index = kohn[2 * s + m], target if kohn[2 * s + m].shape[1] == 4 else 0
        right = twice(ref[0, index, r, a * 32:(a + 1) * 32, :])
        r = lax.dot_general(left, right, (((1,), (1,)), ((), ())), preferred_element_type=jnp.float32)
        return s * 16 + (k >> 3), (k & 7) * SP, r

    def add(total, word, first, r):
        js = [ints[word, first + b] for b in range(SP)]
        old = [total[j] for j in js]
        for b in range(SP):
            total[js[b]] = old[b] + r[b * 16:(b + 1) * 16, :]

    def two_rows(h, pair):
        work, totals = [], []
        for q in range(2):
            r = pair * 2 + q
            work += [(q, r, s, a) for s in range(n) for a in range(SK)]
            total = acc.at[h, r]
            if form == "first":
                total[...] = jnp.zeros((NCW, 16, 128), jnp.float32)
            elif form == "sent":
                scale = decoded_scale(received[h][r, NCW])
                for j in range(NCW):
                    total[j] = total[j] + received[h][r, j].astype(jnp.int32).astype(jnp.float32) * scale
            totals.append(total)
        held = [product(h, *work[i][1:]) for i in range(3)]
        for i in range(len(work)):
            if i + 3 < len(work):
                held.append(product(h, *work[i + 3][1:]))
            add(totals[work[i][0]], *held[i])
        if form in ("coded", "sent"):
            for q in range(2):
                r = pair * 2 + q

                def put(j, value, r=r):
                    outs[h][r, j] = value

                encode(totals[q], put, lambda code, put=put: put(NCW, code.astype(jnp.int16)))

    for h in range(len(halves)):
        if sums:
            sums[h].wait()
        lax.fori_loop(0, 2, lambda pair, _, h=h: (two_rows(h, pair), 0)[1], 0)
        if stores:
            stores[h].start()
    for copy in stores:
        copy.wait()


def panel_sums(name, form, at, kohn, panels, halves, sums=None, received=(), us=4.0):
    n, pieces, groups = len(kohn) // 2, len(panels), len(halves)

    def k_spec(i, place):
        if groups > 2:
            return pl.BlockSpec((1, 4, 4, 128, 128), lambda *_: (place, 0, 0, 0, 0), pipeline_mode=pl.Buffered(1))
        target = {m: t for t, m in halves}[i % 2]
        return pl.BlockSpec((1, 1, 4, 128, 128), lambda *_: (place, target, 0, 0, 0), pipeline_mode=pl.Buffered(1))

    any_spec = pl.BlockSpec(memory_space=pl.ANY)
    sums_spec = pl.BlockSpec(memory_space=pltpu.HBM)
    coded = pl.BlockSpec((4, NCW + 1, 16, 128), lambda *_: (0, 0, 0, 0), pipeline_mode=pl.Buffered(1))
    if form in ("coded", "sent"):
        o_specs = [coded] * 2
        shapes = [jax.ShapeDtypeStruct((4, NCW + 1, 16, 128), jnp.int16)] * 2
    else:
        o_specs = [sums_spec if groups > 2 else any_spec]
        shapes = [jax.ShapeDtypeStruct((max(groups // 2, 1), 8, NCW, 16, 128), jnp.float32)]
    return pl.pallas_call(
        lambda *refs: panel_kernel(n, pieces, halves, form, *refs),
        grid_spec=pltpu.PrefetchScalarGridSpec(
            num_scalar_prefetch=1,
            grid=(1,),
            in_specs=(
                [k_spec(i, place) for i, (_, place) in enumerate(kohn)] + [any_spec] * pieces
                + ([] if sums is None else [sums_spec]) + [coded] * len(received)
            ),
            out_specs=o_specs,
            scratch_shapes=[
                pltpu.VMEM((n * 8 * PART, 128), jnp.bfloat16),
                pltpu.SemaphoreType.DMA((pieces + 1,)),
                pltpu.VMEM((groups, 4, NCW, 16, 128), jnp.float32),
                pltpu.SemaphoreType.DMA((groups,)),
                pltpu.SemaphoreType.DMA((groups,)),
                pltpu.VMEM((n * 16, 128), jnp.int32),
                pltpu.SMEM((n * 16, 128), jnp.int32),
            ],
        ),
        out_shape=shapes,
        compiler_params=pltpu.CompilerParams(vmem_limit_bytes=LIMIT << 20),
        cost_estimate=pl.CostEstimate(flops=int(us * 1.1e9), bytes_accessed=int(us * 2e6), transcendentals=0),
        name=name,
    )(at, *[array for array, _ in kohn], *panels, *([] if sums is None else [sums]), *received)


def pack_kernel(slots, own, prev0, prev1, next0, next1, o_ref, total, codes):
    rows = lax.broadcasted_iota(jnp.int32, (16, 128), 0)
    lane = lax.broadcasted_iota(jnp.int32, (16, 128), 1)

    def clear(n, _):
        for m in range(4):
            o_ref[n * 4 + m] = jnp.zeros((MSG, 128), jnp.int16)
            codes[n * 4 + m] = jnp.zeros((16, 128), jnp.int32)
        return 0

    lax.fori_loop(0, 32, clear, 0)

    def one(m, r):
        row = m * 4 + r
        coded = [((prev0, prev1)[m], r), ((next0, next1)[m], r)]
        scales = [decoded_scale(ref[at, NCW]) for ref, at in coded]
        for group in range(NCW // 8):
            blocks = []
            for j in range(group * 8, group * 8 + 8):
                g = [ref[at, j].astype(jnp.int32).astype(jnp.float32) * scale for (ref, at), scale in zip(coded, scales)]
                blocks.append(own[0, row, j] + g[0] + g[1])
            turned = jnp.concatenate(blocks, axis=0).T
            v = []
            for q in range(8):
                par, mh, zh = q // 4, (q // 2) % 2, q % 2
                at = (zh * 4 + par * 2 + mh) * 16
                v.append(turned[at:at + 16, :])
            for bit in (4, 2, 1):
                keep = (lane & (16 * bit)) == 0
                w = [None] * 8
                for i in range(8):
                    if not i & bit:
                        lo, hi = v[i], v[i | bit]
                        w[i] = jnp.where(keep, lo, pltpu.roll(hi, 16 * bit, 1))
                        w[i | bit] = jnp.where(keep, pltpu.roll(lo, 128 - 16 * bit, 1), hi)
                v = w
            for j in range(8):
                total[group * 8 + j] = v[j]

        def put(j, value):
            slot = slots[row * NCW + j]
            o_ref[slot // 4, pl.ds(pl.multiple_of((slot % 4) * 16, 16), 16), :] = value

        def write_code(code):
            for j in range(NCW):
                slot = slots[row * NCW + j]
                codes[slot // 4] = jnp.where(rows == slot % 4, code, codes[slot // 4])

        encode(total, put, write_code)

    for m in range(2):
        lax.fori_loop(0, 4, lambda r, _, m=m: (one(m, r), 0)[1], 0)

    def finish(n, _):
        for m in range(4):
            o_ref[n * 4 + m, 64:80, :] = codes[n * 4 + m].astype(jnp.int16)
        return 0

    lax.fori_loop(0, 32, finish, 0)


def pack(slots, *parts):
    def whole(array):
        return pl.BlockSpec(
            array.shape, lambda i, *_, n=array.ndim: (0,) * n, pipeline_mode=pl.Buffered(1)
        )

    return pl.pallas_call(
        pack_kernel,
        grid_spec=pltpu.PrefetchScalarGridSpec(
            num_scalar_prefetch=1,
            grid=(1,),
            in_specs=[whole(array) for array in parts],
            out_specs=pl.BlockSpec((128, MSG, 128), lambda i, *_: (0, 0, 0), pipeline_mode=pl.Buffered(1)),
            scratch_shapes=[pltpu.VMEM((NCW, 16, 128), jnp.float32), pltpu.VMEM((128, 16, 128), jnp.int32)],
        ),
        out_shape=jax.ShapeDtypeStruct((128, MSG, 128), jnp.int16),
        compiler_params=pltpu.CompilerParams(vmem_limit_bytes=32 << 20),
        name="pack",
    )(slots, *parts)


def unpack_kernel(r_ref, o_ref, full, scales):
    low32 = (lax.broadcasted_iota(jnp.int32, (16, 128), 1) & 32) == 0
    for n in range(16):
        for c in range(2):
            scales[n * 2 + c] = decoded_scale(r_ref[0, c, n, 64:80, :])[:8]

    def one(n, _):
        for s in range(2):
            for t in range(2):
                h = []
                for c in range(2):
                    at = (s * 2 + t) * 16
                    q = r_ref[0, c, n, at:at + 16, :].astype(jnp.int32).astype(jnp.float32)
                    h.append(q * scales[n * 2 + c, s * 2 + t:s * 2 + t + 1, :])
                base = pl.multiple_of(((s * 16 + n) * 2 + t) * 32, 32)
                full[pl.ds(base, 16), :] = jnp.where(low32, h[0], pltpu.roll(h[1], 32, 1))
                full[pl.ds(base + 16, 16), :] = jnp.where(low32, pltpu.roll(h[0], 96, 1), h[1])
        return 0

    lax.fori_loop(0, 16, one, 0, unroll=4)
    for p in range(32):
        o_ref[:, p * 128:(p + 1) * 128] = full[pl.ds(p, 64, stride=32), :]


def unpack(received):
    return pl.pallas_call(
        unpack_kernel,
        grid=(X,),
        in_specs=[pl.BlockSpec((1, C, 16, MSG, 128), lambda x: (x, 0, 0, 0, 0))],
        out_specs=pl.BlockSpec((64, 4096), lambda x: (x, 0)),
        out_shape=jax.ShapeDtypeStruct((256, 4096), jnp.float32),
        scratch_shapes=[pltpu.VMEM((64 * 32, 128), jnp.float32), pltpu.VMEM((32, 8, 128), jnp.float32)],
        compiler_params=pltpu.CompilerParams(vmem_limit_bytes=32 << 20),
        name="unpack",
    )(received)


def local(kohn_blocks, kohn_columns, density_blocks, density_columns, owner_map):
    x, c = lax.axis_index("x"), lax.axis_index("core")
    z, y = lax.axis_index("z"), lax.axis_index("y")
    on_line, on_cross = jnp.where(c == 0, z, y), jnp.where(c == 0, y, z)
    at = jnp.stack([c, on_line, on_cross, x])

    kohn = kohn_blocks.reshape(16, 4, SK * 32, 128)
    kohn_other = over_core(kohn)

    ints = jnp.concatenate([
        kohn_columns.reshape(2, 128), jnp.pad(density_columns.reshape(1, 64), ((0, 0), (0, 64))),
        owner_map.reshape(1, 128), jnp.zeros((12, 128), jnp.int32),
    ])
    dens, kohn = lax.optimization_barrier((density_blocks[0], kohn))

    mine, theirs = split(at, dens, ints)
    shard = jnp.concatenate([mine, over_core(theirs)])
    shard, kohn, kohn_other = lax.optimization_barrier((shard, kohn, kohn_other))
    left, right = over_x(shard, 1), over_x(shard, -1)

    kohn, ahead, back = regroup(at, kohn, kohn_other)
    kohn_prev, kohn_next = over_line(ahead, 1), over_line(back, -1)
    opposite0, opposite1 = over_line(kohn_prev[2:], 1), over_line(kohn_next[2:], -1)

    owners = jnp.stack([owner_map.reshape(128), shard[PART + 8 * 128 + 3].astype(jnp.int32)])
    hit = (owners[..., None] == jnp.arange(128, dtype=jnp.int32)).astype(jnp.int32)
    ranks = jnp.sum(jnp.cumsum(hit, axis=1) * hit, axis=2) - 1
    source = jnp.arange(2, dtype=jnp.int32)[:, None] ^ c
    slots = (owners * 4 + source * 2 + ranks).reshape(-1)

    low = jnp.concatenate([shard, left])
    high = jnp.concatenate([right, over_x(left[:PART], 1), over_x(right[PART:], -1)])
    low_sent, high_sent, kohn_prev, kohn_next, slots = lax.optimization_barrier((low, high, kohn_prev, kohn_next, slots))
    prev_low, next_high = over_line(low_sent, 1), over_line(high_sent, -1)
    prev_high, next_low = over_line(high_sent, 1), over_line(low_sent, -1)

    def both(array):
        return [(array, 0), (array, 1)]

    everything = tuple((target, m) for target in range(4) for m in range(2))
    sums, = panel_sums("own_panel", "first", at, both(kohn), [low, high], everything, us=9.0)
    prev_low, next_high, sums = lax.optimization_barrier((prev_low, next_high, sums))
    far_low, far_high = over_line(prev_low, 1), over_line(next_high, -1)
    sums, = panel_sums(
        "near_panels", "more", at, both(kohn_prev) + both(kohn_next), [prev_low, prev_high, next_low, next_high],
        everything, sums, us=16.0,
    )

    sums, opposite0, opposite1 = lax.optimization_barrier((sums, opposite0, opposite1))

    def last(form, halves, received=()):
        kohn = [(opposite0, 0), (opposite1, 0)]
        return panel_sums("last_" + form, form, at, kohn, [far_low, far_high], halves, sums, received)

    via_next, via_prev = last("coded", ((0, 0), (0, 1)))
    via_next, via_prev = over_cross(via_next, 1), over_cross(via_prev, -1)
    next1, prev0 = last("coded", ((1, 1), (2, 0)))
    prev_1, next_0 = over_cross(next1, 1), over_cross(prev0, -1)
    next0, prev1 = last("sent", ((1, 0), (2, 1)), (via_next, via_prev))
    prev_0, next_1 = over_cross(next0, 1), over_cross(prev1, -1)
    own, = last("more", ((3, 0), (3, 1)))

    outgoing = pack(slots, own, prev_0, prev_1, next_0, next_1)
    received = lax.all_to_all(outgoing, ALL, split_axis=0, concat_axis=0, tiled=True)
    return unpack(received.reshape(X, C, 16, MSG, 128))


def solution(mesh):
    grid = Mesh(mesh.devices.reshape(X, C, Z, Y), ALL)
    row, col = ("x", "core"), ("z", "y")
    return jax.shard_map(
        local,
        mesh=grid,
        in_specs=(
            P(row, col, None, None),
            P(row, col, None),
            P(col, row, None, None),
            P(col, row, None),
            P(ALL, None),
        ),
        out_specs=P(ALL, None),
        check_vma=False,
    )
```

```python
import jax
import jax.numpy as jnp
from jax import lax
from jax.experimental import pallas as pl
from jax.experimental.pallas import tpu as pltpu
from jax.sharding import Mesh, PartitionSpec as P

B = 64
HALF = 32
NCW = 32
SK = 4
SP = 8
X, C, Z, Y = 4, 2, 4, 4
ALL = ("x", "core", "z", "y")
PLANE = ("core", "z", "y")
TOP = 32766.0
MSG = 72
LIMIT = 16
PART = 8 * 128 + 16
ORDER = (2, 1, 3, 0)


def lines(along):
    groups = []
    for c in range(C):
        for fixed in range(4):
            on_z = (c ^ along) == 0
            groups.append([(c * Z + (i if on_z else fixed)) * Y + (fixed if on_z else i) for i in range(4)])
    return groups


LINE, CROSS = lines(0), lines(1)


def over(groups, v, step):
    return lax.ppermute(v, PLANE, [(group[i], group[(i + step) % 4]) for group in groups for i in range(4)])


def over_line(v, step):
    return over(LINE, v, step)


def over_cross(v, step):
    return over(CROSS, v, step)


def over_x(v, step):
    return lax.ppermute(v, "x", [(i, (i + step) % X) for i in range(X)])


def over_core(v):
    return lax.ppermute(v, "core", [(0, 1), (1, 0)])


def split_kernel(core, d_ref, i_ref, mine, theirs, flat0, wide0, flat1, wide1):
    lane32 = lax.broadcasted_iota(jnp.int32, (32, 128), 1)
    lane64 = lax.broadcasted_iota(jnp.int32, (64, 128), 1)

    def one(k, flat, wide):
        rows = d_ref[k].astype(jnp.float32)
        for p in range(32):
            flat[p * 8:(p + 1) * 8, :] = rows[:, p * 128:(p + 1) * 128]
        for b in range(4):
            lo, hi = flat[pl.ds(b, 32, stride=8), :], flat[pl.ds(b + 4, 32, stride=8), :]
            wide[b, pl.ds(0, 32, stride=2), :] = jnp.where(lane32 < 64, lo, pltpu.roll(hi, 64, 1))
            wide[b, pl.ds(1, 32, stride=2), :] = jnp.where(lane32 < 64, pltpu.roll(lo, 64, 1), hi)
        v = [wide[b] for b in range(4)]
        for bit in (2, 1):
            keep = (lane64 & (16 * bit)) == 0
            w = [None] * 4
            for i in range(4):
                if not i & bit:
                    lo, hi = v[i], v[i | bit]
                    w[i] = jnp.where(keep, lo, pltpu.roll(hi, 16 * bit, 1))
                    w[i | bit] = jnp.where(keep, pltpu.roll(lo, 128 - 16 * bit, 1), hi)
            v = w
        first = jnp.concatenate([v[0], v[1]], axis=0).T
        second = jnp.concatenate([v[2], v[3]], axis=0).T
        swapped = core[0] == 1
        at = pl.ds(pl.multiple_of(k * 128, 128), 128)
        mine[at, :] = jnp.where(swapped, second, first).astype(jnp.bfloat16)
        theirs[at, :] = jnp.where(swapped, first, second).astype(jnp.bfloat16)

    def two(i, _):
        one(i * 2, flat0, wide0)
        one(i * 2 + 1, flat1, wide1)
        return 0

    lax.fori_loop(0, 4, two, 0)
    ints = i_ref[...].astype(jnp.float32).astype(jnp.bfloat16)
    mine[8 * 128:, :] = ints
    theirs[8 * 128:, :] = ints


def split(core, dens, ints):
    half = jax.ShapeDtypeStruct((PART, 128), jnp.bfloat16)
    whole = pl.BlockSpec((PART, 128), lambda i, *_: (0, 0))
    return pl.pallas_call(
        split_kernel,
        grid_spec=pltpu.PrefetchScalarGridSpec(
            num_scalar_prefetch=1, grid=(1,),
            in_specs=[
                pl.BlockSpec((8, SP, B * B), lambda i, *_: (0, 0, 0)), pl.BlockSpec((16, 128), lambda i, *_: (0, 0))
            ],
            out_specs=[whole, whole],
            scratch_shapes=[pltpu.VMEM((256, 128), jnp.float32), pltpu.VMEM((4, B, 128), jnp.float32)] * 2,
        ),
        out_shape=[half, half],
        name="split",
    )(core, dens, ints)


def regroup_kernel(at, mine, other, own, ahead, back, sems):
    swapped, line, cross = at[0] == 1, at[1], at[2]
    copies = []
    for step in range(4):
        t = (line + step) % 4
        for i, rel in enumerate(ORDER):
            o = (cross + rel) % 4
            row = jnp.where(swapped, o * 4 + t, t * 4 + o)
            for m, src in enumerate((mine, other)):
                dst = (own.at[m, i], ahead.at[m, i], (ahead, back)[m].at[2, i], back.at[m, i])[step]
                copies.append(pltpu.make_async_copy(src.at[row], dst, sems.at[len(copies)]))
    for copy in copies:
        copy.start()
    for copy in copies:
        copy.wait()


def regroup(at, mine, other):
    shapes = [(2, 4, 4, 128, 128), (3, 4, 4, 128, 128), (3, 4, 4, 128, 128)]
    return pl.pallas_call(
        regroup_kernel,
        grid_spec=pltpu.PrefetchScalarGridSpec(
            num_scalar_prefetch=1, grid=(1,),
            in_specs=[pl.BlockSpec(memory_space=pl.ANY)] * 2,
            out_specs=[pl.BlockSpec(s, lambda i, *_: (0,) * 5, pipeline_mode=pl.Buffered(1)) for s in shapes],
            scratch_shapes=[pltpu.SemaphoreType.DMA((32,))],
        ),
        out_shape=[jax.ShapeDtypeStruct(shape, jnp.bfloat16) for shape in shapes],
        compiler_params=pltpu.CompilerParams(vmem_limit_bytes=12 << 20),
        name="regroup",
    )(at, mine, other)


def encode(values, put, write_code):
    top = jnp.zeros((16, 128), jnp.float32)
    for j in range(NCW):
        top = jnp.maximum(top, jnp.abs(values[j]))
    top = jnp.maximum(jnp.max(top, axis=0, keepdims=True), 2.0 ** -110)
    code = jnp.floor(jnp.log2(top) * 256.0) + 1.0
    scale = jnp.broadcast_to(jnp.exp2(code * (-1.0 / 256.0)) * TOP, (16, 128))
    write_code(jnp.broadcast_to(code.astype(jnp.int32), (16, 128)))
    for j in range(NCW):
        put(j, jnp.floor(values[j] * scale + 0.5).astype(jnp.int32).astype(jnp.int16))


def decoded_scale(code):
    return jnp.exp2(code.astype(jnp.int32).astype(jnp.float32) * (1.0 / 256.0)) * (1.0 / TOP)


def panel_kernel(n, pieces, halves, form, at, *refs):
    kohn, refs = refs[:2 * n], refs[2 * n:]
    panels, refs = refs[:pieces], refs[pieces:]
    if form != "first":
        sums_in, refs = refs[0], refs[1:]
    received = ()
    if form in ("sent", "own"):
        received, refs = refs[:2], refs[2:]
    outs, (dens, sems, acc, in_sems, out_sems, staged, ints) = refs[:-7], refs[-7:]
    size = n * 8 * PART // pieces
    core, line, cross, x = at[0], at[1], at[2], at[3]

    loads = [pltpu.make_async_copy(panels[s], dens.at[pl.ds(s * size, size)], sems.at[s]) for s in range(pieces)]
    sums = []
    if form != "first":
        for h, (target, m) in enumerate(halves):
            src = sums_in.at[target, pl.ds(m * 4, 4)]
            sums.append(pltpu.make_async_copy(src, acc.at[h], in_sems.at[h]))
    stores = []
    if form in ("first", "more", "own"):
        for h, (target, m) in enumerate(halves):
            dst = outs[0].at[target if len(halves) > 2 else 0, pl.ds(m * 4, 4)]
            stores.append(pltpu.make_async_copy(acc.at[h], dst, out_sems.at[h]))
    for copy in loads + sums:
        copy.start()
    for copy in loads:
        copy.wait()
    for s in range(n):
        rows = [dens[pl.ds((s * 8 + p) * PART + 8 * 128, 16), :].astype(jnp.float32) for p in range(8)]
        rows = [row[2:3] for row in rows] + [rows[0][0:2], rows[1][0:2], jnp.zeros((4, 128), jnp.float32)]
        staged[s * 16:(s + 1) * 16, :] = jnp.concatenate(rows, axis=0).astype(jnp.int32)
    copy = pltpu.make_async_copy(staged, ints, sems.at[pieces])
    copy.start()
    copy.wait()

    low = (lax.broadcasted_iota(jnp.int32, (32, 128), 1) < 64).astype(jnp.float32).astype(jnp.bfloat16)
    high = 1 - low

    def twice(blk):
        turned = jnp.concatenate([blk[:, B:], blk[:, :B]], axis=1)
        return jnp.concatenate([blk * low, turned * low, turned * high, blk * high], axis=0)

    def product(h, r, s, a):
        target, m = halves[h]
        goal = (cross + ORDER[target]) & 3
        place = jnp.where(core == 1, goal * 4 + line, line * 4 + goal)
        k = ints[s * 16 + 8 + m * 2 + (place >> 3), (place & 7) * 16 + r * 4 + a]
        slot = (120 >> (2 * (((k >> 4) - x) & 3))) & 3
        k = slot * 16 + ((k & 15) ^ (8 * core))
        part = s * 8 + (k >> 3)
        left = dens[pl.ds(pl.multiple_of(part * PART + (k & 7) * 128, 16), 128), :]
        ref, index = kohn[2 * s + m], target if kohn[2 * s + m].shape[1] == 4 else 0
        right = twice(ref[0, index, r, a * 32:(a + 1) * 32, :])
        r = lax.dot_general(left, right, (((1,), (1,)), ((), ())), preferred_element_type=jnp.float32)
        return s * 16 + (k >> 3), (k & 7) * SP, r

    def add(total, word, first, r):
        js = [ints[word, first + b] for b in range(SP)]
        old = [total[j] for j in js]
        for b in range(SP):
            total[js[b]] = old[b] + r[b * 16:(b + 1) * 16, :]

    def two_rows(h, pair):
        work, totals = [], []
        for q in range(2):
            r = pair * 2 + q
            work += [(q, r, s, a) for s in range(n) for a in range(SK)]
            total = acc.at[h, r]
            if form == "first":
                total[...] = jnp.zeros((NCW, 16, 128), jnp.float32)
            elif received:
                scale = decoded_scale(received[h][r, NCW])
                for j in range(NCW):
                    total[j] = total[j] + received[h][r, j].astype(jnp.int32).astype(jnp.float32) * scale
            totals.append(total)
        held = [product(h, *work[i][1:]) for i in range(3)]
        for i in range(len(work)):
            if i + 3 < len(work):
                held.append(product(h, *work[i + 3][1:]))
            add(totals[work[i][0]], *held[i])
        if form in ("coded", "sent"):
            for q in range(2):
                r = pair * 2 + q

                def put(j, value, r=r):
                    outs[h][r, j] = value

                encode(totals[q], put, lambda code, put=put: put(NCW, code.astype(jnp.int16)))

    for h in range(len(halves)):
        if sums:
            sums[h].wait()
        lax.fori_loop(0, 2, lambda pair, _, h=h: (two_rows(h, pair), 0)[1], 0)
        if stores:
            stores[h].start()
    for copy in stores:
        copy.wait()


def panel_sums(name, form, at, kohn, panels, halves, sums=None, received=(), us=4.0):
    n, pieces, groups = len(kohn) // 2, len(panels), len(halves)

    def k_spec(i, place):
        if groups > 2:
            return pl.BlockSpec((1, 4, 4, 128, 128), lambda *_: (place, 0, 0, 0, 0), pipeline_mode=pl.Buffered(1))
        target = {m: t for t, m in halves}[i % 2]
        return pl.BlockSpec((1, 1, 4, 128, 128), lambda *_: (place, target, 0, 0, 0), pipeline_mode=pl.Buffered(1))

    any_spec = pl.BlockSpec(memory_space=pl.ANY)
    sums_spec = pl.BlockSpec(memory_space=pltpu.HBM)
    coded = pl.BlockSpec((4, NCW + 1, 16, 128), lambda *_: (0, 0, 0, 0), pipeline_mode=pl.Buffered(1))
    if form in ("coded", "sent"):
        o_specs = [coded] * 2
        shapes = [jax.ShapeDtypeStruct((4, NCW + 1, 16, 128), jnp.int16)] * 2
    else:
        o_specs = [sums_spec if groups > 2 else any_spec]
        shapes = [jax.ShapeDtypeStruct((max(groups // 2, 1), 8, NCW, 16, 128), jnp.float32)]
    return pl.pallas_call(
        lambda *refs: panel_kernel(n, pieces, halves, form, *refs),
        grid_spec=pltpu.PrefetchScalarGridSpec(
            num_scalar_prefetch=1,
            grid=(1,),
            in_specs=(
                [k_spec(i, place) for i, (_, place) in enumerate(kohn)] + [any_spec] * pieces
                + ([] if sums is None else [sums_spec]) + [coded] * len(received)
            ),
            out_specs=o_specs,
            scratch_shapes=[
                pltpu.VMEM((n * 8 * PART, 128), jnp.bfloat16),
                pltpu.SemaphoreType.DMA((pieces + 1,)),
                pltpu.VMEM((groups, 4, NCW, 16, 128), jnp.float32),
                pltpu.SemaphoreType.DMA((groups,)),
                pltpu.SemaphoreType.DMA((groups,)),
                pltpu.VMEM((n * 16, 128), jnp.int32),
                pltpu.SMEM((n * 16, 128), jnp.int32),
            ],
        ),
        out_shape=shapes,
        compiler_params=pltpu.CompilerParams(vmem_limit_bytes=LIMIT << 20),
        cost_estimate=pl.CostEstimate(flops=int(us * 1.1e9), bytes_accessed=int(us * 2e6), transcendentals=0),
        name=name,
    )(at, *[array for array, _ in kohn], *panels, *([] if sums is None else [sums]), *received)


def pack_kernel(slots, own, prev0, next1, o_ref, total, codes):
    rows = lax.broadcasted_iota(jnp.int32, (8, 128), 0)
    lane = lax.broadcasted_iota(jnp.int32, (16, 128), 1)

    def clear(n, _):
        for m in range(4):
            o_ref[n * 4 + m] = jnp.zeros((MSG, 128), jnp.int16)
            codes[n * 4 + m] = jnp.zeros((8, 128), jnp.int32)
        return 0

    lax.fori_loop(0, 32, clear, 0)

    def one(m, r):
        row = m * 4 + r
        coded = (prev0, next1)[m]
        scale = decoded_scale(coded[r, NCW])
        for group in range(NCW // 8):
            blocks = []
            for j in range(group * 8, group * 8 + 8):
                blocks.append(own[0, row, j] + coded[r, j].astype(jnp.int32).astype(jnp.float32) * scale)
            turned = jnp.concatenate(blocks, axis=0).T
            v = []
            for q in range(8):
                par, mh, zh = q // 4, (q // 2) % 2, q % 2
                at = (zh * 4 + par * 2 + mh) * 16
                v.append(turned[at:at + 16, :])
            for bit in (4, 2, 1):
                keep = (lane & (16 * bit)) == 0
                w = [None] * 8
                for i in range(8):
                    if not i & bit:
                        lo, hi = v[i], v[i | bit]
                        w[i] = jnp.where(keep, lo, pltpu.roll(hi, 16 * bit, 1))
                        w[i | bit] = jnp.where(keep, pltpu.roll(lo, 128 - 16 * bit, 1), hi)
                v = w
            for j in range(8):
                total[group * 8 + j] = v[j]

        def put(j, value):
            slot = slots[row * NCW + j]
            o_ref[slot // 4, pl.ds(pl.multiple_of((slot % 4) * 16, 16), 16), :] = value

        def write_code(code):
            for j in range(NCW):
                slot = slots[row * NCW + j]
                codes[slot // 4] = jnp.where(rows == slot % 4, code[:8], codes[slot // 4])

        encode(total, put, write_code)

    for m in range(2):
        lax.fori_loop(0, 4, lambda r, _, m=m: (one(m, r), 0)[1], 0)

    def finish(n, _):
        for m in range(4):
            o_ref[n * 4 + m, 64:72, :] = codes[n * 4 + m].astype(jnp.int16)
        return 0

    lax.fori_loop(0, 32, finish, 0)


def pack(slots, *parts):
    def whole(array):
        return pl.BlockSpec(
            array.shape, lambda i, *_, n=array.ndim: (0,) * n, pipeline_mode=pl.Buffered(1)
        )

    return pl.pallas_call(
        pack_kernel,
        grid_spec=pltpu.PrefetchScalarGridSpec(
            num_scalar_prefetch=1,
            grid=(1,),
            in_specs=[whole(array) for array in parts],
            out_specs=pl.BlockSpec((128, MSG, 128), lambda i, *_: (0, 0, 0), pipeline_mode=pl.Buffered(1)),
            scratch_shapes=[pltpu.VMEM((NCW, 16, 128), jnp.float32), pltpu.VMEM((128, 8, 128), jnp.int32)],
        ),
        out_shape=jax.ShapeDtypeStruct((128, MSG, 128), jnp.int16),
        compiler_params=pltpu.CompilerParams(vmem_limit_bytes=32 << 20),
        name="pack",
    )(slots, *parts)


def unpack_kernel(r_ref, o_ref, full, scales):
    low32 = (lax.broadcasted_iota(jnp.int32, (16, 128), 1) & 32) == 0
    for n in range(16):
        for c in range(2):
            scales[n * 2 + c] = decoded_scale(r_ref[0, c, n, 64:72, :])

    def one(n, _):
        for s in range(2):
            for t in range(2):
                h = []
                for c in range(2):
                    at = (s * 2 + t) * 16
                    q = r_ref[0, c, n, at:at + 16, :].astype(jnp.int32).astype(jnp.float32)
                    h.append(q * scales[n * 2 + c, s * 2 + t:s * 2 + t + 1, :])
                base = pl.multiple_of(((s * 16 + n) * 2 + t) * 32, 32)
                full[pl.ds(base, 16), :] = jnp.where(low32, h[0], pltpu.roll(h[1], 32, 1))
                full[pl.ds(base + 16, 16), :] = jnp.where(low32, pltpu.roll(h[0], 96, 1), h[1])
        return 0

    lax.fori_loop(0, 16, one, 0, unroll=4)
    for p in range(32):
        o_ref[:, p * 128:(p + 1) * 128] = full[pl.ds(p, 64, stride=32), :]


def unpack(received):
    return pl.pallas_call(
        unpack_kernel,
        grid=(X,),
        in_specs=[pl.BlockSpec((1, C, 16, MSG, 128), lambda x: (x, 0, 0, 0, 0))],
        out_specs=pl.BlockSpec((64, 4096), lambda x: (x, 0)),
        out_shape=jax.ShapeDtypeStruct((256, 4096), jnp.float32),
        scratch_shapes=[pltpu.VMEM((64 * 32, 128), jnp.float32), pltpu.VMEM((32, 8, 128), jnp.float32)],
        compiler_params=pltpu.CompilerParams(vmem_limit_bytes=32 << 20),
        name="unpack",
    )(received)


def local(kohn_blocks, kohn_columns, density_blocks, density_columns, owner_map):
    x, c = lax.axis_index("x"), lax.axis_index("core")
    z, y = lax.axis_index("z"), lax.axis_index("y")
    on_line, on_cross = jnp.where(c == 0, z, y), jnp.where(c == 0, y, z)
    at = jnp.stack([c, on_line, on_cross, x])

    kohn = kohn_blocks.reshape(16, 4, SK * 32, 128)
    kohn_other = over_core(kohn)

    ints = jnp.concatenate([
        kohn_columns.reshape(2, 128), jnp.pad(density_columns.reshape(1, 64), ((0, 0), (0, 64))),
        owner_map.reshape(1, 128), jnp.zeros((12, 128), jnp.int32),
    ])
    dens, kohn = lax.optimization_barrier((density_blocks[0], kohn))

    mine, theirs = split(at, dens, ints)
    shard = jnp.concatenate([mine, over_core(theirs)])
    shard, kohn, kohn_other = lax.optimization_barrier((shard, kohn, kohn_other))
    left, right = over_x(shard, 1), over_x(shard, -1)

    kohn, ahead, back = regroup(at, kohn, kohn_other)
    kohn_prev, kohn_next = over_line(ahead, 1), over_line(back, -1)
    opposite0, opposite1 = over_line(kohn_prev[2:], 1), over_line(kohn_next[2:], -1)

    owners = jnp.stack([owner_map.reshape(128), shard[PART + 8 * 128 + 3].astype(jnp.int32)])
    hit = (owners[..., None] == jnp.arange(128, dtype=jnp.int32)).astype(jnp.int32)
    ranks = jnp.sum(jnp.cumsum(hit, axis=1) * hit, axis=2) - 1
    source = jnp.arange(2, dtype=jnp.int32)[:, None] ^ c
    slots = (owners * 4 + source * 2 + ranks).reshape(-1)

    low = jnp.concatenate([shard, left])
    high = jnp.concatenate([right, over_x(left[:PART], 1), over_x(right[PART:], -1)])
    low_sent, high_sent, kohn_prev, kohn_next, slots = lax.optimization_barrier((low, high, kohn_prev, kohn_next, slots))
    prev_low, next_high = over_line(low, 1), over_line(high, -1)
    prev_high, next_low = over_line(high_sent, 1), over_line(low_sent, -1)

    def both(array):
        return [(array, 0), (array, 1)]

    everything = tuple((target, m) for target in range(4) for m in range(2))
    sums, = panel_sums("own_panel", "first", at, both(kohn), [low, high], everything, us=9.0)
    prev_low, next_high, sums = lax.optimization_barrier((prev_low, next_high, sums))
    far_low, far_high = over_line(prev_low, 1), over_line(next_high, -1)
    sums, = panel_sums(
        "near_panels", "more", at, both(kohn_prev) + both(kohn_next), [prev_low, prev_high, next_low, next_high],
        everything, sums, us=16.0,
    )

    sums, opposite0, opposite1 = lax.optimization_barrier((sums, opposite0, opposite1))

    def last(form, halves, received=()):
        kohn = [(opposite0, 0), (opposite1, 0)]
        return panel_sums("last_" + form, form, at, kohn, [far_low, far_high], halves, sums, received)

    via_next, via_prev = last("coded", ((0, 0), (0, 1)))
    via_next, via_prev = over_cross(via_next, 1), over_cross(via_prev, -1)
    next1, prev0 = last("coded", ((1, 1), (2, 0)))
    prev_1, next_0 = over_cross(next1, 1), over_cross(prev0, -1)
    next0, prev1 = last("sent", ((1, 0), (2, 1)), (via_next, via_prev))
    prev_0, next_1 = over_cross(next0, 1), over_cross(prev1, -1)
    own, = last("own", ((3, 0), (3, 1)), (next_0, prev_1))

    outgoing = pack(slots, own, prev_0, next_1)
    received = lax.all_to_all(outgoing, ALL, split_axis=0, concat_axis=0, tiled=True)
    return unpack(received.reshape(X, C, 16, MSG, 128))


def solution(mesh):
    grid = Mesh(mesh.devices.reshape(X, C, Z, Y), ALL)
    row, col = ("x", "core"), ("z", "y")
    return jax.shard_map(
        local,
        mesh=grid,
        in_specs=(
            P(row, col, None, None),
            P(row, col, None),
            P(col, row, None, None),
            P(col, row, None),
            P(ALL, None),
        ),
        out_specs=P(ALL, None),
        check_vma=False,
    )
```

```python
import jax
import jax.numpy as jnp
from jax import lax
from jax.experimental import pallas as pl
from jax.experimental.pallas import tpu as pltpu
from jax.sharding import Mesh, PartitionSpec as P

B = 64
HALF = 32
NCW = 32
SK = 4
SP = 8
X, C, Z, Y = 4, 2, 4, 4
ALL = ("x", "core", "z", "y")
PLANE = ("core", "z", "y")
TOP = 32766.0
MSG = 72
LIMIT = 16
PART = 8 * 128 + 16
ORDER = (2, 1, 3, 0)


def lines(along):
    groups = []
    for c in range(C):
        for fixed in range(4):
            on_z = (c ^ along) == 0
            groups.append([(c * Z + (i if on_z else fixed)) * Y + (fixed if on_z else i) for i in range(4)])
    return groups


LINE, CROSS = lines(0), lines(1)


def over(groups, v, step):
    return lax.ppermute(v, PLANE, [(group[i], group[(i + step) % 4]) for group in groups for i in range(4)])


def over_line(v, step):
    return over(LINE, v, step)


def over_cross(v, step):
    return over(CROSS, v, step)


def over_x(v, step):
    return lax.ppermute(v, "x", [(i, (i + step) % X) for i in range(X)])


def over_core(v):
    return lax.ppermute(v, "core", [(0, 1), (1, 0)])


def split_kernel(core, d_ref, i_ref, mine, theirs, flat0, wide0, flat1, wide1):
    lane32 = lax.broadcasted_iota(jnp.int32, (32, 128), 1)
    lane64 = lax.broadcasted_iota(jnp.int32, (64, 128), 1)

    def one(k, flat, wide):
        rows = d_ref[k].astype(jnp.float32)
        for p in range(32):
            flat[p * 8:(p + 1) * 8, :] = rows[:, p * 128:(p + 1) * 128]
        for b in range(4):
            lo, hi = flat[pl.ds(b, 32, stride=8), :], flat[pl.ds(b + 4, 32, stride=8), :]
            wide[b, pl.ds(0, 32, stride=2), :] = jnp.where(lane32 < 64, lo, pltpu.roll(hi, 64, 1))
            wide[b, pl.ds(1, 32, stride=2), :] = jnp.where(lane32 < 64, pltpu.roll(lo, 64, 1), hi)
        v = [wide[b] for b in range(4)]
        for bit in (2, 1):
            keep = (lane64 & (16 * bit)) == 0
            w = [None] * 4
            for i in range(4):
                if not i & bit:
                    lo, hi = v[i], v[i | bit]
                    w[i] = jnp.where(keep, lo, pltpu.roll(hi, 16 * bit, 1))
                    w[i | bit] = jnp.where(keep, pltpu.roll(lo, 128 - 16 * bit, 1), hi)
            v = w
        first = jnp.concatenate([v[0], v[1]], axis=0).T
        second = jnp.concatenate([v[2], v[3]], axis=0).T
        swapped = core[0] == 1
        at = pl.ds(pl.multiple_of(k * 128, 128), 128)
        mine[at, :] = jnp.where(swapped, second, first).astype(jnp.bfloat16)
        theirs[at, :] = jnp.where(swapped, first, second).astype(jnp.bfloat16)

    def two(i, _):
        one(i * 2, flat0, wide0)
        one(i * 2 + 1, flat1, wide1)
        return 0

    lax.fori_loop(0, 4, two, 0)
    ints = i_ref[...].astype(jnp.float32).astype(jnp.bfloat16)
    mine[8 * 128:, :] = ints
    theirs[8 * 128:, :] = ints


def split(core, dens, ints):
    half = jax.ShapeDtypeStruct((PART, 128), jnp.bfloat16)
    whole = pl.BlockSpec((PART, 128), lambda i, *_: (0, 0))
    return pl.pallas_call(
        split_kernel,
        grid_spec=pltpu.PrefetchScalarGridSpec(
            num_scalar_prefetch=1, grid=(1,),
            in_specs=[
                pl.BlockSpec((8, SP, B * B), lambda i, *_: (0, 0, 0)), pl.BlockSpec((16, 128), lambda i, *_: (0, 0))
            ],
            out_specs=[whole, whole],
            scratch_shapes=[pltpu.VMEM((256, 128), jnp.float32), pltpu.VMEM((4, B, 128), jnp.float32)] * 2,
        ),
        out_shape=[half, half],
        name="split",
    )(core, dens, ints)


def regroup_kernel(at, mine, other, own, ahead, back, sems):
    swapped, line, cross = at[0] == 1, at[1], at[2]
    copies = []
    for step in range(4):
        t = (line + step) % 4
        for i, rel in enumerate(ORDER):
            o = (cross + rel) % 4
            row = jnp.where(swapped, o * 4 + t, t * 4 + o)
            for m, src in enumerate((mine, other)):
                dst = (own.at[m, i], ahead.at[m, i], (ahead, back)[m].at[2, i], back.at[m, i])[step]
                copies.append(pltpu.make_async_copy(src.at[row], dst, sems.at[len(copies)]))
    for copy in copies:
        copy.start()
    for copy in copies:
        copy.wait()


def regroup(at, mine, other):
    shapes = [(2, 4, 4, 128, 128), (3, 4, 4, 128, 128), (3, 4, 4, 128, 128)]
    return pl.pallas_call(
        regroup_kernel,
        grid_spec=pltpu.PrefetchScalarGridSpec(
            num_scalar_prefetch=1, grid=(1,),
            in_specs=[pl.BlockSpec(memory_space=pl.ANY)] * 2,
            out_specs=[pl.BlockSpec(s, lambda i, *_: (0,) * 5, pipeline_mode=pl.Buffered(1)) for s in shapes],
            scratch_shapes=[pltpu.SemaphoreType.DMA((32,))],
        ),
        out_shape=[jax.ShapeDtypeStruct(shape, jnp.bfloat16) for shape in shapes],
        compiler_params=pltpu.CompilerParams(vmem_limit_bytes=12 << 20),
        name="regroup",
    )(at, mine, other)


def encode(values, put, write_code):
    top = jnp.zeros((16, 128), jnp.float32)
    for j in range(NCW):
        top = jnp.maximum(top, jnp.abs(values[j]))
    top = jnp.maximum(jnp.max(top, axis=0, keepdims=True), 2.0 ** -110)
    code = jnp.floor(jnp.log2(top) * 256.0) + 1.0
    scale = jnp.broadcast_to(jnp.exp2(code * (-1.0 / 256.0)) * TOP, (16, 128))
    write_code(jnp.broadcast_to(code.astype(jnp.int32), (16, 128)))
    for j in range(NCW):
        put(j, jnp.floor(values[j] * scale + 0.5).astype(jnp.int32).astype(jnp.int16))


def decoded_scale(code):
    return jnp.exp2(code.astype(jnp.int32).astype(jnp.float32) * (1.0 / 256.0)) * (1.0 / TOP)


def panel_kernel(n, pieces, halves, form, at, *refs):
    kohn, refs = refs[:2 * n], refs[2 * n:]
    panels, refs = refs[:pieces], refs[pieces:]
    if form != "first":
        sums_in, refs = refs[0], refs[1:]
    received = ()
    if form in ("sent", "own"):
        received, refs = refs[:2], refs[2:]
    outs, (dens, sems, acc0, acc1, in_sems, out_sems, staged, ints) = refs[:-8], refs[-8:]
    accs = (acc0, acc1)
    size = n * 8 * PART // pieces
    core, line, cross, x = at[0], at[1], at[2], at[3]

    loads = [pltpu.make_async_copy(panels[s], dens.at[pl.ds(s * size, size)], sems.at[s]) for s in range(pieces)]
    sums = []
    if form != "first":
        for h, (target, m) in enumerate(halves):
            for q in range(2):
                src = sums_in.at[target, pl.ds(m * 4 + q * 2, 2)]
                sums.append(pltpu.make_async_copy(src, accs[q].at[h], in_sems.at[h * 2 + q]))
    stores = []
    if form in ("first", "more", "own"):
        for h, (target, m) in enumerate(halves):
            for q in range(2):
                dst = outs[0].at[target if len(halves) > 2 else 0, pl.ds(m * 4 + q * 2, 2)]
                stores.append(pltpu.make_async_copy(accs[q].at[h], dst, out_sems.at[h * 2 + q]))
    for copy in loads + sums:
        copy.start()
    for copy in loads:
        copy.wait()
    for s in range(n):
        rows = [dens[pl.ds((s * 8 + p) * PART + 8 * 128, 16), :].astype(jnp.float32) for p in range(8)]
        rows = [row[2:3] for row in rows] + [rows[0][0:2], rows[1][0:2], jnp.zeros((4, 128), jnp.float32)]
        staged[s * 16:(s + 1) * 16, :] = jnp.concatenate(rows, axis=0).astype(jnp.int32)
    copy = pltpu.make_async_copy(staged, ints, sems.at[pieces])
    copy.start()
    copy.wait()

    low = (lax.broadcasted_iota(jnp.int32, (32, 128), 1) < 64).astype(jnp.float32).astype(jnp.bfloat16)
    high = 1 - low

    def twice(blk):
        turned = jnp.concatenate([blk[:, B:], blk[:, :B]], axis=1)
        return jnp.concatenate([blk * low, turned * low, turned * high, blk * high], axis=0)

    def product(h, r, s, a):
        target, m = halves[h]
        goal = (cross + ORDER[target]) & 3
        place = jnp.where(core == 1, goal * 4 + line, line * 4 + goal)
        k = ints[s * 16 + 8 + m * 2 + (place >> 3), (place & 7) * 16 + r * 4 + a]
        slot = (120 >> (2 * (((k >> 4) - x) & 3))) & 3
        k = slot * 16 + ((k & 15) ^ (8 * core))
        part = s * 8 + (k >> 3)
        left = dens[pl.ds(pl.multiple_of(part * PART + (k & 7) * 128, 16), 128), :]
        ref, index = kohn[2 * s + m], target if kohn[2 * s + m].shape[1] == 4 else 0
        right = twice(ref[0, index, r, a * 32:(a + 1) * 32, :])
        r = lax.dot_general(left, right, (((1,), (1,)), ((), ())), preferred_element_type=jnp.float32)
        return s * 16 + (k >> 3), (k & 7) * SP, r

    def add(total, word, first, r):
        js = [ints[word, first + b] for b in range(SP)]
        old = [total[j] for j in js]
        for b in range(SP):
            total[js[b]] = old[b] + r[b * 16:(b + 1) * 16, :]

    def two_rows(h, pair):
        totals = []
        work = [(q, q * 2 + pair, s, a) for s in range(n) for a in range(SK) for q in range(2)]
        for q in range(2):
            r = q * 2 + pair
            total = accs[q].at[h, pair]
            if form == "first":
                total[...] = jnp.zeros((NCW, 16, 128), jnp.float32)
            elif received:
                scale = decoded_scale(received[h][r, NCW])
                for j in range(NCW):
                    total[j] = total[j] + received[h][r, j].astype(jnp.int32).astype(jnp.float32) * scale
            totals.append(total)
        held = [product(h, *work[i][1:]) for i in range(4)]
        for i in range(len(work)):
            if i + 4 < len(work):
                held.append(product(h, *work[i + 4][1:]))
            add(totals[work[i][0]], *held[i])
        if form in ("coded", "sent"):
            for q in range(2):
                r = q * 2 + pair

                def put(j, value, r=r):
                    outs[h][r, j] = value

                encode(totals[q], put, lambda code, put=put: put(NCW, code.astype(jnp.int16)))

    for h in range(len(halves)):
        for copy in sums[2 * h:2 * h + 2]:
            copy.wait()
        lax.fori_loop(0, 2, lambda pair, _, h=h: (two_rows(h, pair), 0)[1], 0)
        for copy in stores[2 * h:2 * h + 2]:
            copy.start()
    for copy in stores:
        copy.wait()


def panel_sums(name, form, at, kohn, panels, halves, sums=None, received=(), us=4.0):
    n, pieces, groups = len(kohn) // 2, len(panels), len(halves)

    def k_spec(i, place):
        if groups > 2:
            return pl.BlockSpec((1, 4, 4, 128, 128), lambda *_: (place, 0, 0, 0, 0), pipeline_mode=pl.Buffered(1))
        target = {m: t for t, m in halves}[i % 2]
        return pl.BlockSpec((1, 1, 4, 128, 128), lambda *_: (place, target, 0, 0, 0), pipeline_mode=pl.Buffered(1))

    any_spec = pl.BlockSpec(memory_space=pl.ANY)
    sums_spec = pl.BlockSpec(memory_space=pltpu.HBM)
    coded = pl.BlockSpec((4, NCW + 1, 16, 128), lambda *_: (0, 0, 0, 0), pipeline_mode=pl.Buffered(1))
    if form in ("coded", "sent"):
        o_specs = [coded] * 2
        shapes = [jax.ShapeDtypeStruct((4, NCW + 1, 16, 128), jnp.int16)] * 2
    else:
        o_specs = [sums_spec if groups > 2 else any_spec]
        shapes = [jax.ShapeDtypeStruct((max(groups // 2, 1), 8, NCW, 16, 128), jnp.float32)]
    return pl.pallas_call(
        lambda *refs: panel_kernel(n, pieces, halves, form, *refs),
        grid_spec=pltpu.PrefetchScalarGridSpec(
            num_scalar_prefetch=1,
            grid=(1,),
            in_specs=(
                [k_spec(i, place) for i, (_, place) in enumerate(kohn)] + [any_spec] * pieces
                + ([] if sums is None else [sums_spec]) + [coded] * len(received)
            ),
            out_specs=o_specs,
            scratch_shapes=[
                pltpu.VMEM((n * 8 * PART, 128), jnp.bfloat16),
                pltpu.SemaphoreType.DMA((pieces + 1,)),
                pltpu.VMEM((groups, 2, NCW, 16, 128), jnp.float32),
                pltpu.VMEM((groups, 2, NCW, 16, 128), jnp.float32),
                pltpu.SemaphoreType.DMA((groups * 2,)),
                pltpu.SemaphoreType.DMA((groups * 2,)),
                pltpu.VMEM((n * 16, 128), jnp.int32),
                pltpu.SMEM((n * 16, 128), jnp.int32),
            ],
        ),
        out_shape=shapes,
        compiler_params=pltpu.CompilerParams(vmem_limit_bytes=LIMIT << 20),
        cost_estimate=pl.CostEstimate(flops=int(us * 1.1e9), bytes_accessed=int(us * 2e6), transcendentals=0),
        name=name,
    )(at, *[array for array, _ in kohn], *panels, *([] if sums is None else [sums]), *received)


def pack_kernel(slots, own, prev0, next1, o_ref, total, codes):
    rows = lax.broadcasted_iota(jnp.int32, (8, 128), 0)
    lane = lax.broadcasted_iota(jnp.int32, (16, 128), 1)

    def clear(n, _):
        for m in range(4):
            o_ref[n * 4 + m] = jnp.zeros((MSG, 128), jnp.int16)
            codes[n * 4 + m] = jnp.zeros((8, 128), jnp.int32)
        return 0

    lax.fori_loop(0, 32, clear, 0)

    def one(m, r):
        row = m * 4 + r
        coded = (prev0, next1)[m]
        scale = decoded_scale(coded[r, NCW])
        for group in range(NCW // 8):
            blocks = []
            for j in range(group * 8, group * 8 + 8):
                blocks.append(own[0, row, j] + coded[r, j].astype(jnp.int32).astype(jnp.float32) * scale)
            turned = jnp.concatenate(blocks, axis=0).T
            v = []
            for q in range(8):
                par, mh, zh = q // 4, (q // 2) % 2, q % 2
                at = (zh * 4 + par * 2 + mh) * 16
                v.append(turned[at:at + 16, :])
            for bit in (4, 2, 1):
                keep = (lane & (16 * bit)) == 0
                w = [None] * 8
                for i in range(8):
                    if not i & bit:
                        lo, hi = v[i], v[i | bit]
                        w[i] = jnp.where(keep, lo, pltpu.roll(hi, 16 * bit, 1))
                        w[i | bit] = jnp.where(keep, pltpu.roll(lo, 128 - 16 * bit, 1), hi)
                v = w
            for j in range(8):
                total[group * 8 + j] = v[j]

        def put(j, value):
            slot = slots[row * NCW + j]
            o_ref[slot // 4, pl.ds(pl.multiple_of((slot % 4) * 16, 16), 16), :] = value

        def write_code(code):
            for j in range(NCW):
                slot = slots[row * NCW + j]
                codes[slot // 4] = jnp.where(rows == slot % 4, code[:8], codes[slot // 4])

        encode(total, put, write_code)

    for m in range(2):
        lax.fori_loop(0, 4, lambda r, _, m=m: (one(m, r), 0)[1], 0)

    def finish(n, _):
        for m in range(4):
            o_ref[n * 4 + m, 64:72, :] = codes[n * 4 + m].astype(jnp.int16)
        return 0

    lax.fori_loop(0, 32, finish, 0)


def pack(slots, *parts):
    def whole(array):
        return pl.BlockSpec(
            array.shape, lambda i, *_, n=array.ndim: (0,) * n, pipeline_mode=pl.Buffered(1)
        )

    return pl.pallas_call(
        pack_kernel,
        grid_spec=pltpu.PrefetchScalarGridSpec(
            num_scalar_prefetch=1,
            grid=(1,),
            in_specs=[whole(array) for array in parts],
            out_specs=pl.BlockSpec((128, MSG, 128), lambda i, *_: (0, 0, 0), pipeline_mode=pl.Buffered(1)),
            scratch_shapes=[pltpu.VMEM((NCW, 16, 128), jnp.float32), pltpu.VMEM((128, 8, 128), jnp.int32)],
        ),
        out_shape=jax.ShapeDtypeStruct((128, MSG, 128), jnp.int16),
        compiler_params=pltpu.CompilerParams(vmem_limit_bytes=32 << 20),
        name="pack",
    )(slots, *parts)


def unpack_kernel(r_ref, o_ref, full, scales):
    low32 = (lax.broadcasted_iota(jnp.int32, (16, 128), 1) & 32) == 0
    for n in range(16):
        for c in range(2):
            scales[n * 2 + c] = decoded_scale(r_ref[0, c, n, 64:72, :])

    def one(n, _):
        for s in range(2):
            for t in range(2):
                h = []
                for c in range(2):
                    at = (s * 2 + t) * 16
                    q = r_ref[0, c, n, at:at + 16, :].astype(jnp.int32).astype(jnp.float32)
                    h.append(q * scales[n * 2 + c, s * 2 + t:s * 2 + t + 1, :])
                base = pl.multiple_of(((s * 16 + n) * 2 + t) * 32, 32)
                full[pl.ds(base, 16), :] = jnp.where(low32, h[0], pltpu.roll(h[1], 32, 1))
                full[pl.ds(base + 16, 16), :] = jnp.where(low32, pltpu.roll(h[0], 96, 1), h[1])
        return 0

    lax.fori_loop(0, 16, one, 0, unroll=8)
    for p in range(32):
        o_ref[:, p * 128:(p + 1) * 128] = full[pl.ds(p, 64, stride=32), :]


def unpack(received):
    return pl.pallas_call(
        unpack_kernel,
        grid=(X,),
        in_specs=[pl.BlockSpec((1, C, 16, MSG, 128), lambda x: (x, 0, 0, 0, 0))],
        out_specs=pl.BlockSpec((64, 4096), lambda x: (x, 0)),
        out_shape=jax.ShapeDtypeStruct((256, 4096), jnp.float32),
        scratch_shapes=[pltpu.VMEM((64 * 32, 128), jnp.float32), pltpu.VMEM((32, 8, 128), jnp.float32)],
        compiler_params=pltpu.CompilerParams(vmem_limit_bytes=32 << 20),
        name="unpack",
    )(received)


def local(kohn_blocks, kohn_columns, density_blocks, density_columns, owner_map):
    x, c = lax.axis_index("x"), lax.axis_index("core")
    z, y = lax.axis_index("z"), lax.axis_index("y")
    on_line, on_cross = jnp.where(c == 0, z, y), jnp.where(c == 0, y, z)
    at = jnp.stack([c, on_line, on_cross, x])

    kohn = kohn_blocks.reshape(16, 4, SK * 32, 128)
    kohn_other = over_core(kohn)

    ints = jnp.concatenate([
        kohn_columns.reshape(2, 128), jnp.pad(density_columns.reshape(1, 64), ((0, 0), (0, 64))),
        owner_map.reshape(1, 128), jnp.zeros((12, 128), jnp.int32),
    ])
    dens, kohn = lax.optimization_barrier((density_blocks[0], kohn))

    mine, theirs = split(at, dens, ints)
    shard = jnp.concatenate([mine, over_core(theirs)])
    shard, kohn, kohn_other = lax.optimization_barrier((shard, kohn, kohn_other))
    left, right = over_x(shard, 1), over_x(shard, -1)

    kohn, ahead, back = regroup(at, kohn, kohn_other)
    kohn_prev, kohn_next = over_line(ahead, 1), over_line(back, -1)
    opposite0, opposite1 = over_line(kohn_prev[2:], 1), over_line(kohn_next[2:], -1)

    owners = jnp.stack([owner_map.reshape(128), shard[PART + 8 * 128 + 3].astype(jnp.int32)])
    hit = (owners[..., None] == jnp.arange(128, dtype=jnp.int32)).astype(jnp.int32)
    ranks = jnp.sum(jnp.cumsum(hit, axis=1) * hit, axis=2) - 1
    source = jnp.arange(2, dtype=jnp.int32)[:, None] ^ c
    slots = (owners * 4 + source * 2 + ranks).reshape(-1)

    low = jnp.concatenate([shard, left])
    high = jnp.concatenate([right, over_x(left[:PART], 1), over_x(right[PART:], -1)])
    low_sent, high_sent, kohn_prev, kohn_next, slots = lax.optimization_barrier((low, high, kohn_prev, kohn_next, slots))
    prev_low, next_high = over_line(low, 1), over_line(high, -1)
    prev_high, next_low = over_line(high_sent, 1), over_line(low_sent, -1)

    def both(array):
        return [(array, 0), (array, 1)]

    everything = tuple((target, m) for target in range(4) for m in range(2))
    sums, = panel_sums("own_panel", "first", at, both(kohn), [low, high], everything, us=9.0)
    prev_low, next_high, sums = lax.optimization_barrier((prev_low, next_high, sums))
    far_low, far_high = over_line(prev_low, 1), over_line(next_high, -1)
    sums, = panel_sums(
        "near_panels", "more", at, both(kohn_prev) + both(kohn_next), [prev_low, prev_high, next_low, next_high],
        everything, sums, us=16.0,
    )

    sums, opposite0, opposite1 = lax.optimization_barrier((sums, opposite0, opposite1))

    def last(form, halves, received=()):
        kohn = [(opposite0, 0), (opposite1, 0)]
        return panel_sums("last_" + form, form, at, kohn, [far_low, far_high], halves, sums, received)

    via_next, via_prev = last("coded", ((0, 0), (0, 1)))
    via_next, via_prev = over_cross(via_next, 1), over_cross(via_prev, -1)
    next1, prev0 = last("coded", ((1, 1), (2, 0)))
    prev_1, next_0 = over_cross(next1, 1), over_cross(prev0, -1)
    next0, prev1 = last("sent", ((1, 0), (2, 1)), (via_next, via_prev))
    prev_0, next_1 = over_cross(next0, 1), over_cross(prev1, -1)
    own, = last("own", ((3, 0), (3, 1)), (next_0, prev_1))

    outgoing = pack(slots, own, prev_0, next_1)
    received = lax.all_to_all(outgoing, ALL, split_axis=0, concat_axis=0, tiled=True)
    return unpack(received.reshape(X, C, 16, MSG, 128))


def solution(mesh):
    grid = Mesh(mesh.devices.reshape(X, C, Z, Y), ALL)
    row, col = ("x", "core"), ("z", "y")
    return jax.shard_map(
        local,
        mesh=grid,
        in_specs=(
            P(row, col, None, None),
            P(row, col, None),
            P(col, row, None, None),
            P(col, row, None),
            P(ALL, None),
        ),
        out_specs=P(ALL, None),
        check_vma=False,
    )
```

```python
import jax
import jax.numpy as jnp
from jax import lax
from jax.experimental import pallas as pl
from jax.experimental.pallas import tpu as pltpu
from jax.sharding import Mesh, PartitionSpec as P

B = 64
HALF = 32
NCW = 32
SK = 4
SP = 8
X, C, Z, Y = 4, 2, 4, 4
ALL = ("x", "core", "z", "y")
PLANE = ("core", "z", "y")
TOP = 32766.0
MSG = 72
LIMIT = 16
PART = 8 * 128 + 16
ORDER = (2, 1, 3, 0)


def lines(along):
    groups = []
    for c in range(C):
        for fixed in range(4):
            on_z = (c ^ along) == 0
            groups.append([(c * Z + (i if on_z else fixed)) * Y + (fixed if on_z else i) for i in range(4)])
    return groups


LINE, CROSS = lines(0), lines(1)


def over(groups, v, step):
    return lax.ppermute(v, PLANE, [(group[i], group[(i + step) % 4]) for group in groups for i in range(4)])


def over_line(v, step):
    return over(LINE, v, step)


def over_cross(v, step):
    return over(CROSS, v, step)


def over_x(v, step):
    return lax.ppermute(v, "x", [(i, (i + step) % X) for i in range(X)])


def over_core(v):
    return lax.ppermute(v, "core", [(0, 1), (1, 0)])


def split_kernel(core, d_ref, i_ref, mine, theirs, flat0, wide0, flat1, wide1):
    lane32 = lax.broadcasted_iota(jnp.int32, (32, 128), 1)
    lane64 = lax.broadcasted_iota(jnp.int32, (64, 128), 1)

    def one(k, flat, wide):
        rows = d_ref[k].astype(jnp.float32)
        for p in range(32):
            flat[p * 8:(p + 1) * 8, :] = rows[:, p * 128:(p + 1) * 128]
        for b in range(4):
            lo, hi = flat[pl.ds(b, 32, stride=8), :], flat[pl.ds(b + 4, 32, stride=8), :]
            wide[b, pl.ds(0, 32, stride=2), :] = jnp.where(lane32 < 64, lo, pltpu.roll(hi, 64, 1))
            wide[b, pl.ds(1, 32, stride=2), :] = jnp.where(lane32 < 64, pltpu.roll(lo, 64, 1), hi)
        v = [wide[b] for b in range(4)]
        for bit in (2, 1):
            keep = (lane64 & (16 * bit)) == 0
            w = [None] * 4
            for i in range(4):
                if not i & bit:
                    lo, hi = v[i], v[i | bit]
                    w[i] = jnp.where(keep, lo, pltpu.roll(hi, 16 * bit, 1))
                    w[i | bit] = jnp.where(keep, pltpu.roll(lo, 128 - 16 * bit, 1), hi)
            v = w
        first = jnp.concatenate([v[0], v[1]], axis=0).T
        second = jnp.concatenate([v[2], v[3]], axis=0).T
        swapped = core[0] == 1
        at = pl.ds(pl.multiple_of(k * 128, 128), 128)
        mine[at, :] = jnp.where(swapped, second, first).astype(jnp.bfloat16)
        theirs[at, :] = jnp.where(swapped, first, second).astype(jnp.bfloat16)

    def two(i, _):
        one(i * 2, flat0, wide0)
        one(i * 2 + 1, flat1, wide1)
        return 0

    lax.fori_loop(0, 4, two, 0)
    ints = i_ref[...].astype(jnp.float32).astype(jnp.bfloat16)
    mine[8 * 128:, :] = ints
    theirs[8 * 128:, :] = ints


def split(core, dens, ints):
    half = jax.ShapeDtypeStruct((PART, 128), jnp.bfloat16)
    whole = pl.BlockSpec((PART, 128), lambda i, *_: (0, 0))
    return pl.pallas_call(
        split_kernel,
        grid_spec=pltpu.PrefetchScalarGridSpec(
            num_scalar_prefetch=1, grid=(1,),
            in_specs=[
                pl.BlockSpec((8, SP, B * B), lambda i, *_: (0, 0, 0)), pl.BlockSpec((16, 128), lambda i, *_: (0, 0))
            ],
            out_specs=[whole, whole],
            scratch_shapes=[pltpu.VMEM((256, 128), jnp.float32), pltpu.VMEM((4, B, 128), jnp.float32)] * 2,
        ),
        out_shape=[half, half],
        name="split",
    )(core, dens, ints)


def regroup_kernel(at, mine, other, ahead, back, sems):
    swapped, line, cross = at[0] == 1, at[1], at[2]
    copies = []
    for step in (1, 2, 3):
        t = (line + step) % 4
        for i, rel in enumerate(ORDER):
            o = (cross + rel) % 4
            row = jnp.where(swapped, o * 4 + t, t * 4 + o)
            for m, src in enumerate((mine, other)):
                dst = (ahead.at[m, i], (ahead, back)[m].at[2, i], back.at[m, i])[step - 1]
                copies.append(pltpu.make_async_copy(src.at[row], dst, sems.at[len(copies)]))
    for copy in copies:
        copy.start()
    for copy in copies:
        copy.wait()


def regroup(at, mine, other):
    shapes = [(3, 4, 4, 128, 128)] * 2
    return pl.pallas_call(
        regroup_kernel,
        grid_spec=pltpu.PrefetchScalarGridSpec(
            num_scalar_prefetch=1, grid=(1,),
            in_specs=[pl.BlockSpec(memory_space=pl.ANY)] * 2,
            out_specs=[pl.BlockSpec(s, lambda i, *_: (0,) * 5, pipeline_mode=pl.Buffered(1)) for s in shapes],
            scratch_shapes=[pltpu.SemaphoreType.DMA((24,))],
        ),
        out_shape=[jax.ShapeDtypeStruct(shape, jnp.bfloat16) for shape in shapes],
        compiler_params=pltpu.CompilerParams(vmem_limit_bytes=12 << 20),
        name="regroup",
    )(at, mine, other)


def encode(values, put, write_code):
    top = jnp.zeros((16, 128), jnp.float32)
    for j in range(NCW):
        top = jnp.maximum(top, jnp.abs(values[j]))
    top = jnp.maximum(jnp.max(top, axis=0, keepdims=True), 2.0 ** -110)
    code = jnp.floor(jnp.log2(top) * 256.0) + 1.0
    scale = jnp.broadcast_to(jnp.exp2(code * (-1.0 / 256.0)) * TOP, (16, 128))
    write_code(jnp.broadcast_to(code.astype(jnp.int32), (16, 128)))
    for j in range(NCW):
        put(j, jnp.floor(values[j] * scale + 0.5).astype(jnp.int32).astype(jnp.int16))


def decoded_scale(code):
    return jnp.exp2(code.astype(jnp.int32).astype(jnp.float32) * (1.0 / 256.0)) * (1.0 / TOP)


def panel_kernel(n, pieces, halves, form, at, *refs):
    kohn, refs = refs[:2 * n], refs[2 * n:]
    panels, refs = refs[:pieces], refs[pieces:]
    if form == "first":
        picked, picked_sems, refs = refs[-2], refs[-1], refs[:-2]
    if form != "first":
        sums_in, refs = refs[0], refs[1:]
    received = ()
    if form in ("sent", "own"):
        received, refs = refs[:2], refs[2:]
    outs, (dens, sems, acc0, acc1, in_sems, out_sems, staged, ints) = refs[:-8], refs[-8:]
    accs = (acc0, acc1)
    size = n * 8 * PART // pieces
    core, line, cross, x = at[0], at[1], at[2], at[3]

    loads = [pltpu.make_async_copy(panels[s], dens.at[pl.ds(s * size, size)], sems.at[s]) for s in range(pieces)]
    sums = []
    if form == "first":
        for i, rel in enumerate(ORDER):
            goal = (cross + rel) & 3
            row = jnp.where(core == 1, goal * 4 + line, line * 4 + goal)
            for m in range(2):
                loads.append(pltpu.make_async_copy(kohn[m].at[row], picked.at[m, i], picked_sems.at[m * 4 + i]))
    else:
        for h, (target, m) in enumerate(halves):
            for q in range(2):
                src = sums_in.at[target, pl.ds(m * 4 + q * 2, 2)]
                sums.append(pltpu.make_async_copy(src, accs[q].at[h], in_sems.at[h * 2 + q]))
    stores = []
    if form in ("first", "more", "own"):
        for h, (target, m) in enumerate(halves):
            for q in range(2):
                dst = outs[0].at[target if len(halves) > 2 else 0, pl.ds(m * 4 + q * 2, 2)]
                stores.append(pltpu.make_async_copy(accs[q].at[h], dst, out_sems.at[h * 2 + q]))
    for copy in loads + sums:
        copy.start()
    for copy in loads:
        copy.wait()
    for s in range(n):
        rows = [dens[pl.ds((s * 8 + p) * PART + 8 * 128, 16), :].astype(jnp.float32) for p in range(8)]
        rows = [row[2:3] for row in rows] + [rows[0][0:2], rows[1][0:2], jnp.zeros((4, 128), jnp.float32)]
        staged[s * 16:(s + 1) * 16, :] = jnp.concatenate(rows, axis=0).astype(jnp.int32)
    copy = pltpu.make_async_copy(staged, ints, sems.at[pieces])
    copy.start()
    copy.wait()

    low = (lax.broadcasted_iota(jnp.int32, (32, 128), 1) < 64).astype(jnp.float32).astype(jnp.bfloat16)
    high = 1 - low

    def twice(blk):
        turned = jnp.concatenate([blk[:, B:], blk[:, :B]], axis=1)
        return jnp.concatenate([blk * low, turned * low, turned * high, blk * high], axis=0)

    def product(h, r, s, a):
        target, m = halves[h]
        goal = (cross + ORDER[target]) & 3
        place = jnp.where(core == 1, goal * 4 + line, line * 4 + goal)
        k = ints[s * 16 + 8 + m * 2 + (place >> 3), (place & 7) * 16 + r * 4 + a]
        slot = (120 >> (2 * (((k >> 4) - x) & 3))) & 3
        k = slot * 16 + ((k & 15) ^ (8 * core))
        part = s * 8 + (k >> 3)
        left = dens[pl.ds(pl.multiple_of(part * PART + (k & 7) * 128, 16), 128), :]
        if form == "first":
            ref, index = picked.at[m], target
        else:
            ref, index = kohn[2 * s + m].at[0], target if kohn[2 * s + m].shape[1] == 4 else 0
        right = twice(ref[index, r, a * 32:(a + 1) * 32, :])
        r = lax.dot_general(left, right, (((1,), (1,)), ((), ())), preferred_element_type=jnp.float32)
        return s * 16 + (k >> 3), (k & 7) * SP, r

    def add(total, word, first, r):
        js = [ints[word, first + b] for b in range(SP)]
        old = [total[j] for j in js]
        for b in range(SP):
            total[js[b]] = old[b] + r[b * 16:(b + 1) * 16, :]

    def two_rows(h, pair):
        totals = []
        work = [(q, q * 2 + pair, s, a) for s in range(n) for a in range(SK) for q in range(2)]
        for q in range(2):
            r = q * 2 + pair
            total = accs[q].at[h, pair]
            if form == "first":
                total[...] = jnp.zeros((NCW, 16, 128), jnp.float32)
            elif received:
                scale = decoded_scale(received[h][r, NCW])
                for j in range(NCW):
                    total[j] = total[j] + received[h][r, j].astype(jnp.int32).astype(jnp.float32) * scale
            totals.append(total)
        held = [product(h, *work[i][1:]) for i in range(4)]
        for i in range(len(work)):
            if i + 4 < len(work):
                held.append(product(h, *work[i + 4][1:]))
            add(totals[work[i][0]], *held[i])
        if form in ("coded", "sent"):
            for q in range(2):
                r = q * 2 + pair

                def put(j, value, r=r):
                    outs[h][r, j] = value

                encode(totals[q], put, lambda code, put=put: put(NCW, code.astype(jnp.int16)))

    for h in range(len(halves)):
        for copy in sums[2 * h:2 * h + 2]:
            copy.wait()
        lax.fori_loop(0, 2, lambda pair, _, h=h: (two_rows(h, pair), 0)[1], 0)
        for copy in stores[2 * h:2 * h + 2]:
            copy.start()
    for copy in stores:
        copy.wait()


def panel_sums(name, form, at, kohn, panels, halves, sums=None, received=(), us=4.0):
    n, pieces, groups = len(kohn) // 2, len(panels), len(halves)

    def k_spec(i, place):
        if groups > 2:
            return pl.BlockSpec((1, 4, 4, 128, 128), lambda *_: (place, 0, 0, 0, 0), pipeline_mode=pl.Buffered(1))
        target = {m: t for t, m in halves}[i % 2]
        return pl.BlockSpec((1, 1, 4, 128, 128), lambda *_: (place, target, 0, 0, 0), pipeline_mode=pl.Buffered(1))

    any_spec = pl.BlockSpec(memory_space=pl.ANY)
    sums_spec = pl.BlockSpec(memory_space=pltpu.HBM)
    coded = pl.BlockSpec((4, NCW + 1, 16, 128), lambda *_: (0, 0, 0, 0), pipeline_mode=pl.Buffered(1))
    if form in ("coded", "sent"):
        o_specs = [coded] * 2
        shapes = [jax.ShapeDtypeStruct((4, NCW + 1, 16, 128), jnp.int16)] * 2
    else:
        o_specs = [sums_spec if groups > 2 else any_spec]
        shapes = [jax.ShapeDtypeStruct((max(groups // 2, 1), 8, NCW, 16, 128), jnp.float32)]
    return pl.pallas_call(
        lambda *refs: panel_kernel(n, pieces, halves, form, *refs),
        grid_spec=pltpu.PrefetchScalarGridSpec(
            num_scalar_prefetch=1,
            grid=(1,),
            in_specs=(
                [any_spec if form == "first" else k_spec(i, place) for i, (_, place) in enumerate(kohn)]
                + [any_spec] * pieces
                + ([] if sums is None else [sums_spec]) + [coded] * len(received)
            ),
            out_specs=o_specs,
            scratch_shapes=[
                pltpu.VMEM((n * 8 * PART, 128), jnp.bfloat16),
                pltpu.SemaphoreType.DMA((pieces + 1,)),
                pltpu.VMEM((groups, 2, NCW, 16, 128), jnp.float32),
                pltpu.VMEM((groups, 2, NCW, 16, 128), jnp.float32),
                pltpu.SemaphoreType.DMA((groups * 2,)),
                pltpu.SemaphoreType.DMA((groups * 2,)),
                pltpu.VMEM((n * 16, 128), jnp.int32),
                pltpu.SMEM((n * 16, 128), jnp.int32),
            ] + [
                pltpu.VMEM((2, 4, 4, 128, 128), jnp.bfloat16), pltpu.SemaphoreType.DMA((8,))
            ] * (form == "first"),
        ),
        out_shape=shapes,
        compiler_params=pltpu.CompilerParams(vmem_limit_bytes=LIMIT << 20),
        cost_estimate=pl.CostEstimate(flops=int(us * 1.1e9), bytes_accessed=int(us * 2e6), transcendentals=0),
        name=name,
    )(at, *[array for array, _ in kohn], *panels, *([] if sums is None else [sums]), *received)


def pack_kernel(slots, own, prev0, next1, o_ref, total, codes):
    rows = lax.broadcasted_iota(jnp.int32, (8, 128), 0)
    lane = lax.broadcasted_iota(jnp.int32, (16, 128), 1)

    def clear(n, _):
        for m in range(4):
            o_ref[n * 4 + m] = jnp.zeros((MSG, 128), jnp.int16)
            codes[n * 4 + m] = jnp.zeros((8, 128), jnp.int32)
        return 0

    lax.fori_loop(0, 32, clear, 0)

    def one(m, r):
        row = m * 4 + r
        coded = (prev0, next1)[m]
        scale = decoded_scale(coded[r, NCW])
        for group in range(NCW // 8):
            blocks = []
            for j in range(group * 8, group * 8 + 8):
                blocks.append(own[0, row, j] + coded[r, j].astype(jnp.int32).astype(jnp.float32) * scale)
            turned = jnp.concatenate(blocks, axis=0).T
            v = []
            for q in range(8):
                par, mh, zh = q // 4, (q // 2) % 2, q % 2
                at = (zh * 4 + par * 2 + mh) * 16
                v.append(turned[at:at + 16, :])
            for bit in (4, 2, 1):
                keep = (lane & (16 * bit)) == 0
                w = [None] * 8
                for i in range(8):
                    if not i & bit:
                        lo, hi = v[i], v[i | bit]
                        w[i] = jnp.where(keep, lo, pltpu.roll(hi, 16 * bit, 1))
                        w[i | bit] = jnp.where(keep, pltpu.roll(lo, 128 - 16 * bit, 1), hi)
                v = w
            for j in range(8):
                total[group * 8 + j] = v[j]

        def put(j, value):
            slot = slots[row * NCW + j]
            o_ref[slot // 4, pl.ds(pl.multiple_of((slot % 4) * 16, 16), 16), :] = value

        def write_code(code):
            for j in range(NCW):
                slot = slots[row * NCW + j]
                codes[slot // 4] = jnp.where(rows == slot % 4, code[:8], codes[slot // 4])

        encode(total, put, write_code)

    for m in range(2):
        lax.fori_loop(0, 4, lambda r, _, m=m: (one(m, r), 0)[1], 0)

    def finish(n, _):
        for m in range(4):
            o_ref[n * 4 + m, 64:72, :] = codes[n * 4 + m].astype(jnp.int16)
        return 0

    lax.fori_loop(0, 32, finish, 0)


def pack(slots, *parts):
    def whole(array):
        return pl.BlockSpec(
            array.shape, lambda i, *_, n=array.ndim: (0,) * n, pipeline_mode=pl.Buffered(1)
        )

    return pl.pallas_call(
        pack_kernel,
        grid_spec=pltpu.PrefetchScalarGridSpec(
            num_scalar_prefetch=1,
            grid=(1,),
            in_specs=[whole(array) for array in parts],
            out_specs=pl.BlockSpec((128, MSG, 128), lambda i, *_: (0, 0, 0), pipeline_mode=pl.Buffered(1)),
            scratch_shapes=[pltpu.VMEM((NCW, 16, 128), jnp.float32), pltpu.VMEM((128, 8, 128), jnp.int32)],
        ),
        out_shape=jax.ShapeDtypeStruct((128, MSG, 128), jnp.int16),
        compiler_params=pltpu.CompilerParams(vmem_limit_bytes=32 << 20),
        name="pack",
    )(slots, *parts)


def unpack_kernel(r_ref, o_ref, full, scales):
    low32 = (lax.broadcasted_iota(jnp.int32, (16, 128), 1) & 32) == 0
    for n in range(16):
        for c in range(2):
            scales[n * 2 + c] = decoded_scale(r_ref[0, c, n, 64:72, :])

    def one(n, _):
        for s in range(2):
            for t in range(2):
                h = []
                for c in range(2):
                    at = (s * 2 + t) * 16
                    q = r_ref[0, c, n, at:at + 16, :].astype(jnp.int32).astype(jnp.float32)
                    h.append(q * scales[n * 2 + c, s * 2 + t:s * 2 + t + 1, :])
                base = pl.multiple_of(((s * 16 + n) * 2 + t) * 32, 32)
                full[pl.ds(base, 16), :] = jnp.where(low32, h[0], pltpu.roll(h[1], 32, 1))
                full[pl.ds(base + 16, 16), :] = jnp.where(low32, pltpu.roll(h[0], 96, 1), h[1])
        return 0

    lax.fori_loop(0, 16, one, 0, unroll=8)
    for p in range(32):
        o_ref[:, p * 128:(p + 1) * 128] = full[pl.ds(p, 64, stride=32), :]


def unpack(received):
    return pl.pallas_call(
        unpack_kernel,
        grid=(X,),
        in_specs=[pl.BlockSpec((1, C, 16, MSG, 128), lambda x: (x, 0, 0, 0, 0))],
        out_specs=pl.BlockSpec((64, 4096), lambda x: (x, 0)),
        out_shape=jax.ShapeDtypeStruct((256, 4096), jnp.float32),
        scratch_shapes=[pltpu.VMEM((64 * 32, 128), jnp.float32), pltpu.VMEM((32, 8, 128), jnp.float32)],
        compiler_params=pltpu.CompilerParams(vmem_limit_bytes=32 << 20),
        name="unpack",
    )(received)


def local(kohn_blocks, kohn_columns, density_blocks, density_columns, owner_map):
    x, c = lax.axis_index("x"), lax.axis_index("core")
    z, y = lax.axis_index("z"), lax.axis_index("y")
    on_line, on_cross = jnp.where(c == 0, z, y), jnp.where(c == 0, y, z)
    at = jnp.stack([c, on_line, on_cross, x])

    ints = jnp.concatenate([
        kohn_columns.reshape(2, 128), jnp.pad(density_columns.reshape(1, 64), ((0, 0), (0, 64))),
        owner_map.reshape(1, 128), jnp.zeros((12, 128), jnp.int32),
    ])

    mine, theirs = split(at, density_blocks[0], ints)
    kohn, mine, theirs = lax.optimization_barrier((kohn_blocks, mine, theirs))
    kohn = kohn.reshape(16, 4, SK * 32, 128)
    kohn_other = over_core(kohn)
    shard = jnp.concatenate([mine, over_core(theirs)])
    shard, kohn, kohn_other = lax.optimization_barrier((shard, kohn, kohn_other))
    left, right = over_x(shard, 1), over_x(shard, -1)

    ahead, back = regroup(at, kohn, kohn_other)
    kohn_prev, kohn_next = over_line(ahead, 1), over_line(back, -1)
    opposite0, opposite1 = over_line(kohn_prev[2:], 1), over_line(kohn_next[2:], -1)

    owners = jnp.stack([owner_map.reshape(128), shard[PART + 8 * 128 + 3].astype(jnp.int32)])
    hit = (owners[..., None] == jnp.arange(128, dtype=jnp.int32)).astype(jnp.int32)
    ranks = jnp.sum(jnp.cumsum(hit, axis=1) * hit, axis=2) - 1
    source = jnp.arange(2, dtype=jnp.int32)[:, None] ^ c
    slots = (owners * 4 + source * 2 + ranks).reshape(-1)

    low = jnp.concatenate([shard, left])
    high = jnp.concatenate([right, over_x(left[:PART], 1), over_x(right[PART:], -1)])
    low_sent, high_sent, kohn_prev, kohn_next, slots = lax.optimization_barrier((low, high, kohn_prev, kohn_next, slots))
    prev_low, next_high = over_line(low, 1), over_line(high, -1)
    prev_high, next_low = over_line(high_sent, 1), over_line(low_sent, -1)

    def both(array):
        return [(array, 0), (array, 1)]

    everything = tuple((target, m) for target in range(4) for m in range(2))
    sums, = panel_sums("own_panel", "first", at, [(kohn, 0), (kohn_other, 0)], [low, high], everything, us=9.0)
    prev_low, next_high, sums = lax.optimization_barrier((prev_low, next_high, sums))
    far_low, far_high = over_line(prev_low, 1), over_line(next_high, -1)
    sums, = panel_sums(
        "near_panels", "more", at, both(kohn_prev) + both(kohn_next), [prev_low, prev_high, next_low, next_high],
        everything, sums, us=16.0,
    )

    sums, opposite0, opposite1 = lax.optimization_barrier((sums, opposite0, opposite1))

    def last(form, halves, received=()):
        kohn = [(opposite0, 0), (opposite1, 0)]
        return panel_sums("last_" + form, form, at, kohn, [far_low, far_high], halves, sums, received)

    via_next, via_prev = last("coded", ((0, 0), (0, 1)))
    via_next, via_prev = over_cross(via_next, 1), over_cross(via_prev, -1)
    next1, prev0 = last("coded", ((1, 1), (2, 0)))
    prev_1, next_0 = over_cross(next1, 1), over_cross(prev0, -1)
    next0, prev1 = last("sent", ((1, 0), (2, 1)), (via_next, via_prev))
    prev_0, next_1 = over_cross(next0, 1), over_cross(prev1, -1)
    own, = last("own", ((3, 0), (3, 1)), (next_0, prev_1))

    outgoing = pack(slots, own, prev_0, next_1)
    received = lax.all_to_all(outgoing, ALL, split_axis=0, concat_axis=0, tiled=True)
    return unpack(received.reshape(X, C, 16, MSG, 128))


def solution(mesh):
    grid = Mesh(mesh.devices.reshape(X, C, Z, Y), ALL)
    row, col = ("x", "core"), ("z", "y")
    return jax.shard_map(
        local,
        mesh=grid,
        in_specs=(
            P(row, col, None, None),
            P(row, col, None),
            P(col, row, None, None),
            P(col, row, None),
            P(ALL, None),
        ),
        out_specs=P(ALL, None),
        check_vma=False,
    )
```

```python
import jax
import jax.numpy as jnp
from jax import lax
from jax.experimental import pallas as pl
from jax.experimental.pallas import tpu as pltpu
from jax.sharding import Mesh, PartitionSpec as P

B = 64
HALF = 32
NCW = 32
SK = 4
SP = 8
X, C, Z, Y = 4, 2, 4, 4
ALL = ("x", "core", "z", "y")
PLANE = ("core", "z", "y")
TOP = 32766.0
MSG = 72
LIMIT = 16
PART = 8 * 128 + 16
ORDER = (2, 1, 3, 0)


def lines(along):
    groups = []
    for c in range(C):
        for fixed in range(4):
            on_z = (c ^ along) == 0
            groups.append([(c * Z + (i if on_z else fixed)) * Y + (fixed if on_z else i) for i in range(4)])
    return groups


LINE, CROSS = lines(0), lines(1)


def over(groups, v, step):
    return lax.ppermute(v, PLANE, [(group[i], group[(i + step) % 4]) for group in groups for i in range(4)])


def over_line(v, step):
    return over(LINE, v, step)


def over_cross(v, step):
    return over(CROSS, v, step)


def over_x(v, step):
    return lax.ppermute(v, "x", [(i, (i + step) % X) for i in range(X)])


def over_core(v):
    return lax.ppermute(v, "core", [(0, 1), (1, 0)])


def split_kernel(core, d_ref, i_ref, mine, theirs, flat0, wide0, flat1, wide1):
    lane32 = lax.broadcasted_iota(jnp.int32, (32, 128), 1)
    lane64 = lax.broadcasted_iota(jnp.int32, (64, 128), 1)

    def one(k, flat, wide):
        rows = d_ref[k].astype(jnp.float32)
        for p in range(32):
            flat[p * 8:(p + 1) * 8, :] = rows[:, p * 128:(p + 1) * 128]
        for b in range(4):
            lo, hi = flat[pl.ds(b, 32, stride=8), :], flat[pl.ds(b + 4, 32, stride=8), :]
            wide[b, pl.ds(0, 32, stride=2), :] = jnp.where(lane32 < 64, lo, pltpu.roll(hi, 64, 1))
            wide[b, pl.ds(1, 32, stride=2), :] = jnp.where(lane32 < 64, pltpu.roll(lo, 64, 1), hi)
        v = [wide[b] for b in range(4)]
        for bit in (2, 1):
            keep = (lane64 & (16 * bit)) == 0
            w = [None] * 4
            for i in range(4):
                if not i & bit:
                    lo, hi = v[i], v[i | bit]
                    w[i] = jnp.where(keep, lo, pltpu.roll(hi, 16 * bit, 1))
                    w[i | bit] = jnp.where(keep, pltpu.roll(lo, 128 - 16 * bit, 1), hi)
            v = w
        first = jnp.concatenate([v[0], v[1]], axis=0).T
        second = jnp.concatenate([v[2], v[3]], axis=0).T
        swapped = core[0] == 1
        at = pl.ds(pl.multiple_of(k * 128, 128), 128)
        mine[at, :] = jnp.where(swapped, second, first).astype(jnp.bfloat16)
        theirs[at, :] = jnp.where(swapped, first, second).astype(jnp.bfloat16)

    def two(i, _):
        one(i * 2, flat0, wide0)
        one(i * 2 + 1, flat1, wide1)
        return 0

    lax.fori_loop(0, 4, two, 0)
    ints = i_ref[...].astype(jnp.float32).astype(jnp.bfloat16)
    mine[8 * 128:, :] = ints
    theirs[8 * 128:, :] = ints


def split(core, dens, ints):
    half = jax.ShapeDtypeStruct((PART, 128), jnp.bfloat16)
    whole = pl.BlockSpec((PART, 128), lambda i, *_: (0, 0))
    return pl.pallas_call(
        split_kernel,
        grid_spec=pltpu.PrefetchScalarGridSpec(
            num_scalar_prefetch=1, grid=(1,),
            in_specs=[
                pl.BlockSpec((8, SP, B * B), lambda i, *_: (0, 0, 0)), pl.BlockSpec((16, 128), lambda i, *_: (0, 0))
            ],
            out_specs=[whole, whole],
            scratch_shapes=[pltpu.VMEM((256, 128), jnp.float32), pltpu.VMEM((4, B, 128), jnp.float32)] * 2,
        ),
        out_shape=[half, half],
        name="split",
    )(core, dens, ints)


def regroup_kernel(at, mine, other, own, ahead, back, sems):
    swapped, line, cross = at[0] == 1, at[1], at[2]
    copies = []
    for step in range(4):
        t = (line + step) % 4
        for i, rel in enumerate(ORDER):
            o = (cross + rel) % 4
            row = jnp.where(swapped, o * 4 + t, t * 4 + o)
            for m, src in enumerate((mine, other)):
                dst = (own.at[m, i], ahead.at[m, i], (ahead, back)[m].at[2, i], back.at[m, i])[step]
                copies.append(pltpu.make_async_copy(src.at[row], dst, sems.at[len(copies)]))
    for copy in copies:
        copy.start()
    for copy in copies:
        copy.wait()


def regroup(at, mine, other):
    shapes = [(2, 4, 4, 128, 128), (3, 4, 4, 128, 128), (3, 4, 4, 128, 128)]
    return pl.pallas_call(
        regroup_kernel,
        grid_spec=pltpu.PrefetchScalarGridSpec(
            num_scalar_prefetch=1, grid=(1,),
            in_specs=[pl.BlockSpec(memory_space=pl.ANY)] * 2,
            out_specs=[pl.BlockSpec(s, lambda i, *_: (0,) * 5, pipeline_mode=pl.Buffered(1)) for s in shapes],
            scratch_shapes=[pltpu.SemaphoreType.DMA((32,))],
        ),
        out_shape=[jax.ShapeDtypeStruct(shape, jnp.bfloat16) for shape in shapes],
        compiler_params=pltpu.CompilerParams(vmem_limit_bytes=12 << 20),
        name="regroup",
    )(at, mine, other)


def encode(values, put, write_code):
    top = jnp.zeros((16, 128), jnp.float32)
    for j in range(NCW):
        top = jnp.maximum(top, jnp.abs(values[j]))
    top = jnp.maximum(jnp.max(top, axis=0, keepdims=True), 2.0 ** -110)
    code = jnp.floor(jnp.log2(top) * 256.0) + 1.0
    scale = jnp.broadcast_to(jnp.exp2(code * (-1.0 / 256.0)) * TOP, (16, 128))
    write_code(jnp.broadcast_to(code.astype(jnp.int32), (16, 128)))
    for j in range(NCW):
        put(j, jnp.floor(values[j] * scale + 0.5).astype(jnp.int32).astype(jnp.int16))


def decoded_scale(code):
    return jnp.exp2(code.astype(jnp.int32).astype(jnp.float32) * (1.0 / 256.0)) * (1.0 / TOP)


def panel_kernel(n, pieces, halves, form, at, *refs):
    kohn, refs = refs[:2 * n], refs[2 * n:]
    panels, refs = refs[:pieces], refs[pieces:]
    if form != "first":
        sums_in, refs = refs[0], refs[1:]
    received = ()
    if form in ("sent", "own"):
        received, refs = refs[:2], refs[2:]
    outs, (dens, sems, acc0, acc1, in_sems, out_sems, staged, ints) = refs[:-8], refs[-8:]
    accs = (acc0, acc1)
    size = n * 8 * PART // pieces
    core, line, cross, x = at[0], at[1], at[2], at[3]

    loads = [pltpu.make_async_copy(panels[s], dens.at[pl.ds(s * size, size)], sems.at[s]) for s in range(pieces)]
    sums = []
    if form != "first":
        for h, (target, m) in enumerate(halves):
            for q in range(2):
                src = sums_in.at[target, pl.ds(m * 4 + q * 2, 2)]
                sums.append(pltpu.make_async_copy(src, accs[q].at[h], in_sems.at[h * 2 + q]))
    stores = []
    if form in ("first", "more", "own"):
        for h, (target, m) in enumerate(halves):
            for q in range(2):
                dst = outs[0].at[target if len(halves) > 2 else 0, pl.ds(m * 4 + q * 2, 2)]
                stores.append(pltpu.make_async_copy(accs[q].at[h], dst, out_sems.at[h * 2 + q]))
    for copy in loads + sums:
        copy.start()
    for copy in loads:
        copy.wait()
    for s in range(n):
        rows = [dens[pl.ds((s * 8 + p) * PART + 8 * 128, 16), :].astype(jnp.float32) for p in range(8)]
        rows = [row[2:3] for row in rows] + [rows[0][0:2], rows[1][0:2], jnp.zeros((4, 128), jnp.float32)]
        staged[s * 16:(s + 1) * 16, :] = jnp.concatenate(rows, axis=0).astype(jnp.int32)
    copy = pltpu.make_async_copy(staged, ints, sems.at[pieces])
    copy.start()
    copy.wait()

    low = (lax.broadcasted_iota(jnp.int32, (32, 128), 1) < 64).astype(jnp.float32).astype(jnp.bfloat16)
    high = 1 - low

    def twice(blk):
        turned = jnp.concatenate([blk[:, B:], blk[:, :B]], axis=1)
        return jnp.concatenate([blk * low, turned * low, turned * high, blk * high], axis=0)

    def product(h, r, s, a):
        target, m = halves[h]
        goal = (cross + ORDER[target]) & 3
        place = jnp.where(core == 1, goal * 4 + line, line * 4 + goal)
        k = ints[s * 16 + 8 + m * 2 + (place >> 3), (place & 7) * 16 + r * 4 + a]
        slot = (120 >> (2 * (((k >> 4) - x) & 3))) & 3
        k = slot * 16 + ((k & 15) ^ (8 * core))
        part = s * 8 + (k >> 3)
        left = dens[pl.ds(pl.multiple_of(part * PART + (k & 7) * 128, 16), 128), :]
        ref, index = kohn[2 * s + m], target if kohn[2 * s + m].shape[1] == 4 else 0
        right = twice(ref[0, index, r, a * 32:(a + 1) * 32, :])
        r = lax.dot_general(left, right, (((1,), (1,)), ((), ())), preferred_element_type=jnp.float32)
        return s * 16 + (k >> 3), (k & 7) * SP, r

    def add(total, word, first, r):
        js = [ints[word, first + b] for b in range(SP)]
        old = [total[j] for j in js]
        for b in range(SP):
            total[js[b]] = old[b] + r[b * 16:(b + 1) * 16, :]

    def two_rows(h, pair):
        totals = []
        work = [(q, q * 2 + pair, s, a) for s in range(n) for a in range(SK) for q in range(2)]
        for q in range(2):
            r = q * 2 + pair
            total = accs[q].at[h, pair]
            if form == "first":
                total[...] = jnp.zeros((NCW, 16, 128), jnp.float32)
            elif received:
                scale = decoded_scale(received[h][r, NCW])
                for j in range(NCW):
                    total[j] = total[j] + received[h][r, j].astype(jnp.int32).astype(jnp.float32) * scale
            totals.append(total)
        held = [product(h, *work[i][1:]) for i in range(4)]
        for i in range(len(work)):
            if i + 4 < len(work):
                held.append(product(h, *work[i + 4][1:]))
            add(totals[work[i][0]], *held[i])
        if form in ("coded", "sent"):
            for q in range(2):
                r = q * 2 + pair

                def put(j, value, r=r):
                    outs[h][r, j] = value

                encode(totals[q], put, lambda code, put=put: put(NCW, code.astype(jnp.int16)))

    for h in range(len(halves)):
        for copy in sums[2 * h:2 * h + 2]:
            copy.wait()
        if len(halves) > 2:
            lax.fori_loop(0, 2, lambda pair, _, h=h: (two_rows(h, pair), 0)[1], 0)
        else:
            two_rows(h, 0)
            two_rows(h, 1)
        for copy in stores[2 * h:2 * h + 2]:
            copy.start()
    for copy in stores:
        copy.wait()


def panel_sums(name, form, at, kohn, panels, halves, sums=None, received=(), us=4.0):
    n, pieces, groups = len(kohn) // 2, len(panels), len(halves)

    def k_spec(i, place):
        if groups > 2:
            return pl.BlockSpec((1, 4, 4, 128, 128), lambda *_: (place, 0, 0, 0, 0), pipeline_mode=pl.Buffered(1))
        target = {m: t for t, m in halves}[i % 2]
        return pl.BlockSpec((1, 1, 4, 128, 128), lambda *_: (place, target, 0, 0, 0), pipeline_mode=pl.Buffered(1))

    any_spec = pl.BlockSpec(memory_space=pl.ANY)
    sums_spec = pl.BlockSpec(memory_space=pltpu.HBM)
    coded = pl.BlockSpec((4, NCW + 1, 16, 128), lambda *_: (0, 0, 0, 0), pipeline_mode=pl.Buffered(1))
    if form in ("coded", "sent"):
        o_specs = [coded] * 2
        shapes = [jax.ShapeDtypeStruct((4, NCW + 1, 16, 128), jnp.int16)] * 2
    else:
        o_specs = [sums_spec if groups > 2 else any_spec]
        shapes = [jax.ShapeDtypeStruct((max(groups // 2, 1), 8, NCW, 16, 128), jnp.float32)]
    return pl.pallas_call(
        lambda *refs: panel_kernel(n, pieces, halves, form, *refs),
        grid_spec=pltpu.PrefetchScalarGridSpec(
            num_scalar_prefetch=1,
            grid=(1,),
            in_specs=(
                [k_spec(i, place) for i, (_, place) in enumerate(kohn)] + [any_spec] * pieces
                + ([] if sums is None else [sums_spec]) + [coded] * len(received)
            ),
            out_specs=o_specs,
            scratch_shapes=[
                pltpu.VMEM((n * 8 * PART, 128), jnp.bfloat16),
                pltpu.SemaphoreType.DMA((pieces + 1,)),
                pltpu.VMEM((groups, 2, NCW, 16, 128), jnp.float32),
                pltpu.VMEM((groups, 2, NCW, 16, 128), jnp.float32),
                pltpu.SemaphoreType.DMA((groups * 2,)),
                pltpu.SemaphoreType.DMA((groups * 2,)),
                pltpu.VMEM((n * 16, 128), jnp.int32),
                pltpu.SMEM((n * 16, 128), jnp.int32),
            ],
        ),
        out_shape=shapes,
        compiler_params=pltpu.CompilerParams(vmem_limit_bytes=LIMIT << 20),
        cost_estimate=pl.CostEstimate(flops=int(us * 1.1e9), bytes_accessed=int(us * 2e6), transcendentals=0),
        name=name,
    )(at, *[array for array, _ in kohn], *panels, *([] if sums is None else [sums]), *received)


def pack_kernel(slots, own, prev0, next1, o_ref, total0, total1, codes):
    rows = lax.broadcasted_iota(jnp.int32, (8, 128), 0)
    lane = lax.broadcasted_iota(jnp.int32, (16, 128), 1)

    def clear(n, _):
        for m in range(4):
            o_ref[n * 4 + m] = jnp.zeros((MSG, 128), jnp.int16)
            codes[n * 4 + m] = jnp.zeros((8, 128), jnp.int32)
        return 0

    lax.fori_loop(0, 32, clear, 0)

    def one(m, r):
        row = m * 4 + r
        coded, total = (prev0, next1)[m], (total0, total1)[m]
        scale = decoded_scale(coded[r, NCW])
        for group in range(NCW // 8):
            blocks = []
            for j in range(group * 8, group * 8 + 8):
                blocks.append(own[0, row, j] + coded[r, j].astype(jnp.int32).astype(jnp.float32) * scale)
            turned = jnp.concatenate(blocks, axis=0).T
            v = []
            for q in range(8):
                par, mh, zh = q // 4, (q // 2) % 2, q % 2
                at = (zh * 4 + par * 2 + mh) * 16
                v.append(turned[at:at + 16, :])
            for bit in (4, 2, 1):
                keep = (lane & (16 * bit)) == 0
                w = [None] * 8
                for i in range(8):
                    if not i & bit:
                        lo, hi = v[i], v[i | bit]
                        w[i] = jnp.where(keep, lo, pltpu.roll(hi, 16 * bit, 1))
                        w[i | bit] = jnp.where(keep, pltpu.roll(lo, 128 - 16 * bit, 1), hi)
                v = w
            for j in range(8):
                total[group * 8 + j] = v[j]

        def put(j, value):
            slot = slots[row * NCW + j]
            o_ref[slot // 4, pl.ds(pl.multiple_of((slot % 4) * 16, 16), 16), :] = value

        def write_code(code):
            for j in range(NCW):
                slot = slots[row * NCW + j]
                codes[slot // 4] = jnp.where(rows == slot % 4, code[:8], codes[slot // 4])

        return lambda: encode(total, put, write_code)

    def both(r, _):
        for finish_row in [one(m, r) for m in range(2)]:
            finish_row()
        return 0

    lax.fori_loop(0, 4, both, 0)

    def finish(n, _):
        for m in range(4):
            o_ref[n * 4 + m, 64:72, :] = codes[n * 4 + m].astype(jnp.int16)
        return 0

    lax.fori_loop(0, 32, finish, 0)


def pack(slots, *parts):
    def whole(array):
        return pl.BlockSpec(
            array.shape, lambda i, *_, n=array.ndim: (0,) * n, pipeline_mode=pl.Buffered(1)
        )

    return pl.pallas_call(
        pack_kernel,
        grid_spec=pltpu.PrefetchScalarGridSpec(
            num_scalar_prefetch=1,
            grid=(1,),
            in_specs=[whole(array) for array in parts],
            out_specs=pl.BlockSpec((128, MSG, 128), lambda i, *_: (0, 0, 0), pipeline_mode=pl.Buffered(1)),
            scratch_shapes=[pltpu.VMEM((NCW, 16, 128), jnp.float32)] * 2 + [pltpu.VMEM((128, 8, 128), jnp.int32)],
        ),
        out_shape=jax.ShapeDtypeStruct((128, MSG, 128), jnp.int16),
        compiler_params=pltpu.CompilerParams(vmem_limit_bytes=32 << 20),
        name="pack",
    )(slots, *parts)


def unpack_kernel(r_ref, o_ref, full, scales):
    low32 = (lax.broadcasted_iota(jnp.int32, (16, 128), 1) & 32) == 0
    for n in range(16):
        for c in range(2):
            scales[n * 2 + c] = decoded_scale(r_ref[0, c, n, 64:72, :])

    def one(n, _):
        for s in range(2):
            for t in range(2):
                h = []
                for c in range(2):
                    at = (s * 2 + t) * 16
                    q = r_ref[0, c, n, at:at + 16, :].astype(jnp.int32).astype(jnp.float32)
                    h.append(q * scales[n * 2 + c, s * 2 + t:s * 2 + t + 1, :])
                base = pl.multiple_of(((s * 16 + n) * 2 + t) * 32, 32)
                full[pl.ds(base, 16), :] = jnp.where(low32, h[0], pltpu.roll(h[1], 32, 1))
                full[pl.ds(base + 16, 16), :] = jnp.where(low32, pltpu.roll(h[0], 96, 1), h[1])
        return 0

    lax.fori_loop(0, 16, one, 0, unroll=8)
    for p in range(32):
        o_ref[:, p * 128:(p + 1) * 128] = full[pl.ds(p, 64, stride=32), :]


def unpack(received):
    return pl.pallas_call(
        unpack_kernel,
        grid=(X,),
        in_specs=[pl.BlockSpec((1, C, 16, MSG, 128), lambda x: (x, 0, 0, 0, 0))],
        out_specs=pl.BlockSpec((64, 4096), lambda x: (x, 0)),
        out_shape=jax.ShapeDtypeStruct((256, 4096), jnp.float32),
        scratch_shapes=[pltpu.VMEM((64 * 32, 128), jnp.float32), pltpu.VMEM((32, 8, 128), jnp.float32)],
        compiler_params=pltpu.CompilerParams(vmem_limit_bytes=32 << 20),
        name="unpack",
    )(received)


def local(kohn_blocks, kohn_columns, density_blocks, density_columns, owner_map):
    x, c = lax.axis_index("x"), lax.axis_index("core")
    z, y = lax.axis_index("z"), lax.axis_index("y")
    on_line, on_cross = jnp.where(c == 0, z, y), jnp.where(c == 0, y, z)
    at = jnp.stack([c, on_line, on_cross, x])

    kohn = kohn_blocks.reshape(16, 4, SK * 32, 128)
    kohn_other = over_core(kohn)

    ints = jnp.concatenate([
        kohn_columns.reshape(2, 128), jnp.pad(density_columns.reshape(1, 64), ((0, 0), (0, 64))),
        owner_map.reshape(1, 128), jnp.zeros((12, 128), jnp.int32),
    ])
    dens, kohn = lax.optimization_barrier((density_blocks[0], kohn))

    mine, theirs = split(at, dens, ints)
    shard = jnp.concatenate([mine, over_core(theirs)])
    shard, kohn, kohn_other = lax.optimization_barrier((shard, kohn, kohn_other))
    left, right = over_x(shard, 1), over_x(shard, -1)

    kohn, ahead, back = regroup(at, kohn, kohn_other)
    kohn_prev, kohn_next = over_line(ahead, 1), over_line(back, -1)
    opposite0, opposite1 = over_line(kohn_prev[2:], 1), over_line(kohn_next[2:], -1)

    owners = jnp.stack([owner_map.reshape(128), shard[PART + 8 * 128 + 3].astype(jnp.int32)])
    hit = (owners[..., None] == jnp.arange(128, dtype=jnp.int32)).astype(jnp.int32)
    ranks = jnp.sum(jnp.cumsum(hit, axis=1) * hit, axis=2) - 1
    source = jnp.arange(2, dtype=jnp.int32)[:, None] ^ c
    slots = (owners * 4 + source * 2 + ranks).reshape(-1)

    low = jnp.concatenate([shard, left])
    high = jnp.concatenate([right, over_x(left[:PART], 1), over_x(right[PART:], -1)])
    low_sent, high_sent, kohn_prev, kohn_next, slots = lax.optimization_barrier((low, high, kohn_prev, kohn_next, slots))
    prev_low, next_high = over_line(low, 1), over_line(high, -1)
    prev_high, next_low = over_line(high_sent, 1), over_line(low_sent, -1)

    def both(array):
        return [(array, 0), (array, 1)]

    everything = tuple((target, m) for target in range(4) for m in range(2))
    sums, = panel_sums("own_panel", "first", at, both(kohn), [low, high], everything, us=9.0)
    prev_low, next_high, sums = lax.optimization_barrier((prev_low, next_high, sums))
    far_low, far_high = over_line(prev_low, 1), over_line(next_high, -1)
    sums, = panel_sums(
        "near_panels", "more", at, both(kohn_prev) + both(kohn_next), [prev_low, prev_high, next_low, next_high],
        everything, sums, us=16.0,
    )

    sums, opposite0, opposite1 = lax.optimization_barrier((sums, opposite0, opposite1))

    def last(form, halves, received=()):
        kohn = [(opposite0, 0), (opposite1, 0)]
        return panel_sums("last_" + form, form, at, kohn, [far_low, far_high], halves, sums, received)

    via_next, via_prev = last("coded", ((0, 0), (0, 1)))
    via_next, via_prev = over_cross(via_next, 1), over_cross(via_prev, -1)
    next1, prev0 = last("coded", ((1, 1), (2, 0)))
    prev_1, next_0 = over_cross(next1, 1), over_cross(prev0, -1)
    next0, prev1 = last("sent", ((1, 0), (2, 1)), (via_next, via_prev))
    prev_0, next_1 = over_cross(next0, 1), over_cross(prev1, -1)
    own, = last("own", ((3, 0), (3, 1)), (next_0, prev_1))

    outgoing = pack(slots, own, prev_0, next_1)
    received = lax.all_to_all(outgoing, ALL, split_axis=0, concat_axis=0, tiled=True)
    return unpack(received.reshape(X, C, 16, MSG, 128))


def solution(mesh):
    grid = Mesh(mesh.devices.reshape(X, C, Z, Y), ALL)
    row, col = ("x", "core"), ("z", "y")
    return jax.shard_map(
        local,
        mesh=grid,
        in_specs=(
            P(row, col, None, None),
            P(row, col, None),
            P(col, row, None, None),
            P(col, row, None),
            P(ALL, None),
        ),
        out_specs=P(ALL, None),
        check_vma=False,
    )
```

```python
import jax
import jax.numpy as jnp
from jax import lax
from jax.experimental import pallas as pl
from jax.experimental.pallas import tpu as pltpu
from jax.sharding import Mesh, PartitionSpec as P

B = 64
HALF = 32
NCW = 32
SK = 4
SP = 8
X, C, Z, Y = 4, 2, 4, 4
ALL = ("x", "core", "z", "y")
PLANE = ("core", "z", "y")
TOP = 32766.0
MSG = 72
LIMIT = 16
PART = 8 * 128 + 16
ORDER = (2, 1, 3, 0)


def lines(along):
    groups = []
    for c in range(C):
        for fixed in range(4):
            on_z = (c ^ along) == 0
            groups.append([(c * Z + (i if on_z else fixed)) * Y + (fixed if on_z else i) for i in range(4)])
    return groups


LINE, CROSS = lines(0), lines(1)


def over(groups, v, step):
    return lax.ppermute(v, PLANE, [(group[i], group[(i + step) % 4]) for group in groups for i in range(4)])


def over_line(v, step):
    return over(LINE, v, step)


def over_cross(v, step):
    return over(CROSS, v, step)


def over_x(v, step):
    return lax.ppermute(v, "x", [(i, (i + step) % X) for i in range(X)])


def over_core(v):
    return lax.ppermute(v, "core", [(0, 1), (1, 0)])


def split_kernel(core, d_ref, i_ref, mine, theirs, flat0, wide0, flat1, wide1):
    lane32 = lax.broadcasted_iota(jnp.int32, (32, 128), 1)
    lane64 = lax.broadcasted_iota(jnp.int32, (64, 128), 1)

    def one(k, flat, wide):
        rows = d_ref[k].astype(jnp.float32)
        for p in range(32):
            flat[p * 8:(p + 1) * 8, :] = rows[:, p * 128:(p + 1) * 128]
        for b in range(4):
            lo, hi = flat[pl.ds(b, 32, stride=8), :], flat[pl.ds(b + 4, 32, stride=8), :]
            wide[b, pl.ds(0, 32, stride=2), :] = jnp.where(lane32 < 64, lo, pltpu.roll(hi, 64, 1))
            wide[b, pl.ds(1, 32, stride=2), :] = jnp.where(lane32 < 64, pltpu.roll(lo, 64, 1), hi)
        v = [wide[b] for b in range(4)]
        for bit in (2, 1):
            keep = (lane64 & (16 * bit)) == 0
            w = [None] * 4
            for i in range(4):
                if not i & bit:
                    lo, hi = v[i], v[i | bit]
                    w[i] = jnp.where(keep, lo, pltpu.roll(hi, 16 * bit, 1))
                    w[i | bit] = jnp.where(keep, pltpu.roll(lo, 128 - 16 * bit, 1), hi)
            v = w
        first = jnp.concatenate([v[0], v[1]], axis=0).T
        second = jnp.concatenate([v[2], v[3]], axis=0).T
        swapped = core[0] == 1
        at = pl.ds(pl.multiple_of(k * 128, 128), 128)
        mine[at, :] = jnp.where(swapped, second, first).astype(jnp.bfloat16)
        theirs[at, :] = jnp.where(swapped, first, second).astype(jnp.bfloat16)

    def two(i, _):
        one(i * 2, flat0, wide0)
        one(i * 2 + 1, flat1, wide1)
        return 0

    lax.fori_loop(0, 4, two, 0)
    ints = i_ref[...].astype(jnp.float32).astype(jnp.bfloat16)
    mine[8 * 128:, :] = ints
    theirs[8 * 128:, :] = ints


def split(core, dens, ints):
    half = jax.ShapeDtypeStruct((PART, 128), jnp.bfloat16)
    whole = pl.BlockSpec((PART, 128), lambda i, *_: (0, 0))
    return pl.pallas_call(
        split_kernel,
        grid_spec=pltpu.PrefetchScalarGridSpec(
            num_scalar_prefetch=1, grid=(1,),
            in_specs=[
                pl.BlockSpec((8, SP, B * B), lambda i, *_: (0, 0, 0)), pl.BlockSpec((16, 128), lambda i, *_: (0, 0))
            ],
            out_specs=[whole, whole],
            scratch_shapes=[pltpu.VMEM((256, 128), jnp.float32), pltpu.VMEM((4, B, 128), jnp.float32)] * 2,
        ),
        out_shape=[half, half],
        name="split",
    )(core, dens, ints)


def regroup_kernel(at, mine, other, own, ahead, back, sems):
    swapped, line, cross = at[0] == 1, at[1], at[2]
    copies = []
    for step in range(4):
        t = (line + step) % 4
        for i, rel in enumerate(ORDER):
            o = (cross + rel) % 4
            row = jnp.where(swapped, o * 4 + t, t * 4 + o)
            for m, src in enumerate((mine, other)):
                dst = (own.at[m, i], ahead.at[m, i], (ahead, back)[m].at[2, i], back.at[m, i])[step]
                copies.append(pltpu.make_async_copy(src.at[row], dst, sems.at[len(copies)]))
    for copy in copies:
        copy.start()
    for copy in copies:
        copy.wait()


def regroup(at, mine, other):
    shapes = [(2, 4, 4, 128, 128), (3, 4, 4, 128, 128), (3, 4, 4, 128, 128)]
    return pl.pallas_call(
        regroup_kernel,
        grid_spec=pltpu.PrefetchScalarGridSpec(
            num_scalar_prefetch=1, grid=(1,),
            in_specs=[pl.BlockSpec(memory_space=pl.ANY)] * 2,
            out_specs=[pl.BlockSpec(s, lambda i, *_: (0,) * 5, pipeline_mode=pl.Buffered(1)) for s in shapes],
            scratch_shapes=[pltpu.SemaphoreType.DMA((32,))],
        ),
        out_shape=[jax.ShapeDtypeStruct(shape, jnp.bfloat16) for shape in shapes],
        compiler_params=pltpu.CompilerParams(vmem_limit_bytes=12 << 20),
        name="regroup",
    )(at, mine, other)


def encode(values, put, write_code):
    top = jnp.zeros((16, 128), jnp.float32)
    for j in range(NCW):
        top = jnp.maximum(top, jnp.abs(values[j]))
    top = jnp.maximum(jnp.max(top, axis=0, keepdims=True), 2.0 ** -110)
    code = jnp.floor(jnp.log2(top) * 256.0) + 1.0
    scale = jnp.broadcast_to(jnp.exp2(code * (-1.0 / 256.0)) * TOP, (16, 128))
    write_code(jnp.broadcast_to(code.astype(jnp.int32), (16, 128)))
    for j in range(NCW):
        put(j, jnp.floor(values[j] * scale + 0.5).astype(jnp.int32).astype(jnp.int16))


def decoded_scale(code):
    return jnp.exp2(code.astype(jnp.int32).astype(jnp.float32) * (1.0 / 256.0)) * (1.0 / TOP)


def panel_kernel(n, pieces, halves, form, at, *refs):
    kohn, refs = refs[:2 * n], refs[2 * n:]
    panels, refs = refs[:pieces], refs[pieces:]
    if form != "first":
        sums_in, refs = refs[0], refs[1:]
    received = ()
    if form in ("sent", "own"):
        received, refs = refs[:2], refs[2:]
    outs, (dens, sems, acc0, acc1, in_sems, out_sems, staged, ints) = refs[:-8], refs[-8:]
    accs = (acc0, acc1)
    size = n * 8 * PART // pieces
    core, line, cross, x = at[0], at[1], at[2], at[3]

    loads = [pltpu.make_async_copy(panels[s], dens.at[pl.ds(s * size, size)], sems.at[s]) for s in range(pieces)]
    sums = []
    if form != "first":
        for h, (target, m) in enumerate(halves):
            for q in range(2):
                src = sums_in.at[target, pl.ds(m * 4 + q * 2, 2)]
                sums.append(pltpu.make_async_copy(src, accs[q].at[h], in_sems.at[h * 2 + q]))
    stores = []
    if form in ("first", "more", "own"):
        for h, (target, m) in enumerate(halves):
            for q in range(2):
                dst = outs[0].at[target if len(halves) > 2 else 0, pl.ds(m * 4 + q * 2, 2)]
                stores.append(pltpu.make_async_copy(accs[q].at[h], dst, out_sems.at[h * 2 + q]))
    for copy in loads + sums:
        copy.start()
    for copy in loads:
        copy.wait()
    for s in range(n):
        rows = [dens[pl.ds((s * 8 + p) * PART + 8 * 128, 16), :].astype(jnp.float32) for p in range(8)]
        rows = [row[2:3] for row in rows] + [rows[0][0:2], rows[1][0:2], jnp.zeros((4, 128), jnp.float32)]
        staged[s * 16:(s + 1) * 16, :] = jnp.concatenate(rows, axis=0).astype(jnp.int32)
    copy = pltpu.make_async_copy(staged, ints, sems.at[pieces])
    copy.start()
    copy.wait()

    low = (lax.broadcasted_iota(jnp.int32, (32, 128), 1) < 64).astype(jnp.float32).astype(jnp.bfloat16)
    high = 1 - low

    def twice(blk):
        turned = jnp.concatenate([blk[:, B:], blk[:, :B]], axis=1)
        return jnp.concatenate([blk * low, turned * low, turned * high, blk * high], axis=0)

    def product(h, r, s, a):
        target, m = halves[h]
        goal = (cross + ORDER[target]) & 3
        place = jnp.where(core == 1, goal * 4 + line, line * 4 + goal)
        k = ints[s * 16 + 8 + m * 2 + (place >> 3), (place & 7) * 16 + r * 4 + a]
        slot = (120 >> (2 * (((k >> 4) - x) & 3))) & 3
        k = slot * 16 + ((k & 15) ^ (8 * core))
        part = s * 8 + (k >> 3)
        left = dens[pl.ds(pl.multiple_of(part * PART + (k & 7) * 128, 16), 128), :]
        ref, index = kohn[2 * s + m], target if kohn[2 * s + m].shape[1] == 4 else 0
        right = twice(ref[0, index, r, a * 32:(a + 1) * 32, :])
        r = lax.dot_general(left, right, (((1,), (1,)), ((), ())), preferred_element_type=jnp.float32)
        return s * 16 + (k >> 3), (k & 7) * SP, r

    def add(total, word, first, r):
        js = [ints[word, first + b] for b in range(SP)]
        old = [total[j] for j in js]
        for b in range(SP):
            total[js[b]] = old[b] + r[b * 16:(b + 1) * 16, :]

    def two_rows(h, pair):
        totals = []
        work = [(q, q * 2 + pair, s, a) for s in range(n) for a in range(SK) for q in range(2)]
        for q in range(2):
            r = q * 2 + pair
            total = accs[q].at[h, pair]
            if form == "first":
                total[...] = jnp.zeros((NCW, 16, 128), jnp.float32)
            elif received:
                scale = decoded_scale(received[h][r, NCW])
                for j in range(NCW):
                    total[j] = total[j] + received[h][r, j].astype(jnp.int32).astype(jnp.float32) * scale
            totals.append(total)
        held = [product(h, *work[i][1:]) for i in range(4)]
        for i in range(len(work)):
            if i + 4 < len(work):
                held.append(product(h, *work[i + 4][1:]))
            add(totals[work[i][0]], *held[i])
        if form in ("coded", "sent"):
            for q in range(2):
                r = q * 2 + pair

                def put(j, value, r=r):
                    outs[h][r, j] = value

                encode(totals[q], put, lambda code, put=put: put(NCW, code.astype(jnp.int16)))

    for h in range(len(halves)):
        for copy in sums[2 * h:2 * h + 2]:
            copy.wait()
        if len(halves) > 2:
            lax.fori_loop(0, 2, lambda pair, _, h=h: (two_rows(h, pair), 0)[1], 0)
        else:
            two_rows(h, 0)
            two_rows(h, 1)
        for copy in stores[2 * h:2 * h + 2]:
            copy.start()
    for copy in stores:
        copy.wait()


def panel_sums(name, form, at, kohn, panels, halves, sums=None, received=(), us=4.0):
    n, pieces, groups = len(kohn) // 2, len(panels), len(halves)

    def k_spec(i, place):
        if groups > 2:
            return pl.BlockSpec((1, 4, 4, 128, 128), lambda *_: (place, 0, 0, 0, 0), pipeline_mode=pl.Buffered(1))
        target = {m: t for t, m in halves}[i % 2]
        return pl.BlockSpec((1, 1, 4, 128, 128), lambda *_: (place, target, 0, 0, 0), pipeline_mode=pl.Buffered(1))

    any_spec = pl.BlockSpec(memory_space=pl.ANY)
    sums_spec = pl.BlockSpec(memory_space=pltpu.HBM)
    coded = pl.BlockSpec((4, NCW + 1, 16, 128), lambda *_: (0, 0, 0, 0), pipeline_mode=pl.Buffered(1))
    if form in ("coded", "sent"):
        o_specs = [coded] * 2
        shapes = [jax.ShapeDtypeStruct((4, NCW + 1, 16, 128), jnp.int16)] * 2
    else:
        o_specs = [sums_spec if groups > 2 else any_spec]
        shapes = [jax.ShapeDtypeStruct((max(groups // 2, 1), 8, NCW, 16, 128), jnp.float32)]
    return pl.pallas_call(
        lambda *refs: panel_kernel(n, pieces, halves, form, *refs),
        grid_spec=pltpu.PrefetchScalarGridSpec(
            num_scalar_prefetch=1,
            grid=(1,),
            in_specs=(
                [k_spec(i, place) for i, (_, place) in enumerate(kohn)] + [any_spec] * pieces
                + ([] if sums is None else [sums_spec]) + [coded] * len(received)
            ),
            out_specs=o_specs,
            scratch_shapes=[
                pltpu.VMEM((n * 8 * PART, 128), jnp.bfloat16),
                pltpu.SemaphoreType.DMA((pieces + 1,)),
                pltpu.VMEM((groups, 2, NCW, 16, 128), jnp.float32),
                pltpu.VMEM((groups, 2, NCW, 16, 128), jnp.float32),
                pltpu.SemaphoreType.DMA((groups * 2,)),
                pltpu.SemaphoreType.DMA((groups * 2,)),
                pltpu.VMEM((n * 16, 128), jnp.int32),
                pltpu.SMEM((n * 16, 128), jnp.int32),
            ],
        ),
        out_shape=shapes,
        compiler_params=pltpu.CompilerParams(vmem_limit_bytes=LIMIT << 20),
        cost_estimate=pl.CostEstimate(flops=int(us * 1.1e9), bytes_accessed=int(us * 2e6), transcendentals=0),
        name=name,
    )(at, *[array for array, _ in kohn], *panels, *([] if sums is None else [sums]), *received)


def pack_kernel(slots, own, prev0, next1, o_ref, total, codes):
    rows = lax.broadcasted_iota(jnp.int32, (8, 128), 0)
    lane = lax.broadcasted_iota(jnp.int32, (16, 128), 1)

    def clear(n, _):
        for m in range(4):
            o_ref[n * 4 + m] = jnp.zeros((MSG, 128), jnp.int16)
            codes[n * 4 + m] = jnp.zeros((8, 128), jnp.int32)
        return 0

    lax.fori_loop(0, 32, clear, 0)

    def one(m, r):
        row = m * 4 + r
        coded = (prev0, next1)[m]
        scale = decoded_scale(coded[r, NCW])
        for group in range(NCW // 8):
            blocks = []
            for j in range(group * 8, group * 8 + 8):
                blocks.append(own[0, row, j] + coded[r, j].astype(jnp.int32).astype(jnp.float32) * scale)
            turned = jnp.concatenate(blocks, axis=0).T
            v = []
            for q in range(8):
                par, mh, zh = q // 4, (q // 2) % 2, q % 2
                at = (zh * 4 + par * 2 + mh) * 16
                v.append(turned[at:at + 16, :])
            for bit in (4, 2, 1):
                keep = (lane & (16 * bit)) == 0
                w = [None] * 8
                for i in range(8):
                    if not i & bit:
                        lo, hi = v[i], v[i | bit]
                        w[i] = jnp.where(keep, lo, pltpu.roll(hi, 16 * bit, 1))
                        w[i | bit] = jnp.where(keep, pltpu.roll(lo, 128 - 16 * bit, 1), hi)
                v = w
            for j in range(8):
                total[group * 8 + j] = v[j]

        def put(j, value):
            slot = slots[row * NCW + j]
            o_ref[slot // 4, pl.ds(pl.multiple_of((slot % 4) * 16, 16), 16), :] = value

        def write_code(code):
            for j in range(NCW):
                slot = slots[row * NCW + j]
                codes[slot // 4] = jnp.where(rows == slot % 4, code[:8], codes[slot // 4])

        encode(total, put, write_code)

    for m in range(2):
        lax.fori_loop(0, 4, lambda r, _, m=m: (one(m, r), 0)[1], 0)

    def finish(n, _):
        for m in range(4):
            o_ref[n * 4 + m, 64:72, :] = codes[n * 4 + m].astype(jnp.int16)
        return 0

    lax.fori_loop(0, 32, finish, 0)


def pack(slots, *parts):
    def whole(array):
        return pl.BlockSpec(
            array.shape, lambda i, *_, n=array.ndim: (0,) * n, pipeline_mode=pl.Buffered(1)
        )

    return pl.pallas_call(
        pack_kernel,
        grid_spec=pltpu.PrefetchScalarGridSpec(
            num_scalar_prefetch=1,
            grid=(1,),
            in_specs=[whole(array) for array in parts],
            out_specs=pl.BlockSpec((128, MSG, 128), lambda i, *_: (0, 0, 0), pipeline_mode=pl.Buffered(1)),
            scratch_shapes=[pltpu.VMEM((NCW, 16, 128), jnp.float32), pltpu.VMEM((128, 8, 128), jnp.int32)],
        ),
        out_shape=jax.ShapeDtypeStruct((128, MSG, 128), jnp.int16),
        compiler_params=pltpu.CompilerParams(vmem_limit_bytes=32 << 20),
        name="pack",
    )(slots, *parts)


def unpack_kernel(r_ref, o_ref, full, scales):
    low32 = (lax.broadcasted_iota(jnp.int32, (16, 128), 1) & 32) == 0
    for n in range(16):
        for c in range(2):
            scales[n * 2 + c] = decoded_scale(r_ref[0, c, n, 64:72, :])

    def one(n, _):
        for s in range(2):
            for t in range(2):
                h = []
                for c in range(2):
                    at = (s * 2 + t) * 16
                    q = r_ref[0, c, n, at:at + 16, :].astype(jnp.int32).astype(jnp.float32)
                    h.append(q * scales[n * 2 + c, s * 2 + t:s * 2 + t + 1, :])
                base = pl.multiple_of(((s * 16 + n) * 2 + t) * 32, 32)
                full[pl.ds(base, 16), :] = jnp.where(low32, h[0], pltpu.roll(h[1], 32, 1))
                full[pl.ds(base + 16, 16), :] = jnp.where(low32, pltpu.roll(h[0], 96, 1), h[1])
        return 0

    lax.fori_loop(0, 16, one, 0, unroll=8)
    for p in range(32):
        o_ref[:, p * 128:(p + 1) * 128] = full[pl.ds(p, 64, stride=32), :]


def unpack(received):
    return pl.pallas_call(
        unpack_kernel,
        grid=(X,),
        in_specs=[pl.BlockSpec((1, C, 16, MSG, 128), lambda x: (x, 0, 0, 0, 0))],
        out_specs=pl.BlockSpec((64, 4096), lambda x: (x, 0)),
        out_shape=jax.ShapeDtypeStruct((256, 4096), jnp.float32),
        scratch_shapes=[pltpu.VMEM((64 * 32, 128), jnp.float32), pltpu.VMEM((32, 8, 128), jnp.float32)],
        compiler_params=pltpu.CompilerParams(vmem_limit_bytes=32 << 20),
        name="unpack",
    )(received)


def local(kohn_blocks, kohn_columns, density_blocks, density_columns, owner_map):
    x, c = lax.axis_index("x"), lax.axis_index("core")
    z, y = lax.axis_index("z"), lax.axis_index("y")
    on_line, on_cross = jnp.where(c == 0, z, y), jnp.where(c == 0, y, z)
    at = jnp.stack([c, on_line, on_cross, x])

    kohn = kohn_blocks.reshape(16, 4, SK * 32, 128)
    kohn_other = over_core(kohn)

    ints = jnp.concatenate([
        kohn_columns.reshape(2, 128), jnp.pad(density_columns.reshape(1, 64), ((0, 0), (0, 64))),
        owner_map.reshape(1, 128), jnp.zeros((12, 128), jnp.int32),
    ])
    dens, kohn = lax.optimization_barrier((density_blocks[0], kohn))

    mine, theirs = split(at, dens, ints)
    shard = jnp.concatenate([mine, over_core(theirs)])
    shard, kohn, kohn_other = lax.optimization_barrier((shard, kohn, kohn_other))
    left, right = over_x(shard, 1), over_x(shard, -1)

    kohn, ahead, back = regroup(at, kohn, kohn_other)
    kohn_prev, kohn_next = over_line(ahead, 1), over_line(back, -1)
    opposite0, opposite1 = over_line(kohn_prev[2:], 1), over_line(kohn_next[2:], -1)

    owners = jnp.stack([owner_map.reshape(128), shard[PART + 8 * 128 + 3].astype(jnp.int32)])
    hit = (owners[..., None] == jnp.arange(128, dtype=jnp.int32)).astype(jnp.int32)
    ranks = jnp.sum(jnp.cumsum(hit, axis=1) * hit, axis=2) - 1
    source = jnp.arange(2, dtype=jnp.int32)[:, None] ^ c
    slots = (owners * 4 + source * 2 + ranks).reshape(-1)

    low = jnp.concatenate([shard, left])
    high = jnp.concatenate([right, over_x(left[:PART], 1), over_x(right[PART:], -1)])
    low_sent, high_sent, kohn_prev, kohn_next, slots = lax.optimization_barrier((low, high, kohn_prev, kohn_next, slots))
    prev_low, next_high = over_line(low, 1), over_line(high, -1)
    prev_high, next_low = over_line(high_sent, 1), over_line(low_sent, -1)

    def both(array):
        return [(array, 0), (array, 1)]

    everything = tuple((target, m) for target in range(4) for m in range(2))
    sums, = panel_sums("own_panel", "first", at, both(kohn), [low, high], everything, us=9.0)
    prev_low, next_high, sums = lax.optimization_barrier((prev_low, next_high, sums))
    far_low, far_high = over_line(prev_low, 1), over_line(next_high, -1)
    sums, = panel_sums(
        "near_panels", "more", at, both(kohn_prev) + both(kohn_next), [prev_low, prev_high, next_low, next_high],
        everything, sums, us=16.0,
    )

    sums, opposite0, opposite1 = lax.optimization_barrier((sums, opposite0, opposite1))

    def last(form, halves, received=()):
        kohn = [(opposite0, 0), (opposite1, 0)]
        return panel_sums("last_" + form, form, at, kohn, [far_low, far_high], halves, sums, received)

    via_next, via_prev = last("coded", ((0, 0), (0, 1)))
    via_next, via_prev = over_cross(via_next, 1), over_cross(via_prev, -1)
    next1, prev0 = last("coded", ((1, 1), (2, 0)))
    prev_1, next_0 = over_cross(next1, 1), over_cross(prev0, -1)
    next0, prev1 = last("sent", ((1, 0), (2, 1)), (via_next, via_prev))
    prev_0, next_1 = over_cross(next0, 1), over_cross(prev1, -1)
    own, = last("own", ((3, 0), (3, 1)), (next_0, prev_1))

    outgoing = pack(slots, own, prev_0, next_1)
    received = lax.all_to_all(outgoing, ALL, split_axis=0, concat_axis=0, tiled=True)
    return unpack(received.reshape(X, C, 16, MSG, 128))


def solution(mesh):
    grid = Mesh(mesh.devices.reshape(X, C, Z, Y), ALL)
    row, col = ("x", "core"), ("z", "y")
    return jax.shard_map(
        local,
        mesh=grid,
        in_specs=(
            P(row, col, None, None),
            P(row, col, None),
            P(col, row, None, None),
            P(col, row, None),
            P(ALL, None),
        ),
        out_specs=P(ALL, None),
        check_vma=False,
    )
```
